32 devices in a mesh: lat: 4 (over y, x), lon: 8 (over z, core).
Axes of the slice: x: 2, y: 2, z: 4, core: 2. Of those that a mesh axis runs over, the one named last changes fastest.
Arguments:
- sea_heat_deviations: bfloat16 [16, 1024, 3840], P('lat', 'lon'), may hold values from -6 to 6
- missing_date_bitmask: int32 [16, 1024, 256], P('lat', 'lon'), may hold values from 0 to 32704
- ocean_binary_mask: int32 [16, 1024], P('lat', 'lon'), may hold values 0 or 1
- mode_maps: float32 [48, 16, 1024], P(None, 'lat', 'lon'), may hold values from -1 to 1
- mode_series: float32 [48, 3840], P(None, 'lon'), may hold values from -6 to 6
Outputs:
- spatial_out: float32 [48, 16, 1024], P(None, 'lat', 'lon')
- temporal_out: float32 [48, 3840], P(None, 'lon')
The draws below stay inside these ranges and needn't reach their ends.
Inputs may be any that keep to these rules, and one draw needn't show every extreme that they name: `missing_date_bitmask`: bit b of word w of a cell flags day 15 w + b as missing when it is 1; words run up to 32704.
All inputs are finite; a program needn't handle non-finite values. No bound on the sum of `ocean_binary_mask` on one device may be relied on, other than what follows from the above.
Results may differ from the reference program's by a relative error of at most 0.0003.
Values sent between devices are 32-bit elements; how exact they have to be, the bound alone decides.
No kernel may reach another device: no remote copies, remote signals or barrier semaphores. Data moves between devices by JAX's collectives and lax.ppermute only.
A program may use at most 128 MiB of HBM per device.

```python
import jax
import jax.numpy as jnp
from jax import lax

DAILY_LENGTH = 3840
MODES = 48
STEPS = 4
SWEEPS = 4
WORDS = 256
NLATITUDE_BANDS = 16
ZONAL_POSITIONS = 1024


def set_ends(values, stream_key, smallest, top_value):
    index_at = [jax.random.randint(jax.random.fold_in(stream_key, axis), (), 0, length) for axis, length in enumerate(values.shape)]
    main_axis = values.shape.index(max(values.shape))
    next_to = index_at[:main_axis] + [(index_at[main_axis] + 1) % values.shape[main_axis]] + index_at[main_axis + 1:]
    return values.at[tuple(index_at)].set(smallest).at[tuple(next_to)].set(top_value)


def block_scale(own_key, extent, cuts, low, largest):
    def one(axis_at, shards_of):
        heights = jax.random.uniform(jax.random.fold_in(jax.random.fold_in(own_key, 6), axis_at), (shards_of,), jnp.float32, low / len(cuts), largest / len(cuts))
        return jnp.repeat(jnp.exp(heights), extent[axis_at] // shards_of).reshape((-1,) + (1,) * (len(extent) - axis_at - 1))

    loudness = one(*cuts[0])
    for cut in cuts[1:]:
        loudness = loudness * one(*cut)
    return loudness


def gaussian(stream_key, dims, width, reach, pieces=(), kind=jnp.bfloat16):
    gain = block_scale(stream_key, dims, pieces, -0.22, 0.18) if pieces else 1.0
    drawn = jax.random.normal(stream_key, dims, jnp.float32) * width * gain
    return jnp.minimum(jnp.maximum(drawn, -reach), reach).astype(kind)


def setup_inputs(seed: int = 0) -> dict:
    key_of = jax.random.split(jax.random.key(seed), 6)
    return {
        "sea_heat_deviations": gaussian(key_of[0], (NLATITUDE_BANDS, ZONAL_POSITIONS, DAILY_LENGTH), 1.0, 6.0, ((0, 4), (1, 8))),
        "missing_date_bitmask": set_ends(jax.random.randint(key_of[1], (NLATITUDE_BANDS, ZONAL_POSITIONS, WORDS), 0, 32705), jax.random.fold_in(key_of[1], 1), 0, 32704).astype(jnp.int32),
        "ocean_binary_mask": set_ends((jax.random.randint(key_of[2], (NLATITUDE_BANDS, ZONAL_POSITIONS), 0, 5) < 4).astype(jnp.int32), jax.random.fold_in(key_of[2], 1), 0, 1),
        "mode_maps": gaussian(key_of[3], (MODES, NLATITUDE_BANDS, ZONAL_POSITIONS), 0.15, 1.0, ((1, 4), (2, 8)), jnp.float32),
        "mode_series": gaussian(key_of[4], (MODES, DAILY_LENGTH), 1.0, 6.0, ((1, 8),), jnp.float32),
    }


KLAT = 0.2
KLON = 0.05
EPS = 1e-06
HIGH = lax.Precision.HIGHEST

def latitude_cos(rows, nrows):
    degree = -60.0 + 120.0 * (rows.astype(jnp.float32) + 0.5) / nrows
    return jnp.cos(degree * (jnp.pi / 180.0))

def unpack_days(words):
    shifts = jnp.arange(15, dtype=jnp.int32)
    flags = jnp.right_shift(words[..., None], shifts) & 1
    return flags.reshape(words.shape[:-1] + (words.shape[-1] * 15,))

def solve_pair(gram, right):
    determ = gram[0, 0] * gram[1, 1] - gram[0, 1] * gram[1, 0]
    first = (gram[1, 1] * right[0] - gram[0, 1] * right[1]) / determ
    second = (gram[0, 0] * right[1] - gram[1, 0] * right[0]) / determ
    return jnp.stack([first, second])

def sweep(padded, coast, klon_rows):
    center = padded[:, 1:-1, 1:-1]
    north = coast[:-2, 1:-1] * (padded[:, :-2, 1:-1] - center)
    south = coast[2:, 1:-1] * (padded[:, 2:, 1:-1] - center)
    west = coast[1:-1, :-2] * (padded[:, 1:-1, :-2] - center)
    east = coast[1:-1, 2:] * (padded[:, 1:-1, 2:] - center)
    flux = KLAT * (north + south) + klon_rows[1:-1, None] * (west + east)
    return center + coast[1:-1, 1:-1] * flux

def wrap_pad(field):
    lead = [(0, 0)] * (field.ndim - 2)
    padded = jnp.pad(field, lead + [(1, 1), (0, 0)])
    return jnp.concatenate([padded[..., -1:], padded, padded[..., :1]], axis=-1)

def ref_diffuse(field, coast, klon):
    coast_pad = wrap_pad(coast)
    klon_pad = jnp.pad(klon, 1)
    for sweep_index in range(SWEEPS):
        field = sweep(wrap_pad(field), coast_pad, klon_pad)
    return field

def reference(sea_heat_deviations, missing_date_bitmask, ocean_binary_mask, mode_maps, mode_series):
    coast = ocean_binary_mask.astype(jnp.float32)
    cosl = latitude_cos(jnp.arange(NLATITUDE_BANDS), NLATITUDE_BANDS)
    klon = KLON / (cosl * cosl)
    weight = jnp.broadcast_to(cosl[:, None], (NLATITUDE_BANDS, ZONAL_POSITIONS)).reshape(-1)
    miss = unpack_days(missing_date_bitmask).reshape(-1, DAILY_LENGTH) == 1
    given_deviation = sea_heat_deviations.astype(jnp.float32).reshape(-1, DAILY_LENGTH)
    coast_flat = coast.reshape(-1)
    modes_now = mode_maps.reshape(MODES, -1)
    panel = mode_series
    recon = jnp.dot(modes_now.T, panel, precision=HIGH)
    total = MODES * NLATITUDE_BANDS * ZONAL_POSITIONS
    for step in range(STEPS):
        low = 2 * step
        pair_u = modes_now[low:low + 2]
        pair_v = panel[low:low + 2]
        others = recon - jnp.dot(pair_u.T, pair_v, precision=HIGH)
        filled = coast_flat[:, None] * jnp.where(miss, recon, given_deviation)
        resid = filled - others
        proj = jnp.dot(resid, pair_v.T, precision=HIGH).T
        gram = jnp.dot(pair_v, pair_v.T, precision=HIGH)
        fresh = coast_flat * solve_pair(gram, proj)
        fresh = ref_diffuse(fresh.reshape(2, NLATITUDE_BANDS, ZONAL_POSITIONS), coast, klon).reshape(2, -1)
        sums = lax.optimization_barrier(jnp.sum(weight * fresh * fresh, axis=1))
        scale = jnp.sqrt(sums / total + EPS)
        unit = fresh / scale[:, None]
        weighted = unit * weight
        proj_days = jnp.dot(weighted, resid, precision=HIGH)
        gram_u = jnp.dot(weighted, unit.T, precision=HIGH)
        new_v = solve_pair(gram_u, proj_days)
        recon = others + jnp.dot(unit.T, new_v, precision=HIGH)
        modes_now = modes_now.at[low:low + 2].set(unit)
        panel = panel.at[low:low + 2].set(new_v)
    return (modes_now.reshape(MODES, NLATITUDE_BANDS, ZONAL_POSITIONS), panel)
```

```python
import jax
import jax.numpy as jnp
from jax import lax
from jax.sharding import PartitionSpec as P

STEPS = 4
SWEEPS = 4


KLAT = 0.2
KLON = 0.05
EPS = 1e-06
HIGH = lax.Precision.HIGHEST


def pairing(lat_map, lon_map):
    nlat, nlon = (lax.axis_size("lat"), lax.axis_size("lon"))
    return [(i * nlon + j, lat_map(i) * nlon + lon_map(j)) for i in range(nlat) for j in range(nlon)]


def swap(x, lat_bits, lon_bits):
    return lax.ppermute(x, ("lat", "lon"), pairing(lambda i: i ^ lat_bits, lambda j: j ^ lon_bits))


def sum_all(x):
    nlat, nlon = (lax.axis_size("lat"), lax.axis_size("lon"))
    if nlat & (nlat - 1) or nlon & (nlon - 1):
        return lax.psum(x, ("lat", "lon"))
    if nlon > 1:
        x = x + swap(x, 0, 1)
    for size, first, on_lat in ((nlat, 1, True), (nlon, 2, False)):
        bit = first
        while bit < size:
            bits = lambda b: (b, 0) if on_lat else (0, b)
            if 2 * bit < size:
                near, far, both = (swap(x, *bits(b)) for b in (bit, 2 * bit, 3 * bit))
                x = (x + near) + (far + both)
                bit *= 4
            else:
                x = x + swap(x, *bits(bit))
                bit *= 2
    return x


def lat_halo(x, dim, depth):
    count, length = (lax.axis_size("lat"), x.shape[dim])
    last = lax.slice_in_dim(x, length - depth, length, axis=dim)
    first = lax.slice_in_dim(x, 0, depth, axis=dim)
    if count % 2:
        up = [(i, (i + 1) % count) for i in range(count)]
        before = lax.ppermute(last, "lat", up)
        after = lax.ppermute(first, "lat", [(j, i) for i, j in up])
        return jnp.concatenate([before, x, after], axis=dim)
    odd = lax.axis_index("lat") % 2 == 1
    out_a, out_b = (jnp.where(odd, first, last), jnp.where(odd, last, first))
    same = lambda j: j
    got_a = lax.ppermute(out_a, ("lat", "lon"), pairing(lambda i: i ^ 1, same))
    got_b = lax.ppermute(out_b, ("lat", "lon"), pairing(lambda i: (i + 1 if i % 2 else i - 1) % count, same))
    before, after = (jnp.where(odd, got_a, got_b), jnp.where(odd, got_b, got_a))
    return jnp.concatenate([before, x, after], axis=dim)


def lon_halo(x, dim, depth):
    count, length = (lax.axis_size("lon"), x.shape[dim])
    up = [(i, (i + 1) % count) for i in range(count)]
    before = lax.ppermute(lax.slice_in_dim(x, length - depth, length, axis=dim), "lon", up)
    after = lax.ppermute(lax.slice_in_dim(x, 0, depth, axis=dim), "lon", [(j, i) for i, j in up])
    return jnp.concatenate([before, x, after], axis=dim)


def latitude_cos(rows, nrows):
    degree = -60.0 + 120.0 * (rows.astype(jnp.float32) + 0.5) / nrows
    return jnp.cos(degree * (jnp.pi / 180.0))


def unpack_days(words):
    shifts = jnp.arange(15, dtype=jnp.int32)
    flags = jnp.right_shift(words[..., None], shifts) & 1
    return flags.reshape(words.shape[:-1] + (words.shape[-1] * 15,))


def solve_pair(gram, right):
    determ = gram[0, 0] * gram[1, 1] - gram[0, 1] * gram[1, 0]
    first = (gram[1, 1] * right[0] - gram[0, 1] * right[1]) / determ
    second = (gram[0, 0] * right[1] - gram[1, 0] * right[0]) / determ
    return jnp.stack([first, second])


def sweep(padded, coast, klon_rows):
    center = padded[:, 1:-1, 1:-1]
    north = coast[:-2, 1:-1] * (padded[:, :-2, 1:-1] - center)
    south = coast[2:, 1:-1] * (padded[:, 2:, 1:-1] - center)
    west = coast[1:-1, :-2] * (padded[:, 1:-1, :-2] - center)
    east = coast[1:-1, 2:] * (padded[:, 1:-1, 2:] - center)
    flux = KLAT * (north + south) + klon_rows[1:-1, None] * (west + east)
    return center + coast[1:-1, 1:-1] * flux


def shards(sea_heat_deviations, missing_date_bitmask, ocean_binary_mask, mode_maps, mode_series):
    polar_coordinate, zonal_coordinate, calendar_dates = sea_heat_deviations.shape
    modes = mode_maps.shape[0]
    nlat = polar_coordinate * lax.axis_size("lat")
    total = modes * nlat * zonal_coordinate * lax.axis_size("lon")
    row_start = lax.axis_index("lat") * polar_coordinate
    cosl = latitude_cos(row_start + jnp.arange(polar_coordinate), nlat)
    weight = jnp.broadcast_to(cosl[:, None], (polar_coordinate, zonal_coordinate)).reshape(-1)
    coast = ocean_binary_mask.astype(jnp.float32)
    coast_flat = coast.reshape(-1)
    depth = SWEEPS
    coast_pad = lon_halo(lat_halo(coast, 0, depth), 1, depth)
    pad_rows = row_start - depth + jnp.arange(polar_coordinate + 2 * depth)
    inside = ((pad_rows >= 0) & (pad_rows < nlat)).astype(jnp.float32)
    coast_pad = coast_pad * inside[:, None]
    pad_cos = latitude_cos(pad_rows, nlat)
    klon_pad = KLON / (pad_cos * pad_cos)
    miss = unpack_days(missing_date_bitmask).reshape(-1, calendar_dates) == 1
    given_deviation = sea_heat_deviations.astype(jnp.float32).reshape(-1, calendar_dates)
    panel = lax.all_gather(mode_series, "lon", axis=1, tiled=True)
    modes_now = mode_maps.reshape(modes, -1)
    recon = jnp.dot(modes_now.T, panel, precision=HIGH)
    for step in range(STEPS):
        low = 2 * step
        pair_u = modes_now[low : low + 2]
        pair_v = panel[low : low + 2]
        others = recon - jnp.dot(pair_u.T, pair_v, precision=HIGH)
        filled = coast_flat[:, None] * jnp.where(miss, recon, given_deviation)
        resid = filled - others
        proj = jnp.dot(resid, pair_v.T, precision=HIGH).T
        gram = jnp.dot(pair_v, pair_v.T, precision=HIGH)
        fresh = (coast_flat * solve_pair(gram, proj)).reshape(2, polar_coordinate, zonal_coordinate)
        fresh = lon_halo(lat_halo(fresh, 1, depth), 2, depth)
        for cut in range(SWEEPS):
            inner = slice(cut, -cut) if cut else slice(None)
            fresh = sweep(fresh, coast_pad[inner, inner], klon_pad[inner])
        fresh = fresh.reshape(2, -1)
        weighted = fresh * weight
        raw_days = jnp.dot(weighted, resid, precision=HIGH)
        raw_gram = jnp.dot(weighted, fresh.T, precision=HIGH)
        packed = jnp.concatenate([raw_days.reshape(-1), jnp.pad(raw_gram.reshape(-1), (0, 124))]).reshape(-1, 128)
        packed = sum_all(packed).reshape(-1)
        raw_days = packed[: 2 * calendar_dates].reshape(2, calendar_dates)
        raw_gram = packed[2 * calendar_dates : 2 * calendar_dates + 4].reshape(2, 2)
        scale = jnp.sqrt(jnp.diagonal(raw_gram) / total + EPS)
        unit = fresh / scale[:, None]
        proj_days = raw_days / scale[:, None]
        gram_u = raw_gram / (scale[:, None] * scale[None, :])
        new_v = solve_pair(gram_u, proj_days)
        recon = others + jnp.dot(unit.T, new_v, precision=HIGH)
        modes_now = modes_now.at[low : low + 2].set(unit)
        panel = panel.at[low : low + 2].set(new_v)
    share = mode_series.shape[1]
    own_days = lax.dynamic_slice_in_dim(panel, lax.axis_index("lon") * share, share, 1)
    return (modes_now.reshape(modes, polar_coordinate, zonal_coordinate), own_days)


def solution(mesh):
    in_specs = (
        P("lat", "lon", None),
        P("lat", "lon", None),
        P("lat", "lon"),
        P(None, "lat", "lon"),
        P(None, "lon"),
    )
    out_specs = (P(None, "lat", "lon"), P(None, "lon"))
    return jax.shard_map(shards, mesh=mesh, in_specs=in_specs, out_specs=out_specs, check_vma=False)
```

```python
import functools

import jax
import jax.numpy as jnp
from jax import lax
from jax.experimental import pallas as pl
from jax.experimental.pallas import tpu as pltpu
from jax.sharding import PartitionSpec as P

STEPS = 4
SWEEPS = 4
PAIRS = 2 * STEPS
BITS = 15
LANES = 128

KLAT = 0.2
KLON = 0.05
EPS = 1e-06
F32 = jnp.float32
BF16 = jnp.bfloat16
VMEM = pl.BlockSpec(memory_space=pltpu.VMEM)
SMEM = pl.BlockSpec(memory_space=pltpu.SMEM)
NT = (((1,), (1,)), ((), ()))


def pairing(lat_map, lon_map):
    nlat, nlon = (lax.axis_size("lat"), lax.axis_size("lon"))
    return [(i * nlon + j, lat_map(i) * nlon + lon_map(j)) for i in range(nlat) for j in range(nlon)]


def swap(x, lat_bits, lon_bits):
    return lax.ppermute(x, ("lat", "lon"), pairing(lambda i: i ^ lat_bits, lambda j: j ^ lon_bits))


def sum_all(x):
    nlat, nlon = (lax.axis_size("lat"), lax.axis_size("lon"))
    if nlat & (nlat - 1) or nlon & (nlon - 1):
        return lax.psum(x, ("lat", "lon"))
    if nlon > 1:
        x = x + swap(x, 0, 1)
    for size, first, on_lat in ((nlat, 1, True), (nlon, 2, False)):
        bit = first
        while bit < size:
            bits = lambda b: (b, 0) if on_lat else (0, b)
            if 2 * bit < size:
                near, far, both = (swap(x, *bits(b)) for b in (bit, 2 * bit, 3 * bit))
                x = (x + near) + (far + both)
                bit *= 4
            else:
                x = x + swap(x, *bits(bit))
                bit *= 2
    return x


def lat_partners(x):
    count = lax.axis_size("lat")
    same = lambda j: j
    got_a = lax.ppermute(x, ("lat", "lon"), pairing(lambda i: i ^ 1, same))
    got_b = lax.ppermute(x, ("lat", "lon"), pairing(lambda i: (i + 1 if i % 2 else i - 1) % count, same))
    return got_a, got_b


def lon_ring(to_west, to_east):
    count = lax.axis_size("lon")
    up = [(i, (i + 1) % count) for i in range(count)]
    return lax.ppermute(to_east, "lon", up), lax.ppermute(to_west, "lon", [(j, i) for i, j in up])


def split(x):
    high = x.astype(BF16)
    return high, (x - high.astype(F32)).astype(BF16)


def solve_pair(g00, g01, g10, g11, right0, right1):
    determ = g00 * g11 - g01 * g10
    return (g11 * right0 - g01 * right1) / determ, (g00 * right1 - g10 * right0) / determ


def total_of(x):
    return jnp.sum(x, axis=1, keepdims=True)


def lane_ids(shape):
    return lax.broadcasted_iota(jnp.int32, shape, 1)


def to_block(field, rows, reach):
    n, own = (field.shape[0], rows * LANES)
    halo = field[:, own:]
    lane = lane_ids((n, LANES))
    parts = []
    for r in range(rows):
        east = pltpu.roll(halo, (LANES - rows * reach - reach * r) % LANES, 1)
        west = pltpu.roll(halo, (LANES - reach - reach * r) % LANES, 1)
        edge = jnp.where(lane < LANES // 2, east, west)
        parts.append(jnp.concatenate([field[:, r * LANES : (r + 1) * LANES], edge], axis=1))
    return jnp.concatenate(parts, axis=0)


def from_block(block, rows, reach):
    n = block.shape[0] // rows
    lane = lane_ids((n, LANES))
    halo = jnp.zeros((n, LANES), F32)
    own = []
    for r in range(rows):
        part = block[r * n : (r + 1) * n]
        own.append(part[:, :LANES])
        edge = part[:, LANES:]
        east = pltpu.roll(edge, (rows * reach + reach * r) % LANES, 1)
        west = pltpu.roll(edge, (reach * r + reach) % LANES, 1)
        first = reach * r
        halo = jnp.where((lane >= first) & (lane < first + reach), west, halo)
        first = rows * reach + reach * r
        halo = jnp.where((lane >= first) & (lane < first + reach), east, halo)
    return jnp.concatenate(own + [halo], axis=1)


def unpack_words(words, spread_ref, bit_ref):
    top = ((words >> 8) << 8).astype(F32).astype(BF16)
    bottom = (words & 255).astype(F32).astype(BF16)
    spread = spread_ref[...]
    each = jnp.dot(jnp.concatenate([top, bottom], axis=1), spread, preferred_element_type=F32).astype(jnp.int32)
    return jnp.where((each & bit_ref[...]) == 0, 1.0, 0.0).astype(BF16)


def fill_spread(spread_ref, bit_ref):
    days = spread_ref.shape[1]
    word = lax.broadcasted_iota(jnp.int32, (LANES, days), 0)
    rest = lane_ids((LANES, days)) - BITS * word
    hit = jnp.where((rest >= 0) & (rest < BITS), 1.0, 0.0).astype(BF16)
    spread_ref[:LANES] = hit
    spread_ref[LANES:] = hit
    word = jnp.where((rest >= 0) & (rest < BITS), rest, 0)
    bit_ref[...] = jnp.left_shift(1, jnp.sum(word, axis=0, keepdims=True))


def own_flags_kernel(words_ref, coast_ref, x_ref, m_ref, a_ref, spread_ref, bit_ref):
    @pl.when(pl.program_id(0) == 0)
    def _():
        fill_spread(spread_ref, bit_ref)

    coast = coast_ref[...]
    ocean = coast.astype(F32).astype(BF16)
    days = spread_ref.shape[1]
    for g in range(words_ref.shape[1] // LANES):
        words = words_ref[:, g * LANES : (g + 1) * LANES] * coast
        given = unpack_words(words, spread_ref, bit_ref)
        at = slice(g * days, (g + 1) * days)
        m_ref[:, at] = given
        a_ref[:, at] = x_ref[:, at] * given * ocean


def halo_flags_kernel(words_ref, coast_ref, m_ref, spread_ref, bit_ref):
    fill_spread(spread_ref, bit_ref)
    coast = coast_ref[...]
    days = spread_ref.shape[1]
    for g in range(words_ref.shape[1] // LANES):
        words = words_ref[:, g * LANES : (g + 1) * LANES] * coast
        m_ref[:, g * days : (g + 1) * days] = unpack_words(words, spread_ref, bit_ref)


def given_kernel(rows, reach, v_ref, a_ref, xv_ref, west_ref, east_ref):
    high, low = split(v_ref[:PAIRS])
    both = lax.dot_general(jnp.concatenate([high, low], axis=0), a_ref[...], NT, preferred_element_type=F32)
    xv = both[:PAIRS] + both[PAIRS:]
    xv_ref[...] = xv
    lane = lane_ids((PAIRS, LANES))
    west = jnp.zeros((PAIRS, LANES), F32)
    east = west
    for r in range(rows):
        part = xv[:, r * LANES : (r + 1) * LANES]
        first = rows * reach + reach * r
        west = jnp.where((lane >= first) & (lane < first + reach), pltpu.roll(part, first % LANES, 1), west)
        first = reach * r
        east = jnp.where((lane >= first) & (lane < first + reach), pltpu.roll(part, (first + reach) % LANES, 1), east)
    west_ref[...] = west
    east_ref[...] = east


def fields_kernel(step, rows, reach, total, chunk, *refs):
    m_ref, mh_ref, v_ref, u_ref, coast_ref, xv_ref, xw_ref, xe_ref = refs[:8]
    refs = refs[8:]
    older = refs[: 2 * max(step - 1, 0)]
    refs = refs[len(older) :]
    if step:
        sum_ref, block_ref = refs[:2]
        w_ref, vn_ref, un_ref, vs, us = refs[2:]
    else:
        w_ref, vs, us = refs
    days = v_ref.shape[1]
    low = 2 * step
    vs[...] = v_ref[...]
    us[...] = u_ref[...]
    for q in range(step - 1):
        vs[2 * q : 2 * q + 2] = older[2 * q][...]
        us[2 * q : 2 * q + 2] = older[2 * q + 1][...]
    if step:
        vn, un = new_pair(rows, reach, total, sum_ref, block_ref)
        vn_ref[...] = vn
        un_ref[...] = un
        vs[low - 2 : low] = vn
        us[low - 2 : low] = un
    modes = vs.shape[0]
    acc = accH = None
    for first in range(0, days, chunk):
        at = slice(first, first + chunk)
        v = vs[:, at]
        parts = []
        for j in (low, low + 1):
            parts.append(v * v[j : j + 1])
        high, lower = split(jnp.concatenate(parts, axis=0))
        left = jnp.concatenate([high, lower], axis=0)
        own = lax.dot_general(left, m_ref[:, at], NT, preferred_element_type=F32)
        halo = lax.dot_general(left, mh_ref[:, at], NT, preferred_element_type=F32)
        acc = own if acc is None else acc + own
        accH = halo if accH is None else accH + halo
    masked = jnp.concatenate([acc[: 2 * modes] + acc[2 * modes :], accH[: 2 * modes] + accH[2 * modes :]], axis=1)
    lane = lane_ids((PAIRS, LANES))
    xh = jnp.where(lane < LANES // 2, xw_ref[...], xe_ref[...])
    xv = jnp.concatenate([xv_ref[...], xh], axis=1)
    u = us[...]
    proj = [
        xv[low + j : low + j + 1] - jnp.sum(u * masked[j * modes : (j + 1) * modes], axis=0, keepdims=True)
        for j in range(2)
    ]
    v0, v1 = (vs[low : low + 1], vs[low + 1 : low + 2])
    h00, h01, h11 = (total_of(v0 * v0), total_of(v0 * v1), total_of(v1 * v1))
    add0, add1 = solve_pair(h00, h01, h01, h11, proj[0], proj[1])
    coast = coast_ref[...]
    fresh = coast * jnp.concatenate([u[low : low + 1] + add0, u[low + 1 : low + 2] + add1], axis=0)
    count = 2 * rows
    w_ref[:count] = to_block(fresh, rows, reach)
    if step == 0:
        w_ref[count:] = to_block(jnp.concatenate([coast, coast], axis=0), rows, reach)


def new_pair(rows, reach, total, sum_ref, block_ref):
    days = sum_ref.shape[1] - LANES
    gram = sum_ref[:, days:]
    g00, g01, g11 = (gram[0:1, 0:1], gram[0:1, 1:2], gram[1:2, 1:2])
    n0, n1 = (jnp.sqrt(g00 / total + EPS), jnp.sqrt(g11 / total + EPS))
    first, second = solve_pair(
        g00 / (n0 * n0),
        g01 / (n0 * n1),
        g01 / (n0 * n1),
        g11 / (n1 * n1),
        sum_ref[0:1, :days] / n0,
        sum_ref[1:2, :days] / n1,
    )
    field = from_block(block_ref[...], rows, reach)
    unit = jnp.concatenate([field[0:1] / n0, field[1:2] / n1], axis=0)
    return jnp.concatenate([first, second], axis=0), unit


def sums_kernel(step, rows, chunk, *refs):
    m_ref, a_ref, v_ref, u_ref, place_ref, klon_ref, cosl_ref, w_ref, ga_ref, gb_ref = refs[:10]
    refs = refs[10:]
    if step:
        cw_ref, ca_ref, cb_ref = refs[:3]
        refs = refs[3:]
    older = refs[: 2 * step]
    sum_ref, block_ref, vs, us = refs[2 * step :]
    days = v_ref.shape[1]
    low = 2 * step
    own = rows * LANES
    vs[...] = v_ref[...]
    us[...] = u_ref[:, :own]
    for q in range(step):
        vs[2 * q : 2 * q + 2] = older[2 * q][...]
        us[2 * q : 2 * q + 2] = older[2 * q + 1][:, :own]
    count = 2 * rows
    row0, nlat, odd = (place_ref[0], place_ref[1], place_ref[2])

    def assemble(mid, a, b):
        is_odd = odd == 1
        return jnp.concatenate([jnp.where(is_odd, a, b), mid, jnp.where(is_odd, b, a)], axis=0)

    w = assemble(w_ref[:count], ga_ref[:count], gb_ref[:count])
    if step:
        coast = assemble(cw_ref[count:], ca_ref[count:], cb_ref[count:])
    else:
        coast = assemble(w_ref[count:], ga_ref[count:], gb_ref[count:])
    tall = 3 * count
    row = row0 - rows + lax.broadcasted_iota(jnp.int32, (tall, 2 * LANES), 0) // 2
    coast = jnp.where((row >= 0) & (row < nlat), coast, 0.0)
    north = lambda z: pltpu.roll(z, 2, 0)
    south = lambda z: pltpu.roll(z, tall - 2, 0)
    west = lambda z: pltpu.roll(z, 1, 1)
    east = lambda z: pltpu.roll(z, 2 * LANES - 1, 1)
    cn, cs, cw, ce = (north(coast), south(coast), west(coast), east(coast))
    klon = klon_ref[...]
    for _ in range(SWEEPS):
        flux = KLAT * (cn * (north(w) - w) + cs * (south(w) - w)) + klon * (cw * (west(w) - w) + ce * (east(w) - w))
        w = w + coast * flux
    block = w[count : 2 * count]
    block_ref[...] = block
    cells = lambda z: jnp.concatenate([z[2 * r : 2 * r + 2, :LANES] for r in range(rows)], axis=1)
    fresh = cells(block)
    weighted = cells(block * cosl_ref[...])
    u = us[...]
    modes = u.shape[0]
    high, lower = split(jnp.concatenate([u * weighted[0:1], u * weighted[1:2]], axis=0))
    left = jnp.concatenate([high, lower], axis=0)
    high, lower = split(weighted)
    left_a = jnp.concatenate([high, lower], axis=0)
    lane = lane_ids((1, LANES))
    for j in range(2):
        gram = [total_of(weighted[j : j + 1] * fresh[i : i + 1]) for i in range(2)]
        sum_ref[j : j + 1, days:] = jnp.where(lane == 0, gram[0], jnp.where(lane == 1, gram[1], 0.0))
    old = [[total_of(weighted[j : j + 1] * u[low + i : low + i + 1]) for i in range(2)] for j in range(2)]
    for first in range(0, days, chunk):
        at = slice(first, first + chunk)
        masked = jnp.dot(left, m_ref[:, at], preferred_element_type=F32)
        given = jnp.dot(left_a, a_ref[:, at], preferred_element_type=F32)
        v = vs[:, at]
        for j in range(2):
            part = masked[j * modes : (j + 1) * modes] + masked[(2 + j) * modes : (3 + j) * modes]
            sum_ref[j : j + 1, at] = (
                given[j : j + 1]
                + given[2 + j : 3 + j]
                - jnp.sum(v * part, axis=0, keepdims=True)
                + old[j][0] * v[low : low + 1]
                + old[j][1] * v[low + 1 : low + 2]
            )


def last_kernel(rows, reach, total, sum_ref, block_ref, vn_ref, un_ref):
    vn, un = new_pair(rows, reach, total, sum_ref, block_ref)
    vn_ref[...] = vn
    un_ref[...] = un


def call(kernel, name, outs, scratch, args, smem=(), mib=24):
    return pl.pallas_call(
        kernel,
        out_shape=[jax.ShapeDtypeStruct(s, t) for s, t in outs],
        in_specs=[SMEM if i in smem else VMEM for i in range(len(args))],
        out_specs=[VMEM for _ in outs],
        scratch_shapes=[pltpu.VMEM(s, t) for s, t in scratch],
        compiler_params=pltpu.CompilerParams(vmem_limit_bytes=mib * 2**20),
        name=name,
    )(*args)


def latitude_cos(rows, nrows):
    degree = -60.0 + 120.0 * (rows.astype(F32) + 0.5) / nrows
    return jnp.cos(degree * (jnp.pi / 180.0))


def shards(sea_heat_deviations, missing_date_bitmask, ocean_binary_mask, mode_maps, mode_series):
    rows, columns, days = sea_heat_deviations.shape
    modes, words = (mode_maps.shape[0], missing_date_bitmask.shape[2])
    nlat = rows * lax.axis_size("lat")
    total = float(modes * nlat * columns * lax.axis_size("lon"))
    own, reach = (rows * columns, SWEEPS * STEPS)
    sides = 2 * rows * reach
    cells = own + sides
    assert columns == LANES and sides == LANES and rows == SWEEPS and days == BITS * words
    chunk = days // 5
    row0 = lax.axis_index("lat") * rows
    place = jnp.stack([row0, jnp.int32(nlat), lax.axis_index("lat") % 2]).astype(jnp.int32)
    tall = row0 - rows + jnp.arange(6 * rows) // 2
    cos_tall = latitude_cos(tall, nlat)[:, None]
    klon = jnp.broadcast_to(KLON / (cos_tall * cos_tall), (6 * rows, 2 * LANES))
    cosl = jnp.broadcast_to(cos_tall[2 * rows : 4 * rows], (2 * rows, 2 * LANES))

    fields = jnp.concatenate([mode_maps, ocean_binary_mask.astype(F32)[None]], axis=0)
    from_west, from_east = lon_ring(
        fields[:, :, :reach].reshape(modes + 1, -1), fields[:, :, columns - reach :].reshape(modes + 1, -1)
    )
    words_west, words_east = lon_ring(
        missing_date_bitmask[:, :reach].reshape(-1, words), missing_date_bitmask[:, columns - reach :].reshape(-1, words)
    )
    v = lax.all_gather(mode_series, "lon", axis=1, tiled=True)

    words_per = words // LANES
    spread = [pltpu.VMEM((2 * LANES, days // words_per), BF16), pltpu.VMEM((1, days // words_per), jnp.int32)]
    tile = LANES
    m, a = pl.pallas_call(
        own_flags_kernel,
        grid=(own // tile,),
        out_shape=[jax.ShapeDtypeStruct((own, days), BF16)] * 2,
        in_specs=[
            pl.BlockSpec((tile, words), lambda i: (i, 0)),
            pl.BlockSpec((tile, 1), lambda i: (i, 0)),
            pl.BlockSpec((tile, days), lambda i: (i, 0)),
        ],
        out_specs=[pl.BlockSpec((tile, days), lambda i: (i, 0))] * 2,
        scratch_shapes=spread,
        compiler_params=pltpu.CompilerParams(vmem_limit_bytes=24 * 2**20),
        name="own_flags",
    )(
        missing_date_bitmask.reshape(own, words),
        ocean_binary_mask.reshape(own, 1),
        sea_heat_deviations.reshape(own, days),
    )
    all_fields = jnp.concatenate([fields.reshape(modes + 1, own), from_west, from_east], axis=1)
    u, coast = (all_fields[:modes], all_fields[modes:])
    (m_halo,) = call(
        halo_flags_kernel,
        "halo_flags",
        [((sides, days), BF16)],
        [((2 * LANES, days // words_per), BF16), ((1, days // words_per), jnp.int32)],
        [jnp.concatenate([words_west, words_east], axis=0), coast[0, own:].astype(jnp.int32).reshape(sides, 1)],
    )
    xv, to_west, to_east = call(
        functools.partial(given_kernel, rows, reach),
        "given",
        [((PAIRS, own), F32), ((PAIRS, LANES), F32), ((PAIRS, LANES), F32)],
        [],
        [v, a],
    )
    xv_west, xv_east = lon_ring(to_west, to_east)

    count = 2 * rows
    news = []
    summed = block = None
    coasts = ()
    for step in range(STEPS):
        wide = 2 * count if step == 0 else count
        outs = [((wide, 2 * LANES), F32)]
        extra = []
        if step:
            outs += [((2, days), F32), ((2, cells), F32)]
            extra = [*news, summed, block]
        got = call(
            functools.partial(fields_kernel, step, rows, reach, total, chunk),
            f"fields_{step}",
            outs,
            [((modes, days), F32), ((modes, cells), F32)],
            [m, m_halo, v, u, coast, xv, xv_west, xv_east, *extra],
        )
        fresh = got[0]
        news += got[1:]
        got_a, got_b = lat_partners(fresh)
        partial_sums, block = call(
            functools.partial(sums_kernel, step, rows, chunk),
            f"sums_{step}",
            [((2, days + LANES), F32), ((count, 2 * LANES), F32)],
            [((modes, days), F32), ((modes, own), F32)],
            [m, a, v, u, place, klon, cosl, fresh, got_a, got_b, *coasts, *news],
            smem=(4,),
        )
        if step == 0:
            coasts = (fresh, got_a, got_b)
        summed = sum_all(partial_sums)
    news += call(
        functools.partial(last_kernel, rows, reach, total),
        "last",
        [((2, days), F32), ((2, cells), F32)],
        [],
        [summed, block],
    )
    share = mode_series.shape[1]
    new_v = jnp.concatenate(news[0::2], axis=0)
    new_u = jnp.concatenate([z[:, :own] for z in news[1::2]], axis=0).reshape(PAIRS, rows, columns)
    own_days = lax.dynamic_slice_in_dim(new_v, lax.axis_index("lon") * share, share, 1)
    return (
        jnp.concatenate([new_u, mode_maps[PAIRS:]], axis=0),
        jnp.concatenate([own_days, mode_series[PAIRS:]], axis=0),
    )


def solution(mesh):
    in_specs = (
        P("lat", "lon", None),
        P("lat", "lon", None),
        P("lat", "lon"),
        P(None, "lat", "lon"),
        P(None, "lon"),
    )
    out_specs = (P(None, "lat", "lon"), P(None, "lon"))
    return jax.shard_map(shards, mesh=mesh, in_specs=in_specs, out_specs=out_specs, check_vma=False)
```

```python
import functools

import jax
import jax.numpy as jnp
from jax import lax
from jax.experimental import pallas as pl
from jax.experimental.pallas import tpu as pltpu
from jax.sharding import PartitionSpec as P

STEPS = 4
SWEEPS = 4
PAIRS = 2 * STEPS
BITS = 15
LANES = 128

KLAT = 0.2
KLON = 0.05
EPS = 1e-06
F32 = jnp.float32
BF16 = jnp.bfloat16
VMEM = pl.BlockSpec(memory_space=pltpu.VMEM)
SMEM = pl.BlockSpec(memory_space=pltpu.SMEM)
NT = (((1,), (1,)), ((), ()))


def pairing(lat_map, lon_map):
    nlat, nlon = (lax.axis_size("lat"), lax.axis_size("lon"))
    return [(i * nlon + j, lat_map(i) * nlon + lon_map(j)) for i in range(nlat) for j in range(nlon)]


def swap(x, lat_bits, lon_bits):
    return lax.ppermute(x, ("lat", "lon"), pairing(lambda i: i ^ lat_bits, lambda j: j ^ lon_bits))


def sum_all(x):
    nlat, nlon = (lax.axis_size("lat"), lax.axis_size("lon"))
    if nlat & (nlat - 1) or nlon & (nlon - 1):
        return lax.psum(x, ("lat", "lon"))
    core = 1 if nlon > 1 else 0
    if core:
        x = x + swap(x, 0, core)
    for size, first, on_lat in ((nlat, 1, True), (nlon, 2, False)):
        bit = first
        while bit < size:
            bits = lambda b: (b, core) if on_lat else (0, b | core)
            if 2 * bit < size:
                near, far, both = (swap(x, *bits(b)) for b in (bit, 2 * bit, 3 * bit))
                x = (x + near) + (far + both)
                bit *= 4
            else:
                x = x + swap(x, *bits(bit))
                bit *= 2
    return x


def lat_partners(x):
    count = lax.axis_size("lat")
    same = lambda j: j
    got_a = lax.ppermute(x, ("lat", "lon"), pairing(lambda i: i ^ 1, same))
    got_b = lax.ppermute(x, ("lat", "lon"), pairing(lambda i: (i + 1 if i % 2 else i - 1) % count, same))
    return got_a, got_b


def lon_ring(to_west, to_east):
    count = lax.axis_size("lon")
    up = [(i, (i + 1) % count) for i in range(count)]
    return lax.ppermute(to_east, "lon", up), lax.ppermute(to_west, "lon", [(j, i) for i, j in up])


def split(x):
    high = x.astype(BF16)
    return high, (x - high.astype(F32)).astype(BF16)


def solve_pair(g00, g01, g10, g11, right0, right1):
    determ = g00 * g11 - g01 * g10
    return (g11 * right0 - g01 * right1) / determ, (g00 * right1 - g10 * right0) / determ


def total_of(x):
    return jnp.sum(x, axis=1, keepdims=True)


def lane_ids(shape):
    return lax.broadcasted_iota(jnp.int32, shape, 1)


def to_block(field, rows, reach):
    n, own = (field.shape[0], rows * LANES)
    halo = field[:, own:]
    lane = lane_ids((n, LANES))
    parts = []
    for r in range(rows):
        east = pltpu.roll(halo, (LANES - rows * reach - reach * r) % LANES, 1)
        west = pltpu.roll(halo, (LANES - reach - reach * r) % LANES, 1)
        edge = jnp.where(lane < LANES // 2, east, west)
        parts.append(jnp.concatenate([field[:, r * LANES : (r + 1) * LANES], edge], axis=1))
    return jnp.concatenate(parts, axis=0)


def from_block(block, rows, reach):
    n = block.shape[0] // rows
    lane = lane_ids((n, LANES))
    halo = jnp.zeros((n, LANES), F32)
    own = []
    for r in range(rows):
        part = block[r * n : (r + 1) * n]
        own.append(part[:, :LANES])
        edge = part[:, LANES:]
        east = pltpu.roll(edge, (rows * reach + reach * r) % LANES, 1)
        west = pltpu.roll(edge, (reach * r + reach) % LANES, 1)
        first = reach * r
        halo = jnp.where((lane >= first) & (lane < first + reach), west, halo)
        first = rows * reach + reach * r
        halo = jnp.where((lane >= first) & (lane < first + reach), east, halo)
    return jnp.concatenate(own + [halo], axis=1)


def unpack_words(words, spread_ref, bit_ref):
    top = ((words >> 8) << 8).astype(F32).astype(BF16)
    bottom = (words & 255).astype(F32).astype(BF16)
    spread = spread_ref[...]
    each = jnp.dot(jnp.concatenate([top, bottom], axis=1), spread, preferred_element_type=F32).astype(jnp.int32)
    return jnp.where((each & bit_ref[...]) == 0, 1.0, 0.0).astype(BF16)


def fill_spread(spread_ref, bit_ref):
    days = spread_ref.shape[1]
    word = lax.broadcasted_iota(jnp.int32, (LANES, days), 0)
    rest = lane_ids((LANES, days)) - BITS * word
    hit = jnp.where((rest >= 0) & (rest < BITS), 1.0, 0.0).astype(BF16)
    spread_ref[:LANES] = hit
    spread_ref[LANES:] = hit
    word = jnp.where((rest >= 0) & (rest < BITS), rest, 0)
    bit_ref[...] = jnp.left_shift(1, jnp.sum(word, axis=0, keepdims=True))


def as_column(row):
    return jnp.transpose(jnp.broadcast_to(row, (8, LANES)))[:, :1]


def own_flags_kernel(words_ref, coast_ref, x_ref, m_ref, a_ref, spread_ref, bit_ref):
    @pl.when(pl.program_id(0) == 0)
    def _():
        fill_spread(spread_ref, bit_ref)

    coast = as_column(coast_ref[pl.ds(pl.program_id(0), 1), :].astype(F32))
    ocean = coast.astype(BF16)
    coast = coast.astype(jnp.int32)
    days = spread_ref.shape[1]
    for g in range(words_ref.shape[1] // LANES):
        words = words_ref[:, g * LANES : (g + 1) * LANES] * coast
        given = unpack_words(words, spread_ref, bit_ref)
        at = slice(g * days, (g + 1) * days)
        m_ref[:, at] = given
        a_ref[:, at] = x_ref[:, at] * given * ocean


def edges(pieces, reach):
    rows = len(pieces)
    shape = pieces[0].shape
    lane = lane_ids(shape)
    west = jnp.zeros(shape, F32)
    east = west
    for r, part in enumerate(pieces):
        first = rows * reach + reach * r
        west = jnp.where((lane >= first) & (lane < first + reach), pltpu.roll(part, first % LANES, 1), west)
        first = reach * r
        east = jnp.where((lane >= first) & (lane < first + reach), pltpu.roll(part, (first + reach) % LANES, 1), east)
    return west, east


def prep_kernel(reach, maps_ref, coast_ref, words_ref, u_ref, row_ref, west_ref, east_ref):
    modes, rows = maps_ref.shape[:2]
    coast = coast_ref[...].astype(F32)
    pieces = []
    for r in range(rows):
        at = slice(r * LANES, (r + 1) * LANES)
        u = maps_ref[:, r, :]
        u_ref[:, at] = u
        row_ref[:, at] = coast[r : r + 1]
        pieces.append(jnp.concatenate([u, jnp.broadcast_to(coast[r : r + 1], (8, LANES))], axis=0))
    west, east = edges(pieces, reach)
    base = modes + 8
    west_ref[:base] = west
    east_ref[:base] = east
    for g in range(words_ref.shape[2] // LANES):
        for r in range(rows):
            at = slice(base + reach * (rows * g + r), base + reach * (rows * g + r + 1))
            west_ref[at] = words_ref[r, :reach, g * LANES : (g + 1) * LANES].astype(F32)
            east_ref[at] = words_ref[r, LANES - reach :, g * LANES : (g + 1) * LANES].astype(F32)


def halo_flags_kernel(modes, west_ref, east_ref, m_ref, u_ref, row_ref, spread_ref, bit_ref):
    fill_spread(spread_ref, bit_ref)
    base = modes + 8
    lane = lane_ids((base, LANES))
    fields = jnp.where(lane < LANES // 2, west_ref[:base], east_ref[:base])
    u_ref[...] = fields[:modes]
    row_ref[...] = fields[modes : modes + 1]
    coast = as_column(fields[modes : modes + 1]).astype(jnp.int32)
    days = spread_ref.shape[1]
    half = LANES // 2
    for g in range(m_ref.shape[1] // days):
        at = slice(base + half * g, base + half * (g + 1))
        words = jnp.concatenate([west_ref[at], east_ref[at]], axis=0).astype(jnp.int32) * coast
        m_ref[:, g * days : (g + 1) * days] = unpack_words(words, spread_ref, bit_ref)


def given_kernel(rows, reach, *refs):
    a_ref, place_ref = refs[:2]
    pieces = [ref[...] for ref in refs[2:-4]]
    v_ref, xv_ref, west_ref, east_ref = refs[-4:]
    here = place_ref[3]
    bit = 1
    while bit < len(pieces):
        turn = (here // bit) % 2 == 1
        pieces = [jnp.where(turn, pieces[i ^ bit], pieces[i]) for i in range(len(pieces))]
        bit *= 2
    share = pieces[0].shape[1]
    for i, piece in enumerate(pieces):
        v_ref[:, i * share : (i + 1) * share] = piece
    high, low = split(v_ref[:PAIRS])
    both = lax.dot_general(jnp.concatenate([high, low], axis=0), a_ref[...], NT, preferred_element_type=F32)
    xv = both[:PAIRS] + both[PAIRS:]
    xv_ref[...] = xv
    west_ref[...], east_ref[...] = edges([xv[:, r * LANES : (r + 1) * LANES] for r in range(rows)], reach)


def fields_kernel(step, rows, reach, total, chunk, *refs):
    m_ref, mh_ref, v_ref, u_ref, uh_ref, coast_ref, coasth_ref, xv_ref, xw_ref, xe_ref = refs[:10]
    refs = refs[10:]
    older = refs[: 2 * max(step - 1, 0)]
    refs = refs[len(older) :]
    if step:
        sum_ref, block_ref = refs[:2]
        w_ref, vn_ref, un_ref, vs, us = refs[2:]
    else:
        w_ref, vs, us = refs
    days = v_ref.shape[1]
    low = 2 * step
    own = rows * LANES
    vs[...] = v_ref[...]
    us[:, :own] = u_ref[...]
    us[:, own:] = uh_ref[...]
    for q in range(step - 1):
        vs[2 * q : 2 * q + 2] = older[2 * q][...]
        us[2 * q : 2 * q + 2] = older[2 * q + 1][...]
    if step:
        vn, un = new_pair(rows, reach, total, sum_ref, block_ref)
        vn_ref[...] = vn
        un_ref[...] = un
        vs[low - 2 : low] = vn
        us[low - 2 : low] = un
    modes = vs.shape[0]
    acc = acc_h = None
    for first in range(0, days, chunk):
        at = slice(first, first + chunk)
        v = vs[:, at]
        parts = []
        for j in (low, low + 1):
            parts.append(v * v[j : j + 1])
        high, lower = split(jnp.concatenate(parts, axis=0))
        left = jnp.concatenate([high, lower], axis=0)
        mid = lax.dot_general(left, m_ref[:, at], NT, preferred_element_type=F32)
        edge = lax.dot_general(left, mh_ref[:, at], NT, preferred_element_type=F32)
        acc = mid if acc is None else acc + mid
        acc_h = edge if acc_h is None else acc_h + edge
    masked = jnp.concatenate([acc[: 2 * modes] + acc[2 * modes :], acc_h[: 2 * modes] + acc_h[2 * modes :]], axis=1)
    lane = lane_ids((PAIRS, LANES))
    xh = jnp.where(lane < LANES // 2, xw_ref[...], xe_ref[...])
    xv = jnp.concatenate([xv_ref[...], xh], axis=1)
    u = us[...]
    proj = [
        xv[low + j : low + j + 1] - jnp.sum(u * masked[j * modes : (j + 1) * modes], axis=0, keepdims=True)
        for j in range(2)
    ]
    v0, v1 = (vs[low : low + 1], vs[low + 1 : low + 2])
    h00, h01, h11 = (total_of(v0 * v0), total_of(v0 * v1), total_of(v1 * v1))
    add0, add1 = solve_pair(h00, h01, h01, h11, proj[0], proj[1])
    coast = jnp.concatenate([coast_ref[...], coasth_ref[...]], axis=1)
    fresh = coast * jnp.concatenate([u[low : low + 1] + add0, u[low + 1 : low + 2] + add1], axis=0)
    count = 2 * rows
    w_ref[:count] = to_block(fresh, rows, reach)
    if step == 0:
        w_ref[count:] = to_block(jnp.concatenate([coast, coast], axis=0), rows, reach)


def new_pair(rows, reach, total, sum_ref, block_ref):
    days = sum_ref.shape[1] - LANES
    gram = sum_ref[:, days:]
    g00, g01, g11 = (gram[0:1, 0:1], gram[0:1, 1:2], gram[1:2, 1:2])
    n0, n1 = (jnp.sqrt(g00 / total + EPS), jnp.sqrt(g11 / total + EPS))
    first, second = solve_pair(
        g00 / (n0 * n0),
        g01 / (n0 * n1),
        g01 / (n0 * n1),
        g11 / (n1 * n1),
        sum_ref[0:1, :days] / n0,
        sum_ref[1:2, :days] / n1,
    )
    field = from_block(block_ref[...], rows, reach)
    unit = jnp.concatenate([field[0:1] / n0, field[1:2] / n1], axis=0)
    return jnp.concatenate([first, second], axis=0), unit


def sums_kernel(step, rows, chunk, *refs):
    m_ref, a_ref, v_ref, u_ref, place_ref, klon_ref, cosl_ref, w_ref, ga_ref, gb_ref = refs[:10]
    refs = refs[10:]
    if step:
        cw_ref, ca_ref, cb_ref = refs[:3]
        refs = refs[3:]
    older = refs[: 2 * step]
    sum_ref, block_ref, vs, us = refs[2 * step :]
    days = v_ref.shape[1]
    low = 2 * step
    own = rows * LANES
    vs[...] = v_ref[...]
    us[...] = u_ref[...]
    for q in range(step):
        vs[2 * q : 2 * q + 2] = older[2 * q][...]
        us[2 * q : 2 * q + 2] = older[2 * q + 1][:, :own]
    count = 2 * rows
    row0, nlat, odd = (place_ref[0], place_ref[1], place_ref[2])

    def assemble(mid, a, b):
        is_odd = odd == 1
        return jnp.concatenate([jnp.where(is_odd, a, b), mid, jnp.where(is_odd, b, a)], axis=0)

    w = assemble(w_ref[:count], ga_ref[:count], gb_ref[:count])
    if step:
        coast = assemble(cw_ref[count:], ca_ref[count:], cb_ref[count:])
    else:
        coast = assemble(w_ref[count:], ga_ref[count:], gb_ref[count:])
    tall = 3 * count
    row = row0 - rows + lax.broadcasted_iota(jnp.int32, (tall, 2 * LANES), 0) // 2
    coast = jnp.where((row >= 0) & (row < nlat), coast, 0.0)
    north = lambda z: pltpu.roll(z, 2, 0)
    south = lambda z: pltpu.roll(z, tall - 2, 0)
    west = lambda z: pltpu.roll(z, 1, 1)
    east = lambda z: pltpu.roll(z, 2 * LANES - 1, 1)
    cn, cs, cw, ce = (north(coast), south(coast), west(coast), east(coast))
    klon = klon_ref[...]
    for _ in range(SWEEPS):
        flux = KLAT * (cn * (north(w) - w) + cs * (south(w) - w)) + klon * (cw * (west(w) - w) + ce * (east(w) - w))
        w = w + coast * flux
    block = w[count : 2 * count]
    block_ref[...] = block
    cells = lambda z: jnp.concatenate([z[2 * r : 2 * r + 2, :LANES] for r in range(rows)], axis=1)
    fresh = cells(block)
    weighted = cells(block * cosl_ref[...])
    u = us[...]
    modes = u.shape[0]
    high, lower = split(jnp.concatenate([u * weighted[0:1], u * weighted[1:2]], axis=0))
    left = jnp.concatenate([high, lower], axis=0)
    high, lower = split(weighted)
    left_a = jnp.concatenate([high, lower], axis=0)
    lane = lane_ids((1, LANES))
    for j in range(2):
        gram = [total_of(weighted[j : j + 1] * fresh[i : i + 1]) for i in range(2)]
        sum_ref[j : j + 1, days:] = jnp.where(lane == 0, gram[0], jnp.where(lane == 1, gram[1], 0.0))
    old = [[total_of(weighted[j : j + 1] * u[low + i : low + i + 1]) for i in range(2)] for j in range(2)]
    for first in range(0, days, chunk):
        at = slice(first, first + chunk)
        masked = jnp.dot(left, m_ref[:, at], preferred_element_type=F32)
        given = jnp.dot(left_a, a_ref[:, at], preferred_element_type=F32)
        v = vs[:, at]
        for j in range(2):
            part = masked[j * modes : (j + 1) * modes] + masked[(2 + j) * modes : (3 + j) * modes]
            sum_ref[j : j + 1, at] = (
                given[j : j + 1]
                + given[2 + j : 3 + j]
                - jnp.sum(v * part, axis=0, keepdims=True)
                + old[j][0] * v[low : low + 1]
                + old[j][1] * v[low + 1 : low + 2]
            )


def last_kernel(rows, reach, total, sum_ref, block_ref, vn_ref, un_ref):
    vn, un = new_pair(rows, reach, total, sum_ref, block_ref)
    vn_ref[...] = vn
    un_ref[...] = un


def call(kernel, name, outs, scratch, args, smem=(), mib=24, flops=0):
    moved = sum(z.size * z.dtype.itemsize for z in args)
    return pl.pallas_call(
        kernel,
        out_shape=[jax.ShapeDtypeStruct(s, t) for s, t in outs],
        in_specs=[SMEM if i in smem else VMEM for i in range(len(args))],
        out_specs=[VMEM for _ in outs],
        scratch_shapes=[pltpu.VMEM(s, t) for s, t in scratch],
        compiler_params=pltpu.CompilerParams(vmem_limit_bytes=mib * 2**20),
        cost_estimate=pl.CostEstimate(flops=flops, bytes_accessed=moved, transcendentals=0),
        name=name,
    )(*args)


def latitude_cos(rows, nrows):
    degree = -60.0 + 120.0 * (rows.astype(F32) + 0.5) / nrows
    return jnp.cos(degree * (jnp.pi / 180.0))


def shards(sea_heat_deviations, missing_date_bitmask, ocean_binary_mask, mode_maps, mode_series):
    rows, columns, days = sea_heat_deviations.shape
    modes, words = (mode_maps.shape[0], missing_date_bitmask.shape[2])
    nlat = rows * lax.axis_size("lat")
    total = float(modes * nlat * columns * lax.axis_size("lon"))
    own, reach = (rows * columns, SWEEPS * STEPS)
    sides = 2 * rows * reach
    cells = own + sides
    assert columns == LANES and sides == LANES and rows == SWEEPS and days == BITS * words
    chunk = days // 5
    row0 = lax.axis_index("lat") * rows
    here = lax.axis_index("lon")
    place = jnp.stack([row0, jnp.int32(nlat), lax.axis_index("lat") % 2, here]).astype(jnp.int32)
    tall = row0 - rows + jnp.arange(6 * rows) // 2
    cos_tall = latitude_cos(tall, nlat)[:, None]
    klon = jnp.broadcast_to(KLON / (cos_tall * cos_tall), (6 * rows, 2 * LANES))
    cosl = jnp.broadcast_to(cos_tall[2 * rows : 4 * rows], (2 * rows, 2 * LANES))

    tall_edge = modes + 8 + rows * reach * (words // LANES)
    u, coast, to_west, to_east = call(
        functools.partial(prep_kernel, reach),
        "prep",
        [((modes, own), F32), ((1, own), F32), ((tall_edge, LANES), F32), ((tall_edge, LANES), F32)],
        [],
        [mode_maps, ocean_binary_mask, missing_date_bitmask],
    )
    from_west, from_east = lon_ring(to_west, to_east)
    nlon = lax.axis_size("lon")
    if nlon == 8:
        pieces = [mode_series] + [swap(mode_series, 0, b) for b in (2, 4, 6)]
        pieces = [z for piece in pieces for z in (piece, swap(piece, 0, 1))]
    else:
        pieces = [lax.all_gather(mode_series, "lon", axis=1, tiled=True)]

    words_per = words // LANES
    flags_scratch = [((2 * LANES, days // words_per), BF16), ((1, days // words_per), jnp.int32)]
    x = pltpu.with_memory_space_constraint(sea_heat_deviations.reshape(own, days), pltpu.HBM)
    m, a = pl.pallas_call(
        own_flags_kernel,
        grid=(rows,),
        out_shape=[jax.ShapeDtypeStruct((own, days), BF16)] * 2,
        in_specs=[
            pl.BlockSpec((LANES, words), lambda i: (i, 0)),
            pl.BlockSpec((rows, LANES), lambda i: (0, 0)),
            pl.BlockSpec((LANES, days), lambda i: (i, 0)),
        ],
        out_specs=[pl.BlockSpec((LANES, days), lambda i: (i, 0))] * 2,
        scratch_shapes=[pltpu.VMEM(s, t) for s, t in flags_scratch],
        compiler_params=pltpu.CompilerParams(vmem_limit_bytes=24 * 2**20),
        cost_estimate=pl.CostEstimate(flops=4 * LANES * own * days, bytes_accessed=6 * own * days, transcendentals=0),
        name="own_flags",
    )(missing_date_bitmask.reshape(own, words), ocean_binary_mask, x)
    m_halo, u_halo, coast_halo = call(
        functools.partial(halo_flags_kernel, modes),
        "halo_flags",
        [((sides, days), BF16), ((modes, sides), F32), ((1, sides), F32)],
        flags_scratch,
        [from_west, from_east],
        flops=4 * LANES * sides * days,
    )
    v, xv, to_west, to_east = call(
        functools.partial(given_kernel, rows, reach),
        "given",
        [((modes, days), F32), ((PAIRS, own), F32), ((PAIRS, LANES), F32), ((PAIRS, LANES), F32)],
        [],
        [a, place, *pieces],
        smem=(1,),
        flops=4 * PAIRS * own * days,
    )
    xv_west, xv_east = lon_ring(to_west, to_east)

    count = 2 * rows
    news = []
    summed = block = None
    coasts = ()
    for step in range(STEPS):
        wide = 2 * count if step == 0 else count
        outs = [((wide, 2 * LANES), F32)]
        extra = []
        if step:
            outs += [((2, days), F32), ((2, cells), F32)]
            extra = [*news, summed, block]
        got = call(
            functools.partial(fields_kernel, step, rows, reach, total, chunk),
            f"fields_{step}",
            outs,
            [((modes, days), F32), ((modes, cells), F32)],
            [m, m_halo, v, u, u_halo, coast, coast_halo, xv, xv_west, xv_east, *extra],
            flops=8 * modes * cells * days,
        )
        fresh = got[0]
        news += got[1:]
        got_a, got_b = lat_partners(fresh)
        partial_sums, block = call(
            functools.partial(sums_kernel, step, rows, chunk),
            f"sums_{step}",
            [((2, days + LANES), F32), ((count, 2 * LANES), F32)],
            [((modes, days), F32), ((modes, own), F32)],
            [m, a, v, u, place, klon, cosl, fresh, got_a, got_b, *coasts, *news],
            smem=(4,),
            flops=8 * modes * own * days,
        )
        if step == 0:
            coasts = (fresh, got_a, got_b)
        summed = sum_all(partial_sums)
    news += call(
        functools.partial(last_kernel, rows, reach, total),
        "last",
        [((2, days), F32), ((2, cells), F32)],
        [],
        [summed, block],
    )
    share = mode_series.shape[1]
    new_v = jnp.concatenate(news[0::2], axis=0)
    new_u = jnp.concatenate([z[:, :own] for z in news[1::2]], axis=0).reshape(PAIRS, rows, columns)
    own_days = lax.dynamic_slice_in_dim(new_v, lax.axis_index("lon") * share, share, 1)
    return (
        jnp.concatenate([new_u, mode_maps[PAIRS:]], axis=0),
        jnp.concatenate([own_days, mode_series[PAIRS:]], axis=0),
    )


def solution(mesh):
    in_specs = (
        P("lat", "lon", None),
        P("lat", "lon", None),
        P("lat", "lon"),
        P(None, "lat", "lon"),
        P(None, "lon"),
    )
    out_specs = (P(None, "lat", "lon"), P(None, "lon"))
    return jax.shard_map(shards, mesh=mesh, in_specs=in_specs, out_specs=out_specs, check_vma=False)
```

```python
import functools

import jax
import jax.numpy as jnp
from jax import lax
from jax.experimental import pallas as pl
from jax.experimental.pallas import tpu as pltpu
from jax.sharding import PartitionSpec as P

STEPS = 4
SWEEPS = 4
PAIRS = 2 * STEPS
BITS = 15
LANES = 128

KLAT = 0.2
KLON = 0.05
EPS = 1e-06
F32 = jnp.float32
BF16 = jnp.bfloat16
VMEM = pl.BlockSpec(memory_space=pltpu.VMEM)
SMEM = pl.BlockSpec(memory_space=pltpu.SMEM)
NT = (((1,), (1,)), ((), ()))


def pairing(lat_map, lon_map):
    nlat, nlon = (lax.axis_size("lat"), lax.axis_size("lon"))
    return [(i * nlon + j, lat_map(i) * nlon + lon_map(j)) for i in range(nlat) for j in range(nlon)]


def swap(x, lat_bits, lon_bits):
    return lax.ppermute(x, ("lat", "lon"), pairing(lambda i: i ^ lat_bits, lambda j: j ^ lon_bits))


def sum_all(x):
    nlat, nlon = (lax.axis_size("lat"), lax.axis_size("lon"))
    if nlat & (nlat - 1) or nlon & (nlon - 1):
        return lax.psum(x, ("lat", "lon"))
    core = 1 if nlon > 1 else 0
    if core:
        x = x + swap(x, 0, core)
    for size, first, on_lat in ((nlat, 1, True), (nlon, 2, False)):
        bit = first
        while bit < size:
            bits = lambda b: (b, core) if on_lat else (0, b | core)
            if 2 * bit < size:
                near, far, both = (swap(x, *bits(b)) for b in (bit, 2 * bit, 3 * bit))
                x = (x + near) + (far + both)
                bit *= 4
            else:
                x = x + swap(x, *bits(bit))
                bit *= 2
    return x


def lat_partners(x):
    count = lax.axis_size("lat")
    same = lambda j: j
    got_a = lax.ppermute(x, ("lat", "lon"), pairing(lambda i: i ^ 1, same))
    got_b = lax.ppermute(x, ("lat", "lon"), pairing(lambda i: (i + 1 if i % 2 else i - 1) % count, same))
    return got_a, got_b


def lon_ring(to_west, to_east):
    count = lax.axis_size("lon")
    up = [(i, (i + 1) % count) for i in range(count)]
    return lax.ppermute(to_east, "lon", up), lax.ppermute(to_west, "lon", [(j, i) for i, j in up])


def split(x):
    high = x.astype(BF16)
    return high, (x - high.astype(F32)).astype(BF16)


def solve_pair(g00, g01, g10, g11, right0, right1):
    determ = g00 * g11 - g01 * g10
    return (g11 * right0 - g01 * right1) / determ, (g00 * right1 - g10 * right0) / determ


def total_of(x):
    return jnp.sum(x, axis=1, keepdims=True)


def lane_ids(shape):
    return lax.broadcasted_iota(jnp.int32, shape, 1)


def to_block(field, rows, reach):
    n, own = (field.shape[0], rows * LANES)
    halo = field[:, own:]
    lane = lane_ids((n, LANES))
    parts = []
    for r in range(rows):
        east = pltpu.roll(halo, (LANES - rows * reach - reach * r) % LANES, 1)
        west = pltpu.roll(halo, (LANES - reach - reach * r) % LANES, 1)
        edge = jnp.where(lane < LANES // 2, east, west)
        parts.append(jnp.concatenate([field[:, r * LANES : (r + 1) * LANES], edge], axis=1))
    return jnp.concatenate(parts, axis=0)


def from_block(block, rows, reach):
    n = block.shape[0] // rows
    lane = lane_ids((n, LANES))
    halo = jnp.zeros((n, LANES), F32)
    own = []
    for r in range(rows):
        part = block[r * n : (r + 1) * n]
        own.append(part[:, :LANES])
        edge = part[:, LANES:]
        east = pltpu.roll(edge, (rows * reach + reach * r) % LANES, 1)
        west = pltpu.roll(edge, (reach * r + reach) % LANES, 1)
        first = reach * r
        halo = jnp.where((lane >= first) & (lane < first + reach), west, halo)
        first = rows * reach + reach * r
        halo = jnp.where((lane >= first) & (lane < first + reach), east, halo)
    return jnp.concatenate(own + [halo], axis=1)


def unpack_words(words, spread_ref, bit_ref):
    top = ((words >> 8) << 8).astype(F32).astype(BF16)
    bottom = (words & 255).astype(F32).astype(BF16)
    spread = spread_ref[...]
    each = jnp.dot(jnp.concatenate([top, bottom], axis=1), spread, preferred_element_type=F32).astype(jnp.int32)
    return jnp.where((each & bit_ref[...]) == 0, 1.0, 0.0).astype(BF16)


def fill_spread(spread_ref, bit_ref):
    days = spread_ref.shape[1]
    word = lax.broadcasted_iota(jnp.int32, (LANES, days), 0)
    rest = lane_ids((LANES, days)) - BITS * word
    hit = jnp.where((rest >= 0) & (rest < BITS), 1.0, 0.0).astype(BF16)
    spread_ref[:LANES] = hit
    spread_ref[LANES:] = hit
    word = jnp.where((rest >= 0) & (rest < BITS), rest, 0)
    bit_ref[...] = jnp.left_shift(1, jnp.sum(word, axis=0, keepdims=True))


def as_column(row):
    return jnp.transpose(jnp.broadcast_to(row, (8, LANES)))[:, :1]


def own_flags_kernel(words_hbm, coast_hbm, x_hbm, m_ref, a_ref, words_ref, coast_ref, x_ref, spread_ref, bit_ref, sems):
    rows = coast_ref.shape[0]
    loads = [pltpu.make_async_copy(words_hbm, words_ref, sems.at[0]), pltpu.make_async_copy(coast_hbm, coast_ref, sems.at[1])]
    for r in range(rows):
        at = pl.ds(r * LANES, LANES)
        loads.append(pltpu.make_async_copy(x_hbm.at[at], x_ref.at[at], sems.at[2 + r]))
    for load in loads:
        load.start()
    fill_spread(spread_ref, bit_ref)
    loads[0].wait()
    loads[1].wait()
    days = spread_ref.shape[1]
    coasts = jnp.transpose(jnp.concatenate([coast_ref[...].astype(F32)] * (8 // rows), axis=0))
    for r in range(rows):
        coast = coasts[:, r : r + 1]
        ocean = coast.astype(BF16)
        coast = coast.astype(jnp.int32)
        loads[2 + r].wait()
        cell = slice(r * LANES, (r + 1) * LANES)
        for g in range(words_ref.shape[1] // LANES):
            words = words_ref[cell, g * LANES : (g + 1) * LANES] * coast
            given = unpack_words(words, spread_ref, bit_ref)
            at = slice(g * days, (g + 1) * days)
            m_ref[cell, at] = given
            a_ref[cell, at] = x_ref[cell, at] * given * ocean


def edges(pieces, reach):
    rows = len(pieces)
    shape = pieces[0].shape
    lane = lane_ids(shape)
    west = jnp.zeros(shape, F32)
    east = west
    for r, part in enumerate(pieces):
        first = rows * reach + reach * r
        west = jnp.where((lane >= first) & (lane < first + reach), pltpu.roll(part, first % LANES, 1), west)
        first = reach * r
        east = jnp.where((lane >= first) & (lane < first + reach), pltpu.roll(part, (first + reach) % LANES, 1), east)
    return west, east


def prep_kernel(reach, maps_hbm, coast_hbm, words_hbm, u_ref, row_ref, west_ref, east_ref, maps_ref, coast_ref, first_ref, last_ref, sems):
    loads = [
        pltpu.make_async_copy(maps_hbm, maps_ref, sems.at[0]),
        pltpu.make_async_copy(coast_hbm, coast_ref, sems.at[1]),
        pltpu.make_async_copy(words_hbm.at[:, pl.ds(0, reach)], first_ref, sems.at[2]),
        pltpu.make_async_copy(words_hbm.at[:, pl.ds(LANES - reach, reach)], last_ref, sems.at[3]),
    ]
    for load in loads:
        load.start()
    for load in loads:
        load.wait()
    modes, rows = maps_ref.shape[:2]
    coast = coast_ref[...].astype(F32)
    pieces = []
    for r in range(rows):
        at = slice(r * LANES, (r + 1) * LANES)
        u = maps_ref[:, r, :]
        u_ref[:, at] = u
        row_ref[:, at] = coast[r : r + 1]
        pieces.append(jnp.concatenate([u, jnp.broadcast_to(coast[r : r + 1], (8, LANES))], axis=0))
    west, east = edges(pieces, reach)
    base = modes + 8
    west_ref[:base] = west
    east_ref[:base] = east
    for g in range(first_ref.shape[2] // LANES):
        for r in range(rows):
            at = slice(base + reach * (rows * g + r), base + reach * (rows * g + r + 1))
            west_ref[at] = first_ref[r, :, g * LANES : (g + 1) * LANES].astype(F32)
            east_ref[at] = last_ref[r, :, g * LANES : (g + 1) * LANES].astype(F32)


def halo_flags_kernel(modes, west_ref, east_ref, m_ref, u_ref, row_ref, spread_ref, bit_ref):
    fill_spread(spread_ref, bit_ref)
    base = modes + 8
    lane = lane_ids((base, LANES))
    fields = jnp.where(lane < LANES // 2, west_ref[:base], east_ref[:base])
    u_ref[...] = fields[:modes]
    row_ref[...] = fields[modes : modes + 1]
    coast = as_column(fields[modes : modes + 1]).astype(jnp.int32)
    days = spread_ref.shape[1]
    half = LANES // 2
    for g in range(m_ref.shape[1] // days):
        at = slice(base + half * g, base + half * (g + 1))
        words = jnp.concatenate([west_ref[at], east_ref[at]], axis=0).astype(jnp.int32) * coast
        m_ref[:, g * days : (g + 1) * days] = unpack_words(words, spread_ref, bit_ref)


def given_kernel(rows, reach, *refs):
    a_ref, place_ref = refs[:2]
    pieces = [ref[...] for ref in refs[2:-4]]
    v_ref, xv_ref, west_ref, east_ref = refs[-4:]
    here = place_ref[3]
    bit = 1
    while bit < len(pieces):
        turn = (here // bit) % 2 == 1
        pieces = [jnp.where(turn, pieces[i ^ bit], pieces[i]) for i in range(len(pieces))]
        bit *= 2
    share = pieces[0].shape[1]
    for i, piece in enumerate(pieces):
        v_ref[:, i * share : (i + 1) * share] = piece
    high, low = split(v_ref[:PAIRS])
    both = lax.dot_general(jnp.concatenate([high, low], axis=0), a_ref[...], NT, preferred_element_type=F32)
    xv = both[:PAIRS] + both[PAIRS:]
    xv_ref[...] = xv
    west_ref[...], east_ref[...] = edges([xv[:, r * LANES : (r + 1) * LANES] for r in range(rows)], reach)


def fields_kernel(step, rows, reach, total, chunk, *refs):
    m_ref, mh_ref, v_ref, u_ref, uh_ref, coast_ref, coasth_ref, xv_ref, xw_ref, xe_ref = refs[:10]
    refs = refs[10:]
    older = refs[: 2 * max(step - 1, 0)]
    refs = refs[len(older) :]
    if step:
        sum_ref, block_ref = refs[:2]
        w_ref, vn_ref, un_ref, vs, us = refs[2:]
    else:
        w_ref, vs, us = refs
    days = v_ref.shape[1]
    low = 2 * step
    own = rows * LANES
    vs[...] = v_ref[...]
    us[:, :own] = u_ref[...]
    us[:, own:] = uh_ref[...]
    for q in range(step - 1):
        vs[2 * q : 2 * q + 2] = older[2 * q][...]
        us[2 * q : 2 * q + 2] = older[2 * q + 1][...]
    if step:
        vn, un = new_pair(rows, reach, total, sum_ref, block_ref)
        vn_ref[...] = vn
        un_ref[...] = un
        vs[low - 2 : low] = vn
        us[low - 2 : low] = un
    modes = vs.shape[0]
    acc = acc_h = None
    for first in range(0, days, chunk):
        at = slice(first, first + chunk)
        v = vs[:, at]
        parts = []
        for j in (low, low + 1):
            parts.append(v * v[j : j + 1])
        high, lower = split(jnp.concatenate(parts, axis=0))
        left = jnp.concatenate([high, lower], axis=0)
        mid = lax.dot_general(left, m_ref[:, at], NT, preferred_element_type=F32)
        edge = lax.dot_general(left, mh_ref[:, at], NT, preferred_element_type=F32)
        acc = mid if acc is None else acc + mid
        acc_h = edge if acc_h is None else acc_h + edge
    masked = jnp.concatenate([acc[: 2 * modes] + acc[2 * modes :], acc_h[: 2 * modes] + acc_h[2 * modes :]], axis=1)
    lane = lane_ids((PAIRS, LANES))
    xh = jnp.where(lane < LANES // 2, xw_ref[...], xe_ref[...])
    xv = jnp.concatenate([xv_ref[...], xh], axis=1)
    u = us[...]
    proj = [
        xv[low + j : low + j + 1] - jnp.sum(u * masked[j * modes : (j + 1) * modes], axis=0, keepdims=True)
        for j in range(2)
    ]
    v0, v1 = (vs[low : low + 1], vs[low + 1 : low + 2])
    h00, h01, h11 = (total_of(v0 * v0), total_of(v0 * v1), total_of(v1 * v1))
    add0, add1 = solve_pair(h00, h01, h01, h11, proj[0], proj[1])
    coast = jnp.concatenate([coast_ref[...], coasth_ref[...]], axis=1)
    fresh = coast * jnp.concatenate([u[low : low + 1] + add0, u[low + 1 : low + 2] + add1], axis=0)
    count = 2 * rows
    w_ref[:count] = to_block(fresh, rows, reach)
    if step == 0:
        w_ref[count:] = to_block(jnp.concatenate([coast, coast], axis=0), rows, reach)


def new_pair(rows, reach, total, sum_ref, block_ref):
    days = sum_ref.shape[1] - LANES
    gram = sum_ref[:, days:]
    g00, g01, g11 = (gram[0:1, 0:1], gram[0:1, 1:2], gram[1:2, 1:2])
    n0, n1 = (jnp.sqrt(g00 / total + EPS), jnp.sqrt(g11 / total + EPS))
    first, second = solve_pair(
        g00 / (n0 * n0),
        g01 / (n0 * n1),
        g01 / (n0 * n1),
        g11 / (n1 * n1),
        sum_ref[0:1, :days] / n0,
        sum_ref[1:2, :days] / n1,
    )
    field = from_block(block_ref[...], rows, reach)
    unit = jnp.concatenate([field[0:1] / n0, field[1:2] / n1], axis=0)
    return jnp.concatenate([first, second], axis=0), unit


def sums_kernel(step, rows, chunk, *refs):
    m_ref, a_ref, v_ref, u_ref, place_ref, klon_ref, cosl_ref, w_ref, ga_ref, gb_ref = refs[:10]
    refs = refs[10:]
    if step:
        cw_ref, ca_ref, cb_ref = refs[:3]
        refs = refs[3:]
    older = refs[: 2 * step]
    sum_ref, block_ref, vs, us = refs[2 * step :]
    days = v_ref.shape[1]
    low = 2 * step
    own = rows * LANES
    vs[...] = v_ref[...]
    us[...] = u_ref[...]
    for q in range(step):
        vs[2 * q : 2 * q + 2] = older[2 * q][...]
        us[2 * q : 2 * q + 2] = older[2 * q + 1][:, :own]
    count = 2 * rows
    row0, nlat, odd = (place_ref[0], place_ref[1], place_ref[2])

    def assemble(mid, a, b):
        is_odd = odd == 1
        return jnp.concatenate([jnp.where(is_odd, a, b), mid, jnp.where(is_odd, b, a)], axis=0)

    w = assemble(w_ref[:count], ga_ref[:count], gb_ref[:count])
    if step:
        coast = assemble(cw_ref[count:], ca_ref[count:], cb_ref[count:])
    else:
        coast = assemble(w_ref[count:], ga_ref[count:], gb_ref[count:])
    tall = 3 * count
    row = row0 - rows + lax.broadcasted_iota(jnp.int32, (tall, 2 * LANES), 0) // 2
    coast = jnp.where((row >= 0) & (row < nlat), coast, 0.0)
    north = lambda z: pltpu.roll(z, 2, 0)
    south = lambda z: pltpu.roll(z, tall - 2, 0)
    west = lambda z: pltpu.roll(z, 1, 1)
    east = lambda z: pltpu.roll(z, 2 * LANES - 1, 1)
    cn, cs, cw, ce = (north(coast), south(coast), west(coast), east(coast))
    klon = klon_ref[...]
    for _ in range(SWEEPS):
        flux = KLAT * (cn * (north(w) - w) + cs * (south(w) - w)) + klon * (cw * (west(w) - w) + ce * (east(w) - w))
        w = w + coast * flux
    block = w[count : 2 * count]
    block_ref[...] = block
    cells = lambda z: jnp.concatenate([z[2 * r : 2 * r + 2, :LANES] for r in range(rows)], axis=1)
    fresh = cells(block)
    weighted = cells(block * cosl_ref[...])
    u = us[...]
    modes = u.shape[0]
    high, lower = split(jnp.concatenate([u * weighted[0:1], u * weighted[1:2]], axis=0))
    left = jnp.concatenate([high, lower], axis=0)
    high, lower = split(weighted)
    left_a = jnp.concatenate([high, lower], axis=0)
    lane = lane_ids((1, LANES))
    for j in range(2):
        gram = [total_of(weighted[j : j + 1] * fresh[i : i + 1]) for i in range(2)]
        sum_ref[j : j + 1, days:] = jnp.where(lane == 0, gram[0], jnp.where(lane == 1, gram[1], 0.0))
    old = [[total_of(weighted[j : j + 1] * u[low + i : low + i + 1]) for i in range(2)] for j in range(2)]
    for first in range(0, days, chunk):
        at = slice(first, first + chunk)
        masked = jnp.dot(left, m_ref[:, at], preferred_element_type=F32)
        given = jnp.dot(left_a, a_ref[:, at], preferred_element_type=F32)
        v = vs[:, at]
        for j in range(2):
            part = masked[j * modes : (j + 1) * modes] + masked[(2 + j) * modes : (3 + j) * modes]
            sum_ref[j : j + 1, at] = (
                given[j : j + 1]
                + given[2 + j : 3 + j]
                - jnp.sum(v * part, axis=0, keepdims=True)
                + old[j][0] * v[low : low + 1]
                + old[j][1] * v[low + 1 : low + 2]
            )


def last_kernel(rows, reach, total, sum_ref, block_ref, vn_ref, un_ref):
    vn, un = new_pair(rows, reach, total, sum_ref, block_ref)
    vn_ref[...] = vn
    un_ref[...] = un


def call(kernel, name, outs, scratch, args, smem=(), mib=24, flops=0, loads=0):
    moved = sum(z.size * z.dtype.itemsize for z in args)
    place = VMEM
    if loads:
        place = pl.BlockSpec(memory_space=pl.ANY)
        args = [pltpu.with_memory_space_constraint(z, pltpu.HBM) for z in args]
    return pl.pallas_call(
        kernel,
        out_shape=[jax.ShapeDtypeStruct(s, t) for s, t in outs],
        in_specs=[SMEM if i in smem else place for i in range(len(args))],
        out_specs=[VMEM for _ in outs],
        scratch_shapes=[pltpu.VMEM(s, t) for s, t in scratch] + ([pltpu.SemaphoreType.DMA((loads,))] if loads else []),
        compiler_params=pltpu.CompilerParams(vmem_limit_bytes=mib * 2**20),
        cost_estimate=pl.CostEstimate(flops=flops, bytes_accessed=moved, transcendentals=0),
        name=name,
    )(*args)


def latitude_cos(rows, nrows):
    degree = -60.0 + 120.0 * (rows.astype(F32) + 0.5) / nrows
    return jnp.cos(degree * (jnp.pi / 180.0))


def shards(sea_heat_deviations, missing_date_bitmask, ocean_binary_mask, mode_maps, mode_series):
    rows, columns, days = sea_heat_deviations.shape
    modes, words = (mode_maps.shape[0], missing_date_bitmask.shape[2])
    nlat = rows * lax.axis_size("lat")
    total = float(modes * nlat * columns * lax.axis_size("lon"))
    own, reach = (rows * columns, SWEEPS * STEPS)
    sides = 2 * rows * reach
    cells = own + sides
    assert columns == LANES and sides == LANES and rows == SWEEPS and days == BITS * words
    chunk = days // 5
    row0 = lax.axis_index("lat") * rows
    here = lax.axis_index("lon")
    place = jnp.stack([row0, jnp.int32(nlat), lax.axis_index("lat") % 2, here]).astype(jnp.int32)
    tall = row0 - rows + jnp.arange(6 * rows) // 2
    cos_tall = latitude_cos(tall, nlat)[:, None]
    klon = jnp.broadcast_to(KLON / (cos_tall * cos_tall), (6 * rows, 2 * LANES))
    cosl = jnp.broadcast_to(cos_tall[2 * rows : 4 * rows], (2 * rows, 2 * LANES))

    tall_edge = modes + 8 + rows * reach * (words // LANES)
    u, coast, to_west, to_east = call(
        functools.partial(prep_kernel, reach),
        "prep",
        [((modes, own), F32), ((1, own), F32), ((tall_edge, LANES), F32), ((tall_edge, LANES), F32)],
        [(mode_maps.shape, F32), ((rows, LANES), jnp.int32)] + [((rows, reach, words), jnp.int32)] * 2,
        [mode_maps, ocean_binary_mask, missing_date_bitmask],
        loads=4,
    )
    from_west, from_east = lon_ring(to_west, to_east)
    words_per = words // LANES
    flags_scratch = [((2 * LANES, days // words_per), BF16), ((1, days // words_per), jnp.int32)]
    m, a = call(
        own_flags_kernel,
        "own_flags",
        [((own, days), BF16)] * 2,
        [((own, words), jnp.int32), ((rows, LANES), jnp.int32), ((own, days), BF16), *flags_scratch],
        [missing_date_bitmask.reshape(own, words), ocean_binary_mask, sea_heat_deviations.reshape(own, days)],
        flops=4 * LANES * own * days,
        loads=2 + rows,
    )
    nlon = lax.axis_size("lon")
    if nlon == 8:
        pieces = [swap(mode_series, 0, b) for b in (2, 4, 6)]
        *pieces, m, a = lax.optimization_barrier((*pieces, m, a))
        pieces = [z for piece in [mode_series, *pieces] for z in (piece, swap(piece, 0, 1))]
    else:
        pieces = [lax.all_gather(mode_series, "lon", axis=1, tiled=True)]
    m_halo, u_halo, coast_halo = call(
        functools.partial(halo_flags_kernel, modes),
        "halo_flags",
        [((sides, days), BF16), ((modes, sides), F32), ((1, sides), F32)],
        flags_scratch,
        [from_west, from_east],
        flops=4 * LANES * sides * days,
    )
    v, xv, to_west, to_east = call(
        functools.partial(given_kernel, rows, reach),
        "given",
        [((modes, days), F32), ((PAIRS, own), F32), ((PAIRS, LANES), F32), ((PAIRS, LANES), F32)],
        [],
        [a, place, *pieces],
        smem=(1,),
        flops=4 * PAIRS * own * days,
    )
    xv_west, xv_east = lon_ring(to_west, to_east)

    count = 2 * rows
    news = []
    summed = block = None
    coasts = ()
    for step in range(STEPS):
        wide = 2 * count if step == 0 else count
        outs = [((wide, 2 * LANES), F32)]
        extra = []
        if step:
            outs += [((2, days), F32), ((2, cells), F32)]
            extra = [*news, summed, block]
        got = call(
            functools.partial(fields_kernel, step, rows, reach, total, chunk),
            f"fields_{step}",
            outs,
            [((modes, days), F32), ((modes, cells), F32)],
            [m, m_halo, v, u, u_halo, coast, coast_halo, xv, xv_west, xv_east, *extra],
            flops=8 * modes * cells * days,
        )
        fresh = got[0]
        news += got[1:]
        got_a, got_b = lat_partners(fresh)
        partial_sums, block = call(
            functools.partial(sums_kernel, step, rows, chunk),
            f"sums_{step}",
            [((2, days + LANES), F32), ((count, 2 * LANES), F32)],
            [((modes, days), F32), ((modes, own), F32)],
            [m, a, v, u, place, klon, cosl, fresh, got_a, got_b, *coasts, *news],
            smem=(4,),
            flops=8 * modes * own * days,
        )
        if step == 0:
            coasts = (fresh, got_a, got_b)
        summed = sum_all(partial_sums)
    news += call(
        functools.partial(last_kernel, rows, reach, total),
        "last",
        [((2, days), F32), ((2, cells), F32)],
        [],
        [summed, block],
    )
    share = mode_series.shape[1]
    new_v = jnp.concatenate(news[0::2], axis=0)
    new_u = jnp.concatenate([z[:, :own] for z in news[1::2]], axis=0).reshape(PAIRS, rows, columns)
    own_days = lax.dynamic_slice_in_dim(new_v, lax.axis_index("lon") * share, share, 1)
    return (
        jnp.concatenate([new_u, mode_maps[PAIRS:]], axis=0),
        jnp.concatenate([own_days, mode_series[PAIRS:]], axis=0),
    )


def solution(mesh):
    in_specs = (
        P("lat", "lon", None),
        P("lat", "lon", None),
        P("lat", "lon"),
        P(None, "lat", "lon"),
        P(None, "lon"),
    )
    out_specs = (P(None, "lat", "lon"), P(None, "lon"))
    return jax.shard_map(shards, mesh=mesh, in_specs=in_specs, out_specs=out_specs, check_vma=False)
```

```python
import functools

import jax
import jax.numpy as jnp
from jax import lax
from jax.experimental import pallas as pl
from jax.experimental.pallas import tpu as pltpu
from jax.sharding import PartitionSpec as P

STEPS = 4
SWEEPS = 4
PAIRS = 2 * STEPS
BITS = 15
LANES = 128

KLAT = 0.2
KLON = 0.05
EPS = 1e-06
F32 = jnp.float32
BF16 = jnp.bfloat16
VMEM = pl.BlockSpec(memory_space=pltpu.VMEM)
SMEM = pl.BlockSpec(memory_space=pltpu.SMEM)
NT = (((1,), (1,)), ((), ()))


def pairing(lat_map, lon_map):
    nlat, nlon = (lax.axis_size("lat"), lax.axis_size("lon"))
    return [(i * nlon + j, lat_map(i) * nlon + lon_map(j)) for i in range(nlat) for j in range(nlon)]


def swap(x, lat_bits, lon_bits):
    return lax.ppermute(x, ("lat", "lon"), pairing(lambda i: i ^ lat_bits, lambda j: j ^ lon_bits))


def sum_all(x):
    nlat, nlon = (lax.axis_size("lat"), lax.axis_size("lon"))
    if nlat & (nlat - 1) or nlon & (nlon - 1):
        return lax.psum(x, ("lat", "lon"))
    core = 1 if nlon > 1 else 0
    if core:
        x = x + swap(x, 0, core)
    for size, first, on_lat in ((nlat, 1, True), (nlon, 2, False)):
        bit = first
        while bit < size:
            bits = lambda b: (b, core) if on_lat else (0, b | core)
            if 2 * bit < size:
                near, far, both = (swap(x, *bits(b)) for b in (bit, 2 * bit, 3 * bit))
                x = (x + near) + (far + both)
                bit *= 4
            else:
                x = x + swap(x, *bits(bit))
                bit *= 2
    return x


def lat_partners(x):
    count = lax.axis_size("lat")
    same = lambda j: j
    got_a = lax.ppermute(x, ("lat", "lon"), pairing(lambda i: i ^ 1, same))
    got_b = lax.ppermute(x, ("lat", "lon"), pairing(lambda i: (i + 1 if i % 2 else i - 1) % count, same))
    return got_a, got_b


def lon_partners(near, far):
    count = lax.axis_size("lon")
    same = lambda i: i
    got_far = lax.ppermute(far, ("lat", "lon"), pairing(same, lambda j: (j + 1 if j % 2 else j - 1) % count))
    return swap(near, 0, 1), got_far


def split(x):
    high = x.astype(BF16)
    return high, (x - high.astype(F32)).astype(BF16)


def solve_pair(g00, g01, g10, g11, right0, right1):
    determ = g00 * g11 - g01 * g10
    return (g11 * right0 - g01 * right1) / determ, (g00 * right1 - g10 * right0) / determ


def total_of(x):
    return jnp.sum(x, axis=1, keepdims=True)


def lane_ids(shape):
    return lax.broadcasted_iota(jnp.int32, shape, 1)


def to_block(field, rows, reach):
    n, own = (field.shape[0], rows * LANES)
    halo = field[:, own:]
    lane = lane_ids((n, LANES))
    parts = []
    for r in range(rows):
        east = pltpu.roll(halo, (LANES - rows * reach - reach * r) % LANES, 1)
        west = pltpu.roll(halo, (LANES - reach - reach * r) % LANES, 1)
        edge = jnp.where(lane < LANES // 2, east, west)
        parts.append(jnp.concatenate([field[:, r * LANES : (r + 1) * LANES], edge], axis=1))
    return jnp.concatenate(parts, axis=0)


def from_block(block, rows, reach):
    n = block.shape[0] // rows
    lane = lane_ids((n, LANES))
    halo = jnp.zeros((n, LANES), F32)
    own = []
    for r in range(rows):
        part = block[r * n : (r + 1) * n]
        own.append(part[:, :LANES])
        edge = part[:, LANES:]
        east = pltpu.roll(edge, (rows * reach + reach * r) % LANES, 1)
        west = pltpu.roll(edge, (reach * r + reach) % LANES, 1)
        first = reach * r
        halo = jnp.where((lane >= first) & (lane < first + reach), west, halo)
        first = rows * reach + reach * r
        halo = jnp.where((lane >= first) & (lane < first + reach), east, halo)
    return jnp.concatenate(own + [halo], axis=1)


def unpack_words(words, spread_ref, bit_ref):
    top = ((words >> 8) << 8).astype(F32).astype(BF16)
    bottom = (words & 255).astype(F32).astype(BF16)
    spread = spread_ref[...]
    each = jnp.dot(jnp.concatenate([top, bottom], axis=1), spread, preferred_element_type=F32).astype(jnp.int32)
    return jnp.where((each & bit_ref[...]) == 0, 1.0, 0.0).astype(BF16)


def fill_spread(spread_ref, bit_ref):
    days = spread_ref.shape[1]
    word = lax.broadcasted_iota(jnp.int32, (LANES, days), 0)
    rest = lane_ids((LANES, days)) - BITS * word
    hit = jnp.where((rest >= 0) & (rest < BITS), 1.0, 0.0).astype(BF16)
    spread_ref[:LANES] = hit
    spread_ref[LANES:] = hit
    word = jnp.where((rest >= 0) & (rest < BITS), rest, 0)
    bit_ref[...] = jnp.left_shift(1, jnp.sum(word, axis=0, keepdims=True))


def as_column(row):
    return jnp.transpose(jnp.broadcast_to(row, (8, LANES)))[:, :1]


def own_flags_kernel(reach, *refs):
    words_hbm, coast_hbm, x_hbm, maps_hbm = refs[:4]
    m_ref, a_ref, u_ref, row_ref, west_ref, east_ref = refs[4:10]
    words_ref, coast_ref, x_ref, maps_ref, spread_ref, bit_ref, sems = refs[10:]
    rows = coast_ref.shape[0]
    loads = [
        pltpu.make_async_copy(words_hbm, words_ref, sems.at[0]),
        pltpu.make_async_copy(coast_hbm, coast_ref, sems.at[1]),
    ]
    for r in range(rows):
        at = pl.ds(r * LANES, LANES)
        loads.append(pltpu.make_async_copy(x_hbm.at[at], x_ref.at[at], sems.at[2 + r]))
    loads.append(pltpu.make_async_copy(maps_hbm, maps_ref, sems.at[2 + rows]))
    for load in loads:
        load.start()
    fill_spread(spread_ref, bit_ref)
    loads[0].wait()
    loads[1].wait()
    days = spread_ref.shape[1]
    coast_own = coast_ref[...].astype(F32)
    coasts = jnp.transpose(jnp.concatenate([coast_own] * (8 // rows), axis=0))
    for r in range(rows):
        coast = coasts[:, r : r + 1]
        ocean = coast.astype(BF16)
        coast = coast.astype(jnp.int32)
        loads[2 + r].wait()
        cell = slice(r * LANES, (r + 1) * LANES)
        for g in range(words_ref.shape[1] // LANES):
            words = words_ref[cell, g * LANES : (g + 1) * LANES] * coast
            given = unpack_words(words, spread_ref, bit_ref)
            at = slice(g * days, (g + 1) * days)
            m_ref[cell, at] = given
            a_ref[cell, at] = x_ref[cell, at] * given * ocean
    loads[2 + rows].wait()
    modes = maps_ref.shape[0]
    pieces = []
    for r in range(rows):
        at = slice(r * LANES, (r + 1) * LANES)
        u = maps_ref[:, r, :]
        u_ref[:, at] = u
        row_ref[:, at] = coast_own[r : r + 1]
        pieces.append(jnp.concatenate([u, jnp.broadcast_to(coast_own[r : r + 1], (8, LANES))], axis=0))
    base = modes + 8
    west_ref[:base], east_ref[:base] = edges(pieces, reach)
    for g in range(words_ref.shape[1] // LANES):
        for r in range(rows):
            at = slice(base + reach * (rows * g + r), base + reach * (rows * g + r + 1))
            group = slice(g * LANES, (g + 1) * LANES)
            west_ref[at] = words_ref[r * LANES : r * LANES + reach, group].astype(F32)
            east_ref[at] = words_ref[(r + 1) * LANES - reach : (r + 1) * LANES, group].astype(F32)


def edges(pieces, reach):
    rows = len(pieces)
    shape = pieces[0].shape
    lane = lane_ids(shape)
    west = jnp.zeros(shape, F32)
    east = west
    for r, part in enumerate(pieces):
        first = rows * reach + reach * r
        west = jnp.where((lane >= first) & (lane < first + reach), pltpu.roll(part, first % LANES, 1), west)
        first = reach * r
        east = jnp.where((lane >= first) & (lane < first + reach), pltpu.roll(part, (first + reach) % LANES, 1), east)
    return west, east


def given_kernel(rows, reach, *refs):
    a_ref, place_ref, ew_ref, ee_ref = refs[:4]
    pieces = [ref[...] for ref in refs[4:-4]]
    v_ref, xv_ref, near_ref, far_ref = refs[-4:]
    here = place_ref[3]
    bit = 1
    while bit < len(pieces):
        turn = (here // bit) % 2 == 1
        pieces = [jnp.where(turn, pieces[i ^ bit], pieces[i]) for i in range(len(pieces))]
        bit *= 2
    share = pieces[0].shape[1]
    for i, piece in enumerate(pieces):
        v_ref[:, i * share : (i + 1) * share] = piece
    high, low = split(v_ref[:PAIRS])
    both = lax.dot_general(jnp.concatenate([high, low], axis=0), a_ref[...], NT, preferred_element_type=F32)
    xv = both[:PAIRS] + both[PAIRS:]
    xv_ref[...] = xv
    west, east = edges([xv[:, r * LANES : (r + 1) * LANES] for r in range(rows)], reach)
    odd = here % 2 == 1
    tall = ew_ref.shape[0]
    near_ref[:tall] = jnp.where(odd, ew_ref[...], ee_ref[...])
    near_ref[tall:] = jnp.where(odd, west, east)
    far_ref[:tall] = jnp.where(odd, ee_ref[...], ew_ref[...])
    far_ref[tall:] = jnp.where(odd, east, west)


def masked_products(vs, u, low, chunk, m_ref):
    modes, days = vs.shape
    acc = None
    for first in range(0, days, chunk):
        at = slice(first, first + chunk)
        v = vs[:, at]
        high, lower = split(jnp.concatenate([v * v[j : j + 1] for j in (low, low + 1)], axis=0))
        left = jnp.concatenate([high, lower], axis=0)
        part = lax.dot_general(left, m_ref[:, at], NT, preferred_element_type=F32)
        acc = part if acc is None else acc + part
    acc = acc[: 2 * modes] + acc[2 * modes :]
    return jnp.concatenate(
        [jnp.sum(u * acc[j * modes : (j + 1) * modes], axis=0, keepdims=True) for j in range(2)], axis=0
    )


def own_products_kernel(chunk, m_ref, v_ref, u_ref, base_ref):
    base_ref[...] = masked_products(v_ref, u_ref[...], 0, chunk, m_ref)


def new_fields(pair, u_pair, coast, proj):
    v0, v1 = (pair[0:1], pair[1:2])
    h00, h01, h11 = (total_of(v0 * v0), total_of(v0 * v1), total_of(v1 * v1))
    add0, add1 = solve_pair(h00, h01, h01, h11, proj[0:1], proj[1:2])
    return coast * (u_pair + jnp.concatenate([add0, add1], axis=0))


def first_fields_kernel(rows, reach, chunk, *refs):
    near_ref, far_ref, place_ref, v_ref, u_ref, row_ref, xv_ref, base_ref = refs[:8]
    w_ref, m_ref, uh_ref, rowh_ref, xh_ref, spread_ref, bit_ref = refs[8:]
    fill_spread(spread_ref, bit_ref)
    odd = place_ref[3] % 2 == 1
    west = jnp.where(odd, near_ref[...], far_ref[...])
    east = jnp.where(odd, far_ref[...], near_ref[...])
    modes = v_ref.shape[0]
    base = modes + 8
    lane = lane_ids((base, LANES))
    fields = jnp.where(lane < LANES // 2, west[:base], east[:base])
    u_halo = fields[:modes]
    uh_ref[...] = u_halo
    rowh_ref[...] = fields[modes : modes + 1]
    xh = jnp.where(lane[:PAIRS] < LANES // 2, west[-PAIRS:], east[-PAIRS:])
    xh_ref[...] = xh
    coast = as_column(fields[modes : modes + 1]).astype(jnp.int32)
    days = spread_ref.shape[1]
    half = LANES // 2
    for g in range(m_ref.shape[1] // days):
        at = slice(base + half * g, base + half * (g + 1))
        words = jnp.concatenate([west[at], east[at]], axis=0).astype(jnp.int32) * coast
        m_ref[:, g * days : (g + 1) * days] = unpack_words(words, spread_ref, bit_ref)
    halo = xh[:2] - masked_products(v_ref, u_halo, 0, chunk, m_ref)
    proj = jnp.concatenate([xv_ref[:2] - base_ref[...], halo], axis=1)
    u_pair = jnp.concatenate([u_ref[:2], u_halo[:2]], axis=1)
    coast = jnp.concatenate([row_ref[...], fields[modes : modes + 1]], axis=1)
    count = 2 * rows
    w_ref[:count] = to_block(new_fields(v_ref[:2], u_pair, coast, proj), rows, reach)
    w_ref[count:] = to_block(jnp.concatenate([coast, coast], axis=0), rows, reach)


def fields_kernel(step, rows, reach, total, chunk, *refs):
    m_ref, mh_ref, v_ref, u_ref, uh_ref, row_ref, rowh_ref, xv_ref, xh_ref = refs[:9]
    older = refs[9 : 9 + 2 * (step - 1)]
    sum_ref, block_ref, w_ref, vn_ref, un_ref, vs, us = refs[9 + len(older) :]
    low = 2 * step
    own = rows * LANES
    vs[...] = v_ref[...]
    us[:, :own] = u_ref[...]
    us[:, own:] = uh_ref[...]
    for q in range(step - 1):
        vs[2 * q : 2 * q + 2] = older[2 * q][...]
        us[2 * q : 2 * q + 2] = older[2 * q + 1][...]
    vn, un = new_pair(rows, reach, total, sum_ref, block_ref)
    vn_ref[...] = vn
    un_ref[...] = un
    vs[low - 2 : low] = vn
    us[low - 2 : low] = un
    mid = xv_ref[low : low + 2] - masked_products(vs, us[:, :own], low, chunk, m_ref)
    edge = xh_ref[low : low + 2] - masked_products(vs, us[:, own:], low, chunk, mh_ref)
    proj = jnp.concatenate([mid, edge], axis=1)
    coast = jnp.concatenate([row_ref[...], rowh_ref[...]], axis=1)
    w_ref[...] = to_block(new_fields(vs[low : low + 2], us[low : low + 2], coast, proj), rows, reach)


def new_pair(rows, reach, total, sum_ref, block_ref):
    days = sum_ref.shape[1] - LANES
    gram = sum_ref[:, days:]
    g00, g01, g11 = (gram[0:1, 0:1], gram[0:1, 1:2], gram[1:2, 1:2])
    n0, n1 = (jnp.sqrt(g00 / total + EPS), jnp.sqrt(g11 / total + EPS))
    g00, g01, g11 = (g00 / (n0 * n0), g01 / (n0 * n1), g11 / (n1 * n1))
    determ = g00 * g11 - g01 * g01
    p0, p1 = (sum_ref[0:1, :days], sum_ref[1:2, :days])
    cross = g01 / determ
    first = (g11 / determ / n0) * p0 - (cross / n1) * p1
    second = (g00 / determ / n1) * p1 - (cross / n0) * p0
    field = from_block(block_ref[...], rows, reach)
    unit = jnp.concatenate([field[0:1] / n0, field[1:2] / n1], axis=0)
    return jnp.concatenate([first, second], axis=0), unit


def sums_kernel(step, rows, chunk, *refs):
    m_ref, a_ref, v_ref, u_ref, place_ref, klon_ref, cosl_ref, w_ref, ga_ref, gb_ref = refs[:10]
    refs = refs[10:]
    if step:
        cw_ref, ca_ref, cb_ref = refs[:3]
        refs = refs[3:]
    older = refs[: 2 * step]
    sum_ref, block_ref, vs, us = refs[2 * step :]
    days = v_ref.shape[1]
    low = 2 * step
    own = rows * LANES
    vs[...] = v_ref[...]
    us[...] = u_ref[...]
    for q in range(step):
        vs[2 * q : 2 * q + 2] = older[2 * q][...]
        us[2 * q : 2 * q + 2] = older[2 * q + 1][:, :own]
    count = 2 * rows
    row0, nlat, odd = (place_ref[0], place_ref[1], place_ref[2])

    def assemble(mid, a, b):
        is_odd = odd == 1
        return jnp.concatenate([jnp.where(is_odd, a, b), mid, jnp.where(is_odd, b, a)], axis=0)

    w = assemble(w_ref[:count], ga_ref[:count], gb_ref[:count])
    if step:
        coast = assemble(cw_ref[count:], ca_ref[count:], cb_ref[count:])
    else:
        coast = assemble(w_ref[count:], ga_ref[count:], gb_ref[count:])
    tall = 3 * count
    row = row0 - rows + lax.broadcasted_iota(jnp.int32, (tall, 2 * LANES), 0) // 2
    coast = jnp.where((row >= 0) & (row < nlat), coast, 0.0)
    north = lambda z: pltpu.roll(z, 2, 0)
    south = lambda z: pltpu.roll(z, tall - 2, 0)
    west = lambda z: pltpu.roll(z, 1, 1)
    east = lambda z: pltpu.roll(z, 2 * LANES - 1, 1)
    klon = klon_ref[...] * coast
    klat = KLAT * coast
    an, as_, aw, ae = (klat * north(coast), klat * south(coast), klon * west(coast), klon * east(coast))
    stay = 1.0 - (an + as_ + aw + ae)
    for _ in range(SWEEPS):
        w = stay * w + (an * north(w) + as_ * south(w)) + (aw * west(w) + ae * east(w))
    block = w[count : 2 * count]
    block_ref[...] = block
    cells = lambda z: jnp.concatenate([z[2 * r : 2 * r + 2, :LANES] for r in range(rows)], axis=1)
    fresh = cells(block)
    weighted = cells(block * cosl_ref[...])
    u = us[...]
    modes = u.shape[0]
    high, lower = split(jnp.concatenate([u * weighted[0:1], u * weighted[1:2]], axis=0))
    left = jnp.concatenate([high, lower], axis=0)
    high, lower = split(weighted)
    left_a = jnp.concatenate([high, lower], axis=0)
    lane = lane_ids((1, LANES))
    for j in range(2):
        gram = [total_of(weighted[j : j + 1] * fresh[i : i + 1]) for i in range(2)]
        sum_ref[j : j + 1, days:] = jnp.where(lane == 0, gram[0], jnp.where(lane == 1, gram[1], 0.0))
    old = [[total_of(weighted[j : j + 1] * u[low + i : low + i + 1]) for i in range(2)] for j in range(2)]
    for first in range(0, days, chunk):
        at = slice(first, first + chunk)
        masked = jnp.dot(left, m_ref[:, at], preferred_element_type=F32)
        given = jnp.dot(left_a, a_ref[:, at], preferred_element_type=F32)
        v = vs[:, at]
        for j in range(2):
            part = masked[j * modes : (j + 1) * modes] + masked[(2 + j) * modes : (3 + j) * modes]
            sum_ref[j : j + 1, at] = (
                given[j : j + 1]
                + given[2 + j : 3 + j]
                - jnp.sum(v * part, axis=0, keepdims=True)
                + old[j][0] * v[low : low + 1]
                + old[j][1] * v[low + 1 : low + 2]
            )


def last_kernel(rows, reach, total, sum_ref, block_ref, vn_ref, un_ref):
    vn, un = new_pair(rows, reach, total, sum_ref, block_ref)
    vn_ref[...] = vn
    un_ref[...] = un


def call(kernel, name, outs, scratch, args, smem=(), mib=24, flops=0, loads=0):
    moved = sum(z.size * z.dtype.itemsize for z in args)
    place = VMEM
    if loads:
        place = pl.BlockSpec(memory_space=pl.ANY)
        args = [pltpu.with_memory_space_constraint(z, pltpu.HBM) for z in args]
    return pl.pallas_call(
        kernel,
        out_shape=[jax.ShapeDtypeStruct(s, t) for s, t in outs],
        in_specs=[SMEM if i in smem else place for i in range(len(args))],
        out_specs=[VMEM for _ in outs],
        scratch_shapes=[pltpu.VMEM(s, t) for s, t in scratch] + ([pltpu.SemaphoreType.DMA((loads,))] if loads else []),
        compiler_params=pltpu.CompilerParams(vmem_limit_bytes=mib * 2**20),
        cost_estimate=pl.CostEstimate(flops=flops, bytes_accessed=moved, transcendentals=0),
        name=name,
    )(*args)


def latitude_cos(rows, nrows):
    degree = -60.0 + 120.0 * (rows.astype(F32) + 0.5) / nrows
    return jnp.cos(degree * (jnp.pi / 180.0))


def shards(sea_heat_deviations, missing_date_bitmask, ocean_binary_mask, mode_maps, mode_series):
    rows, columns, days = sea_heat_deviations.shape
    modes, words = (mode_maps.shape[0], missing_date_bitmask.shape[2])
    nlat = rows * lax.axis_size("lat")
    total = float(modes * nlat * columns * lax.axis_size("lon"))
    own, reach = (rows * columns, SWEEPS * STEPS)
    sides = 2 * rows * reach
    cells = own + sides
    assert columns == LANES and sides == LANES and rows == SWEEPS and days == BITS * words
    chunk = days // 5
    row0 = lax.axis_index("lat") * rows
    here = lax.axis_index("lon")
    place = jnp.stack([row0, jnp.int32(nlat), lax.axis_index("lat") % 2, here]).astype(jnp.int32)
    tall = row0 - rows + jnp.arange(6 * rows) // 2
    cos_tall = latitude_cos(tall, nlat)[:, None]
    klon = jnp.broadcast_to(KLON / (cos_tall * cos_tall), (6 * rows, 2 * LANES))
    cosl = jnp.broadcast_to(cos_tall[2 * rows : 4 * rows], (2 * rows, 2 * LANES))

    words_per = words // LANES
    flags_scratch = [((2 * LANES, days // words_per), BF16), ((1, days // words_per), jnp.int32)]
    edge = ((modes + 8 + rows * reach * words_per, LANES), F32)
    m, a, u, row, edge_west, edge_east = call(
        functools.partial(own_flags_kernel, reach),
        "own_flags",
        [((own, days), BF16), ((own, days), BF16), ((modes, own), F32), ((1, own), F32), edge, edge],
        [((own, words), jnp.int32), ((rows, LANES), jnp.int32), ((own, days), BF16), (mode_maps.shape, F32), *flags_scratch],
        [missing_date_bitmask.reshape(own, words), ocean_binary_mask, sea_heat_deviations.reshape(own, days), mode_maps],
        flops=4 * LANES * own * days,
        loads=3 + rows,
    )
    if lax.axis_size("lon") == 8:
        pieces = [swap(mode_series, 0, b | 1) for b in (2, 4, 6)]
        *pieces, m, a = lax.optimization_barrier((*pieces, m, a))
        pieces = [z for piece in pieces for z in (swap(piece, 0, 1), piece)]
        pieces = [mode_series, swap(mode_series, 0, 1), *pieces]
    else:
        pieces = [lax.all_gather(mode_series, "lon", axis=1, tiled=True)]
    edge = ((edge[0][0] + PAIRS, LANES), F32)
    v, xv, near, far = call(
        functools.partial(given_kernel, rows, reach),
        "given",
        [((modes, days), F32), ((PAIRS, own), F32), edge, edge],
        [],
        [a, place, edge_west, edge_east, *pieces],
        smem=(1,),
        flops=4 * PAIRS * own * days,
    )
    near, far = lon_partners(near, far)
    (base,) = call(
        functools.partial(own_products_kernel, chunk),
        "own_products",
        [((2, own), F32)],
        [],
        [m, v, u],
        flops=8 * modes * own * days,
    )

    count = 2 * rows
    news = []
    summed = block = None
    coasts = ()
    for step in range(STEPS):
        if step == 0:
            fresh, m_halo, u_halo, row_halo, xv_halo = call(
                functools.partial(first_fields_kernel, rows, reach, chunk),
                "fields_0",
                [
                    ((2 * count, 2 * LANES), F32),
                    ((sides, days), BF16),
                    ((modes, sides), F32),
                    ((1, sides), F32),
                    ((PAIRS, sides), F32),
                ],
                flags_scratch,
                [near, far, place, v, u, row, xv, base],
                smem=(2,),
                flops=8 * modes * sides * days,
            )
        else:
            fresh, *new = call(
                functools.partial(fields_kernel, step, rows, reach, total, chunk),
                f"fields_{step}",
                [((count, 2 * LANES), F32), ((2, days), F32), ((2, cells), F32)],
                [((modes, days), F32), ((modes, cells), F32)],
                [m, m_halo, v, u, u_halo, row, row_halo, xv, xv_halo, *news, summed, block],
                flops=8 * modes * cells * days,
            )
            news += new
        got_a, got_b = lat_partners(fresh)
        partial_sums, block = call(
            functools.partial(sums_kernel, step, rows, chunk),
            f"sums_{step}",
            [((2, days + LANES), F32), ((count, 2 * LANES), F32)],
            [((modes, days), F32), ((modes, own), F32)],
            [m, a, v, u, place, klon, cosl, fresh, got_a, got_b, *coasts, *news],
            smem=(4,),
            flops=8 * modes * own * days,
        )
        if step == 0:
            coasts = (fresh, got_a, got_b)
        summed = sum_all(partial_sums)
    news += call(
        functools.partial(last_kernel, rows, reach, total),
        "last",
        [((2, days), F32), ((2, cells), F32)],
        [],
        [summed, block],
    )
    share = mode_series.shape[1]
    new_v = jnp.concatenate(news[0::2], axis=0)
    new_u = jnp.concatenate([z[:, :own] for z in news[1::2]], axis=0).reshape(PAIRS, rows, columns)
    own_days = lax.dynamic_slice_in_dim(new_v, lax.axis_index("lon") * share, share, 1)
    return (
        jnp.concatenate([new_u, mode_maps[PAIRS:]], axis=0),
        jnp.concatenate([own_days, mode_series[PAIRS:]], axis=0),
    )


def solution(mesh):
    in_specs = (
        P("lat", "lon", None),
        P("lat", "lon", None),
        P("lat", "lon"),
        P(None, "lat", "lon"),
        P(None, "lon"),
    )
    out_specs = (P(None, "lat", "lon"), P(None, "lon"))
    return jax.shard_map(shards, mesh=mesh, in_specs=in_specs, out_specs=out_specs, check_vma=False)
```

```python
import functools

import jax
import jax.numpy as jnp
from jax import lax
from jax.experimental import pallas as pl
from jax.experimental.pallas import tpu as pltpu
from jax.sharding import PartitionSpec as P

STEPS = 4
SWEEPS = 4
PAIRS = 2 * STEPS
BITS = 15
LANES = 128

KLAT = 0.2
KLON = 0.05
EPS = 1e-06
F32 = jnp.float32
BF16 = jnp.bfloat16
VMEM = pl.BlockSpec(memory_space=pltpu.VMEM)
SMEM = pl.BlockSpec(memory_space=pltpu.SMEM)
NT = (((1,), (1,)), ((), ()))


def pairing(lat_map, lon_map):
    nlat, nlon = (lax.axis_size("lat"), lax.axis_size("lon"))
    return [(i * nlon + j, lat_map(i) * nlon + lon_map(j)) for i in range(nlat) for j in range(nlon)]


def swap(x, lat_bits, lon_bits):
    return lax.ppermute(x, ("lat", "lon"), pairing(lambda i: i ^ lat_bits, lambda j: j ^ lon_bits))


def sum_all(x):
    nlat, nlon = (lax.axis_size("lat"), lax.axis_size("lon"))
    if nlat & (nlat - 1) or nlon & (nlon - 1):
        return lax.psum(x, ("lat", "lon"))
    core = 1 if nlon > 1 else 0
    if core:
        x = x + swap(x, 0, core)
    for size, first, on_lat in ((nlat, 1, True), (nlon, 2, False)):
        bit = first
        while bit < size:
            bits = lambda b: (b, core) if on_lat else (0, b | core)
            if 2 * bit < size:
                near, far, both = (swap(x, *bits(b)) for b in (bit, 2 * bit, 3 * bit))
                x = (x + near) + (far + both)
                bit *= 4
            else:
                x = x + swap(x, *bits(bit))
                bit *= 2
    return x


def lat_partners(x):
    count = lax.axis_size("lat")
    same = lambda j: j
    got_a = lax.ppermute(x, ("lat", "lon"), pairing(lambda i: i ^ 1, same))
    got_b = lax.ppermute(x, ("lat", "lon"), pairing(lambda i: (i + 1 if i % 2 else i - 1) % count, same))
    return got_a, got_b


def lon_partners(near, far):
    count = lax.axis_size("lon")
    same = lambda i: i
    got_far = lax.ppermute(far, ("lat", "lon"), pairing(same, lambda j: (j + 1 if j % 2 else j - 1) % count))
    return swap(near, 0, 1), got_far


def split(x):
    high = x.astype(BF16)
    return high, (x - high.astype(F32)).astype(BF16)


def solve_pair(g00, g01, g10, g11, right0, right1):
    determ = g00 * g11 - g01 * g10
    return (g11 * right0 - g01 * right1) / determ, (g00 * right1 - g10 * right0) / determ


def total_of(x):
    return jnp.sum(x, axis=1, keepdims=True)


def lane_ids(shape):
    return lax.broadcasted_iota(jnp.int32, shape, 1)


def to_block(field, rows, reach):
    n, own = (field.shape[0], rows * LANES)
    halo = field[:, own:]
    lane = lane_ids((n, LANES))
    parts = []
    for r in range(rows):
        east = pltpu.roll(halo, (LANES - rows * reach - reach * r) % LANES, 1)
        west = pltpu.roll(halo, (LANES - reach - reach * r) % LANES, 1)
        edge = jnp.where(lane < LANES // 2, east, west)
        parts.append(jnp.concatenate([field[:, r * LANES : (r + 1) * LANES], edge], axis=1))
    return jnp.concatenate(parts, axis=0)


def from_block(block, rows, reach):
    n = block.shape[0] // rows
    lane = lane_ids((n, LANES))
    halo = jnp.zeros((n, LANES), F32)
    own = []
    for r in range(rows):
        part = block[r * n : (r + 1) * n]
        own.append(part[:, :LANES])
        edge = part[:, LANES:]
        east = pltpu.roll(edge, (rows * reach + reach * r) % LANES, 1)
        west = pltpu.roll(edge, (reach * r + reach) % LANES, 1)
        first = reach * r
        halo = jnp.where((lane >= first) & (lane < first + reach), west, halo)
        first = rows * reach + reach * r
        halo = jnp.where((lane >= first) & (lane < first + reach), east, halo)
    return jnp.concatenate(own + [halo], axis=1)


def unpack_words(words, spread_ref, bit_ref):
    top = ((words >> 8) << 8).astype(F32).astype(BF16)
    bottom = (words & 255).astype(F32).astype(BF16)
    spread = spread_ref[...]
    each = jnp.dot(jnp.concatenate([top, bottom], axis=1), spread, preferred_element_type=F32).astype(jnp.int32)
    return jnp.where((each & bit_ref[...]) == 0, 1.0, 0.0).astype(BF16)


def fill_spread(spread_ref, bit_ref):
    days = spread_ref.shape[1]
    word = lax.broadcasted_iota(jnp.int32, (LANES, days), 0)
    rest = lane_ids((LANES, days)) - BITS * word
    hit = jnp.where((rest >= 0) & (rest < BITS), 1.0, 0.0).astype(BF16)
    spread_ref[:LANES] = hit
    spread_ref[LANES:] = hit
    word = jnp.where((rest >= 0) & (rest < BITS), rest, 0)
    bit_ref[...] = jnp.left_shift(1, jnp.sum(word, axis=0, keepdims=True))


def as_column(row):
    return jnp.transpose(jnp.broadcast_to(row, (8, LANES)))[:, :1]


def own_flags_kernel(reach, *refs):
    words_hbm, coast_hbm, x_hbm, maps_hbm, series_hbm, place_ref = refs[:6]
    m_ref, a_ref, u_ref, row_ref, near_ref, far_ref, maps_out, series_out = refs[6:14]
    words_ref, coast_ref, x_ref, maps_ref, series_ref, spread_ref, bit_ref, sems = refs[14:]
    rows = coast_ref.shape[0]
    loads = [
        pltpu.make_async_copy(words_hbm, words_ref, sems.at[0]),
        pltpu.make_async_copy(coast_hbm, coast_ref, sems.at[1]),
    ]
    for r in range(rows):
        at = pl.ds(r * LANES, LANES)
        loads.append(pltpu.make_async_copy(x_hbm.at[at], x_ref.at[at], sems.at[2 + r]))
    loads.append(pltpu.make_async_copy(maps_hbm, maps_ref, sems.at[2 + rows]))
    loads.append(pltpu.make_async_copy(series_hbm, series_ref, sems.at[3 + rows]))
    stores = [
        pltpu.make_async_copy(maps_ref, maps_out, sems.at[4 + rows]),
        pltpu.make_async_copy(series_ref, series_out, sems.at[5 + rows]),
    ]
    for load in loads:
        load.start()
    fill_spread(spread_ref, bit_ref)
    loads[0].wait()
    loads[1].wait()
    days = spread_ref.shape[1]
    coast_own = coast_ref[...].astype(F32)
    coasts = jnp.transpose(jnp.concatenate([coast_own] * (8 // rows), axis=0))
    for r in range(rows):
        coast = coasts[:, r : r + 1]
        ocean = coast.astype(BF16)
        coast = coast.astype(jnp.int32)
        loads[2 + r].wait()
        cell = slice(r * LANES, (r + 1) * LANES)
        for g in range(words_ref.shape[1] // LANES):
            words = words_ref[cell, g * LANES : (g + 1) * LANES] * coast
            given = unpack_words(words, spread_ref, bit_ref)
            at = slice(g * days, (g + 1) * days)
            m_ref[cell, at] = given
            a_ref[cell, at] = x_ref[cell, at] * given * ocean
    for load, store in zip(loads[-2:], stores, strict=True):
        load.wait()
        store.start()
    modes = maps_ref.shape[0]
    pieces = []
    for r in range(rows):
        at = slice(r * LANES, (r + 1) * LANES)
        u = maps_ref[:, r, :]
        u_ref[:, at] = u
        row_ref[:, at] = coast_own[r : r + 1]
        pieces.append(jnp.concatenate([u, jnp.broadcast_to(coast_own[r : r + 1], (8, LANES))], axis=0))
    base = modes + 8
    odd = place_ref[3] % 2 == 1
    west, east = edges(pieces, reach)
    near_ref[:base] = jnp.where(odd, west, east)
    far_ref[:base] = jnp.where(odd, east, west)
    for g in range(words_ref.shape[1] // LANES):
        for r in range(rows):
            at = slice(base + reach * (rows * g + r), base + reach * (rows * g + r + 1))
            group = slice(g * LANES, (g + 1) * LANES)
            west = words_ref[r * LANES : r * LANES + reach, group].astype(F32)
            east = words_ref[(r + 1) * LANES - reach : (r + 1) * LANES, group].astype(F32)
            near_ref[at] = jnp.where(odd, west, east)
            far_ref[at] = jnp.where(odd, east, west)
    for store in stores:
        store.wait()


def edges(pieces, reach):
    rows = len(pieces)
    shape = pieces[0].shape
    lane = lane_ids(shape)
    west = jnp.zeros(shape, F32)
    east = west
    for r, part in enumerate(pieces):
        first = rows * reach + reach * r
        west = jnp.where((lane >= first) & (lane < first + reach), pltpu.roll(part, first % LANES, 1), west)
        first = reach * r
        east = jnp.where((lane >= first) & (lane < first + reach), pltpu.roll(part, (first + reach) % LANES, 1), east)
    return west, east


def given_kernel(rows, reach, *refs):
    a_ref, place_ref = refs[:2]
    pieces = [ref[...] for ref in refs[2:-4]]
    v_ref, xv_ref, near_ref, far_ref = refs[-4:]
    here = place_ref[3]
    bit = 1
    while bit < len(pieces):
        turn = (here // bit) % 2 == 1
        pieces = [jnp.where(turn, pieces[i ^ bit], pieces[i]) for i in range(len(pieces))]
        bit *= 2
    share = pieces[0].shape[1]
    for i, piece in enumerate(pieces):
        v_ref[:, i * share : (i + 1) * share] = piece
    high, low = split(v_ref[:PAIRS])
    both = lax.dot_general(jnp.concatenate([high, low], axis=0), a_ref[...], NT, preferred_element_type=F32)
    xv = both[:PAIRS] + both[PAIRS:]
    xv_ref[...] = xv
    west, east = edges([xv[:, r * LANES : (r + 1) * LANES] for r in range(rows)], reach)
    odd = here % 2 == 1
    near_ref[...] = jnp.where(odd, west, east)
    far_ref[...] = jnp.where(odd, east, west)


def masked_products(vs, u, low, chunk, m_ref):
    modes, days = vs.shape
    acc = None
    for first in range(0, days, chunk):
        at = slice(first, first + chunk)
        v = vs[:, at]
        high, lower = split(jnp.concatenate([v * v[j : j + 1] for j in (low, low + 1)], axis=0))
        left = jnp.concatenate([high, lower], axis=0)
        part = lax.dot_general(left, m_ref[:, at], NT, preferred_element_type=F32)
        acc = part if acc is None else acc + part
    acc = acc[: 2 * modes] + acc[2 * modes :]
    return jnp.concatenate(
        [jnp.sum(u * acc[j * modes : (j + 1) * modes], axis=0, keepdims=True) for j in range(2)], axis=0
    )


def first_products_kernel(chunk, *refs):
    near_ref, far_ref, place_ref, m_ref, v_ref, u_own_ref, row_own_ref = refs[:7]
    base_ref, mh_ref, u_ref, row_ref, spread_ref, bit_ref = refs[7:]
    fill_spread(spread_ref, bit_ref)
    odd = place_ref[3] % 2 == 1
    west = jnp.where(odd, near_ref[...], far_ref[...])
    east = jnp.where(odd, far_ref[...], near_ref[...])
    modes, own = u_own_ref.shape
    base = modes + 8
    lane = lane_ids((base, LANES))
    fields = jnp.where(lane < LANES // 2, west[:base], east[:base])
    u_own, u_halo, row_halo = (u_own_ref[...], fields[:modes], fields[modes : modes + 1])
    u_ref[:, :own] = u_own
    u_ref[:, own:] = u_halo
    row_ref[:, :own] = row_own_ref[...]
    row_ref[:, own:] = row_halo
    coast = as_column(row_halo).astype(jnp.int32)
    days = spread_ref.shape[1]
    half = LANES // 2
    for g in range(mh_ref.shape[1] // days):
        at = slice(base + half * g, base + half * (g + 1))
        words = jnp.concatenate([west[at], east[at]], axis=0).astype(jnp.int32) * coast
        mh_ref[:, g * days : (g + 1) * days] = unpack_words(words, spread_ref, bit_ref)
    base_ref[:, :own] = masked_products(v_ref, u_own, 0, chunk, m_ref)
    base_ref[:, own:] = masked_products(v_ref, u_halo, 0, chunk, mh_ref)


def new_fields(pair, u_pair, coast, proj):
    v0, v1 = (pair[0:1], pair[1:2])
    h00, h01, h11 = (total_of(v0 * v0), total_of(v0 * v1), total_of(v1 * v1))
    add0, add1 = solve_pair(h00, h01, h01, h11, proj[0:1], proj[1:2])
    return coast * (u_pair + jnp.concatenate([add0, add1], axis=0))


def first_fields_kernel(rows, reach, near_ref, far_ref, place_ref, v_ref, u_ref, row_ref, xv_ref, base_ref, w_ref, xh_ref):
    odd = place_ref[3] % 2 == 1
    west = jnp.where(odd, near_ref[...], far_ref[...])
    east = jnp.where(odd, far_ref[...], near_ref[...])
    xh = jnp.where(lane_ids((PAIRS, LANES)) < LANES // 2, west, east)
    xh_ref[...] = xh
    proj = jnp.concatenate([xv_ref[:2], xh[:2]], axis=1) - base_ref[...]
    coast = row_ref[...]
    count = 2 * rows
    w_ref[:count] = to_block(new_fields(v_ref[:2], u_ref[:2], coast, proj), rows, reach)
    w_ref[count:] = to_block(jnp.concatenate([coast, coast], axis=0), rows, reach)


def fields_kernel(step, rows, reach, total, chunk, *refs):
    m_ref, mh_ref, v_ref, u_ref, row_ref, xv_ref, xh_ref, sum_ref, block_ref, w_ref, vs, us = refs
    low = 2 * step
    own = rows * LANES
    vs[...] = v_ref[...]
    us[...] = u_ref[...]
    vs[low - 2 : low], us[low - 2 : low] = new_pair(rows, reach, total, sum_ref, block_ref)
    mid = xv_ref[low : low + 2] - masked_products(vs, us[:, :own], low, chunk, m_ref)
    edge = xh_ref[low : low + 2] - masked_products(vs, us[:, own:], low, chunk, mh_ref)
    proj = jnp.concatenate([mid, edge], axis=1)
    w_ref[...] = to_block(new_fields(vs[low : low + 2], us[low : low + 2], row_ref[...], proj), rows, reach)


def new_pair(rows, reach, total, sum_ref, block_ref):
    days = sum_ref.shape[1] - LANES
    gram = sum_ref[:, days:]
    g00, g01, g11 = (gram[0:1, 0:1], gram[0:1, 1:2], gram[1:2, 1:2])
    n0, n1 = (jnp.sqrt(g00 / total + EPS), jnp.sqrt(g11 / total + EPS))
    g00, g01, g11 = (g00 / (n0 * n0), g01 / (n0 * n1), g11 / (n1 * n1))
    determ = g00 * g11 - g01 * g01
    p0, p1 = (sum_ref[0:1, :days], sum_ref[1:2, :days])
    cross = g01 / determ
    first = (g11 / determ / n0) * p0 - (cross / n1) * p1
    second = (g00 / determ / n1) * p1 - (cross / n0) * p0
    field = from_block(block_ref[...], rows, reach)
    unit = jnp.concatenate([field[0:1] / n0, field[1:2] / n1], axis=0)
    return jnp.concatenate([first, second], axis=0), unit


def sums_kernel(step, rows, chunk, *refs):
    m_ref, a_ref, v_ref, u_ref, place_ref, klon_ref, cosl_ref, w_ref, ga_ref, gb_ref = refs[:10]
    refs = refs[10:]
    if step:
        cw_ref, ca_ref, cb_ref = refs[:3]
        refs = refs[3:]
    sum_ref, block_ref = refs
    days = v_ref.shape[1]
    low = 2 * step
    own = rows * LANES
    count = 2 * rows
    row0, nlat, odd = (place_ref[0], place_ref[1], place_ref[2])

    def assemble(mid, a, b):
        is_odd = odd == 1
        return jnp.concatenate([jnp.where(is_odd, a, b), mid, jnp.where(is_odd, b, a)], axis=0)

    w = assemble(w_ref[:count], ga_ref[:count], gb_ref[:count])
    if step:
        coast = assemble(cw_ref[count:], ca_ref[count:], cb_ref[count:])
    else:
        coast = assemble(w_ref[count:], ga_ref[count:], gb_ref[count:])
    tall = 3 * count
    row = row0 - rows + lax.broadcasted_iota(jnp.int32, (tall, 2 * LANES), 0) // 2
    coast = jnp.where((row >= 0) & (row < nlat), coast, 0.0)
    north = lambda z: pltpu.roll(z, 2, 0)
    south = lambda z: pltpu.roll(z, tall - 2, 0)
    west = lambda z: pltpu.roll(z, 1, 1)
    east = lambda z: pltpu.roll(z, 2 * LANES - 1, 1)
    klon = klon_ref[...] * coast
    klat = KLAT * coast
    an, as_, aw, ae = (klat * north(coast), klat * south(coast), klon * west(coast), klon * east(coast))
    stay = 1.0 - (an + as_ + aw + ae)
    for _ in range(SWEEPS):
        w = stay * w + (an * north(w) + as_ * south(w)) + (aw * west(w) + ae * east(w))
    block = w[count : 2 * count]
    block_ref[...] = block
    cells = lambda z: jnp.concatenate([z[2 * r : 2 * r + 2, :LANES] for r in range(rows)], axis=1)
    fresh = cells(block)
    weighted = cells(block * cosl_ref[...])
    u = u_ref[:, :own]
    modes = u.shape[0]
    high, lower = split(jnp.concatenate([u * weighted[0:1], u * weighted[1:2]], axis=0))
    left = jnp.concatenate([high, lower], axis=0)
    high, lower = split(weighted)
    left_a = jnp.concatenate([high, lower], axis=0)
    lane = lane_ids((1, LANES))
    for j in range(2):
        gram = [total_of(weighted[j : j + 1] * fresh[i : i + 1]) for i in range(2)]
        sum_ref[j : j + 1, days:] = jnp.where(lane == 0, gram[0], jnp.where(lane == 1, gram[1], 0.0))
    old = [[total_of(weighted[j : j + 1] * u[low + i : low + i + 1]) for i in range(2)] for j in range(2)]
    for first in range(0, days, chunk):
        at = slice(first, first + chunk)
        masked = jnp.dot(left, m_ref[:, at], preferred_element_type=F32)
        given = jnp.dot(left_a, a_ref[:, at], preferred_element_type=F32)
        v = v_ref[:, at]
        for j in range(2):
            part = masked[j * modes : (j + 1) * modes] + masked[(2 + j) * modes : (3 + j) * modes]
            sum_ref[j : j + 1, at] = (
                given[j : j + 1]
                + given[2 + j : 3 + j]
                - jnp.sum(v * part, axis=0, keepdims=True)
                + old[j][0] * v[low : low + 1]
                + old[j][1] * v[low + 1 : low + 2]
            )


def last_kernel(rows, reach, total, *refs):
    v_ref, u_ref, sum_ref, block_ref, place_ref = refs[:5]
    maps_out, series_out, maps_new, series_new, sems = refs[7:]
    share = series_new.shape[1]
    stores = [
        pltpu.make_async_copy(maps_new, maps_out.at[pl.ds(0, PAIRS)], sems.at[0]),
        pltpu.make_async_copy(series_new, series_out.at[pl.ds(0, PAIRS)], sems.at[1]),
    ]
    vn, un = new_pair(rows, reach, total, sum_ref, block_ref)
    u = jnp.concatenate([u_ref[: PAIRS - 2], un], axis=0)
    for r in range(rows):
        maps_new[:, r, :] = u[:, r * LANES : (r + 1) * LANES]
    stores[0].start()
    v = jnp.concatenate([v_ref[: PAIRS - 2], vn], axis=0)
    mine = v[:, :share]
    for i in range(1, v.shape[1] // share):
        mine = jnp.where(place_ref[3] == i, v[:, i * share : (i + 1) * share], mine)
    series_new[...] = mine
    stores[1].start()
    for store in stores:
        store.wait()


def call(kernel, name, outs, scratch, args, smem=(), mib=24, flops=0, copies=0, in_hbm=(), out_hbm=(), aliases={}):
    moved = sum(z.size * z.dtype.itemsize for z in args)
    hbm = pl.BlockSpec(memory_space=pl.ANY)
    args = [pltpu.with_memory_space_constraint(z, pltpu.HBM) if i in in_hbm else z for i, z in enumerate(args)]
    return pl.pallas_call(
        kernel,
        out_shape=[jax.ShapeDtypeStruct(s, t) for s, t in outs],
        in_specs=[SMEM if i in smem else hbm if i in in_hbm else VMEM for i in range(len(args))],
        out_specs=[hbm if i in out_hbm else VMEM for i in range(len(outs))],
        scratch_shapes=[pltpu.VMEM(s, t) for s, t in scratch] + ([pltpu.SemaphoreType.DMA((copies,))] if copies else []),
        input_output_aliases=aliases,
        compiler_params=pltpu.CompilerParams(vmem_limit_bytes=mib * 2**20),
        cost_estimate=pl.CostEstimate(flops=flops, bytes_accessed=moved, transcendentals=0),
        name=name,
    )(*args)


def latitude_cos(rows, nrows):
    degree = -60.0 + 120.0 * (rows.astype(F32) + 0.5) / nrows
    return jnp.cos(degree * (jnp.pi / 180.0))


def shards(sea_heat_deviations, missing_date_bitmask, ocean_binary_mask, mode_maps, mode_series):
    rows, columns, days = sea_heat_deviations.shape
    modes, words = (mode_maps.shape[0], missing_date_bitmask.shape[2])
    nlat = rows * lax.axis_size("lat")
    total = float(modes * nlat * columns * lax.axis_size("lon"))
    own, reach = (rows * columns, SWEEPS * STEPS)
    sides = 2 * rows * reach
    cells = own + sides
    assert columns == LANES and sides == LANES and rows == SWEEPS and days == BITS * words
    chunk = days // 5
    row0 = lax.axis_index("lat") * rows
    here = lax.axis_index("lon")
    place = jnp.stack([row0, jnp.int32(nlat), lax.axis_index("lat") % 2, here]).astype(jnp.int32)
    tall = row0 - rows + jnp.arange(6 * rows) // 2
    cos_tall = latitude_cos(tall, nlat)[:, None]
    klon = jnp.broadcast_to(KLON / (cos_tall * cos_tall), (6 * rows, 2 * LANES))
    cosl = jnp.broadcast_to(cos_tall[2 * rows : 4 * rows], (2 * rows, 2 * LANES))

    words_per = words // LANES
    flags_scratch = [((2 * LANES, days // words_per), BF16), ((1, days // words_per), jnp.int32)]
    edge = ((modes + 8 + rows * reach * words_per, LANES), F32)
    inputs = [missing_date_bitmask.reshape(own, words), ocean_binary_mask, sea_heat_deviations.reshape(own, days)]
    inputs += [mode_maps, mode_series]
    place, klon, cosl = lax.optimization_barrier((place, klon, cosl))
    m, a, u, row, near, far, maps_out, series_out = call(
        functools.partial(own_flags_kernel, reach),
        "own_flags",
        [((own, days), BF16), ((own, days), BF16), ((modes, own), F32), ((1, own), F32), edge, edge]
        + [(mode_maps.shape, F32), (mode_series.shape, F32)],
        [((own, words), jnp.int32), ((rows, LANES), jnp.int32), ((own, days), BF16)]
        + [(mode_maps.shape, F32), (mode_series.shape, F32), *flags_scratch],
        [*inputs, place],
        smem=(5,),
        in_hbm=range(5),
        out_hbm=(6, 7),
        copies=6 + rows,
        flops=4 * LANES * own * days,
    )
    if lax.axis_size("lon") == 8:
        pieces = [swap(mode_series, 0, b | 1) for b in (2, 4, 6)]
        *pieces, m, a = lax.optimization_barrier((*pieces, m, a))
        pieces = [z for piece in pieces for z in (swap(piece, 0, 1), piece)]
        pieces = [mode_series, swap(mode_series, 0, 1), *pieces]
    else:
        pieces = [lax.all_gather(mode_series, "lon", axis=1, tiled=True)]
    near, far = lon_partners(near, far)
    v, xv, near_xv, far_xv = call(
        functools.partial(given_kernel, rows, reach),
        "given",
        [((modes, days), F32), ((PAIRS, own), F32), ((PAIRS, LANES), F32), ((PAIRS, LANES), F32)],
        [],
        [a, place, *pieces],
        smem=(1,),
        flops=4 * PAIRS * own * days,
    )
    near_xv, far_xv = lon_partners(near_xv, far_xv)
    base, m_halo, u, row = call(
        functools.partial(first_products_kernel, chunk),
        "first_products",
        [((2, cells), F32), ((sides, days), BF16), ((modes, cells), F32), ((1, cells), F32)],
        flags_scratch,
        [near, far, place, m, v, u, row],
        smem=(2,),
        flops=8 * modes * cells * days,
    )

    count = 2 * rows
    summed = block = None
    coasts = ()
    for step in range(STEPS):
        if step == 0:
            fresh, xv_halo = call(
                functools.partial(first_fields_kernel, rows, reach),
                "fields_0",
                [((2 * count, 2 * LANES), F32), ((PAIRS, sides), F32)],
                [],
                [near_xv, far_xv, place, v, u, row, xv, base],
                smem=(2,),
            )
        else:
            fresh, v, u = call(
                functools.partial(fields_kernel, step, rows, reach, total, chunk),
                f"fields_{step}",
                [((count, 2 * LANES), F32), ((modes, days), F32), ((modes, cells), F32)],
                [],
                [m, m_halo, v, u, row, xv, xv_halo, summed, block],
                flops=8 * modes * cells * days,
            )
        got_a, got_b = lat_partners(fresh)
        partial_sums, block = call(
            functools.partial(sums_kernel, step, rows, chunk),
            f"sums_{step}",
            [((2, days + LANES), F32), ((count, 2 * LANES), F32)],
            [],
            [m, a, v, u, place, klon, cosl, fresh, got_a, got_b, *coasts],
            smem=(4,),
            flops=8 * modes * own * days,
        )
        if step == 0:
            coasts = (fresh, got_a, got_b)
        summed = sum_all(partial_sums)
    return call(
        functools.partial(last_kernel, rows, reach, total),
        "last",
        [(mode_maps.shape, F32), (mode_series.shape, F32)],
        [((PAIRS, rows, columns), F32), ((PAIRS, mode_series.shape[1]), F32)],
        [v, u, summed, block, place, maps_out, series_out],
        smem=(4,),
        in_hbm=(5, 6),
        out_hbm=(0, 1),
        copies=2,
        aliases={5: 0, 6: 1},
    )


def solution(mesh):
    in_specs = (
        P("lat", "lon", None),
        P("lat", "lon", None),
        P("lat", "lon"),
        P(None, "lat", "lon"),
        P(None, "lon"),
    )
    out_specs = (P(None, "lat", "lon"), P(None, "lon"))
    return jax.shard_map(shards, mesh=mesh, in_specs=in_specs, out_specs=out_specs, check_vma=False)
```

```python
import functools

import jax
import jax.numpy as jnp
from jax import lax
from jax.experimental import pallas as pl
from jax.experimental.pallas import tpu as pltpu
from jax.sharding import PartitionSpec as P

STEPS = 4
SWEEPS = 4
PAIRS = 2 * STEPS
BITS = 15
LANES = 128

KLAT = 0.2
KLON = 0.05
EPS = 1e-06
F32 = jnp.float32
BF16 = jnp.bfloat16
VMEM = pl.BlockSpec(memory_space=pltpu.VMEM)
SMEM = pl.BlockSpec(memory_space=pltpu.SMEM)
NT = (((1,), (1,)), ((), ()))


def pairing(lat_map, lon_map):
    nlat, nlon = (lax.axis_size("lat"), lax.axis_size("lon"))
    return [(i * nlon + j, lat_map(i) * nlon + lon_map(j)) for i in range(nlat) for j in range(nlon)]


def swap(x, lat_bits, lon_bits):
    return lax.ppermute(x, ("lat", "lon"), pairing(lambda i: i ^ lat_bits, lambda j: j ^ lon_bits))


def sum_all(x):
    nlat, nlon = (lax.axis_size("lat"), lax.axis_size("lon"))
    if nlat & (nlat - 1) or nlon & (nlon - 1):
        return lax.psum(x, ("lat", "lon"))
    core = 1 if nlon > 1 else 0
    if core:
        x = x + swap(x, 0, core)
    for size, first, on_lat in ((nlat, 1, True), (nlon, 2, False)):
        bit = first
        while bit < size:
            bits = lambda b: (b, core) if on_lat else (0, b | core)
            if 2 * bit < size:
                near, far, both = (swap(x, *bits(b)) for b in (bit, 2 * bit, 3 * bit))
                x = (x + near) + (far + both)
                bit *= 4
            else:
                x = x + swap(x, *bits(bit))
                bit *= 2
    return x


def lat_partners(x):
    count = lax.axis_size("lat")
    same = lambda j: j
    got_a = lax.ppermute(x, ("lat", "lon"), pairing(lambda i: i ^ 1, same))
    got_b = lax.ppermute(x, ("lat", "lon"), pairing(lambda i: (i + 1 if i % 2 else i - 1) % count, same))
    return got_a, got_b


def lon_partners(near, far):
    count = lax.axis_size("lon")
    same = lambda i: i
    got_far = lax.ppermute(far, ("lat", "lon"), pairing(same, lambda j: (j + 1 if j % 2 else j - 1) % count))
    return swap(near, 0, 1), got_far


def split(x):
    high = x.astype(BF16)
    return high, (x - high.astype(F32)).astype(BF16)


def solve_pair(g00, g01, g10, g11, right0, right1):
    determ = g00 * g11 - g01 * g10
    return (g11 * right0 - g01 * right1) / determ, (g00 * right1 - g10 * right0) / determ


def total_of(x):
    return jnp.sum(x, axis=1, keepdims=True)


def lane_ids(shape):
    return lax.broadcasted_iota(jnp.int32, shape, 1)


def to_block(field, rows, reach):
    n, own = (field.shape[0], rows * LANES)
    halo = field[:, own:]
    lane = lane_ids((n, LANES))
    parts = []
    for r in range(rows):
        east = pltpu.roll(halo, (LANES - rows * reach - reach * r) % LANES, 1)
        west = pltpu.roll(halo, (LANES - reach - reach * r) % LANES, 1)
        edge = jnp.where(lane < LANES // 2, east, west)
        parts.append(jnp.concatenate([field[:, r * LANES : (r + 1) * LANES], edge], axis=1))
    return jnp.concatenate(parts, axis=0)


def from_block(block, rows, reach):
    n = block.shape[0] // rows
    lane = lane_ids((n, LANES))
    halo = jnp.zeros((n, LANES), F32)
    own = []
    for r in range(rows):
        part = block[r * n : (r + 1) * n]
        own.append(part[:, :LANES])
        edge = part[:, LANES:]
        east = pltpu.roll(edge, (rows * reach + reach * r) % LANES, 1)
        west = pltpu.roll(edge, (reach * r + reach) % LANES, 1)
        first = reach * r
        halo = jnp.where((lane >= first) & (lane < first + reach), west, halo)
        first = rows * reach + reach * r
        halo = jnp.where((lane >= first) & (lane < first + reach), east, halo)
    return jnp.concatenate(own + [halo], axis=1)


def unpack_words(words, spread_ref, bit_ref):
    top = ((words >> 8) << 8).astype(F32).astype(BF16)
    bottom = (words & 255).astype(F32).astype(BF16)
    spread = spread_ref[...]
    each = jnp.dot(jnp.concatenate([top, bottom], axis=1), spread, preferred_element_type=F32).astype(jnp.int32)
    return jnp.where((each & bit_ref[...]) == 0, 1.0, 0.0).astype(BF16)


def fill_spread(spread_ref, bit_ref):
    days = spread_ref.shape[1]
    word = lax.broadcasted_iota(jnp.int32, (LANES, days), 0)
    rest = lane_ids((LANES, days)) - BITS * word
    hit = jnp.where((rest >= 0) & (rest < BITS), 1.0, 0.0).astype(BF16)
    spread_ref[:LANES] = hit
    spread_ref[LANES:] = hit
    word = jnp.where((rest >= 0) & (rest < BITS), rest, 0)
    bit_ref[...] = jnp.left_shift(1, jnp.sum(word, axis=0, keepdims=True))


def fill_spread_days(spread_ref):
    days = spread_ref.shape[0]
    rest = lax.broadcasted_iota(jnp.int32, (days, LANES), 0) - BITS * lane_ids((days, LANES))
    hit = jnp.where((rest >= 0) & (rest < BITS), 1.0, 0.0).astype(BF16)
    spread_ref[:, :LANES] = hit
    spread_ref[:, LANES:] = hit


def unpack_days(words, spread_ref, m_ref):
    days = spread_ref.shape[0]
    step = days // 5
    for g in range(words.shape[1] // LANES):
        group = words[:, g * LANES : (g + 1) * LANES]
        top = ((group >> 8) << 8).astype(F32).astype(BF16)
        bottom = (group & 255).astype(F32).astype(BF16)
        both = jnp.concatenate([top, bottom], axis=1)
        for first in range(0, days, step):
            each = lax.dot_general(spread_ref[first : first + step], both, NT, preferred_element_type=F32).astype(jnp.int32)
            day = first + lax.broadcasted_iota(jnp.int32, (step, LANES), 0)
            bit = jnp.left_shift(1, day - BITS * ((day * 34953) >> 19))
            for c in range(0, each.shape[1], LANES):
                flags = jnp.where((each[:, c : c + LANES] & bit) == 0, 1.0, 0.0).astype(BF16)
                m_ref[g * days + first : g * days + first + step, c : c + LANES] = flags


def as_column(row):
    return jnp.transpose(jnp.broadcast_to(row, (8, LANES)))[:, :1]


def own_flags_kernel(reach, *refs):
    words_hbm, coast_hbm, x_hbm, maps_hbm, series_hbm, place_ref = refs[:6]
    m_ref, a_ref, mt_ref, spread_days_ref, u_ref, row_ref, near_ref, far_ref, maps_out, series_out = refs[6:16]
    words_ref, coast_ref, x_ref, maps_ref, series_ref, spread_ref, bit_ref, sems = refs[16:]
    rows = coast_ref.shape[0]
    loads = [
        pltpu.make_async_copy(words_hbm, words_ref, sems.at[0]),
        pltpu.make_async_copy(coast_hbm, coast_ref, sems.at[1]),
    ]
    for r in range(rows):
        at = pl.ds(r * LANES, LANES)
        loads.append(pltpu.make_async_copy(x_hbm.at[at], x_ref.at[at], sems.at[2 + r]))
    loads.append(pltpu.make_async_copy(maps_hbm, maps_ref, sems.at[2 + rows]))
    loads.append(pltpu.make_async_copy(series_hbm, series_ref, sems.at[3 + rows]))
    stores = [
        pltpu.make_async_copy(maps_ref, maps_out, sems.at[4 + rows]),
        pltpu.make_async_copy(series_ref, series_out, sems.at[5 + rows]),
    ]
    for load in loads:
        load.start()
    fill_spread(spread_ref, bit_ref)
    fill_spread_days(spread_days_ref)
    loads[0].wait()
    loads[1].wait()
    for load, store in zip(loads[-2:], stores, strict=True):
        load.wait()
        store.start()
    days = spread_ref.shape[1]
    coast_own = coast_ref[...].astype(F32)
    coasts = jnp.transpose(jnp.concatenate([coast_own] * (8 // rows), axis=0))
    for r in range(rows):
        coast = coasts[:, r : r + 1]
        ocean = coast.astype(BF16)
        coast = coast.astype(jnp.int32)
        loads[2 + r].wait()
        cell = slice(r * LANES, (r + 1) * LANES)
        for g in range(words_ref.shape[1] // LANES):
            words = words_ref[cell, g * LANES : (g + 1) * LANES] * coast
            given = unpack_words(words, spread_ref, bit_ref)
            at = slice(g * days, (g + 1) * days)
            m_ref[cell, at] = given
            a_ref[cell, at] = x_ref[cell, at] * given * ocean
    column = jnp.concatenate([coasts[:, r : r + 1] for r in range(rows)], axis=0).astype(jnp.int32)
    unpack_days(words_ref[...] * column, spread_days_ref, mt_ref)
    modes = maps_ref.shape[0]
    pieces = []
    for r in range(rows):
        at = slice(r * LANES, (r + 1) * LANES)
        u = maps_ref[:, r, :]
        u_ref[:, at] = u
        row_ref[:, at] = coast_own[r : r + 1]
        pieces.append(jnp.concatenate([u, jnp.broadcast_to(coast_own[r : r + 1], (8, LANES))], axis=0))
    base = modes + 8
    odd = place_ref[3] % 2 == 1
    west, east = edges(pieces, reach)
    near_ref[:base] = jnp.where(odd, west, east)
    far_ref[:base] = jnp.where(odd, east, west)
    for g in range(words_ref.shape[1] // LANES):
        for r in range(rows):
            at = slice(base + reach * (rows * g + r), base + reach * (rows * g + r + 1))
            group = slice(g * LANES, (g + 1) * LANES)
            west = words_ref[r * LANES : r * LANES + reach, group].astype(F32)
            east = words_ref[(r + 1) * LANES - reach : (r + 1) * LANES, group].astype(F32)
            near_ref[at] = jnp.where(odd, west, east)
            far_ref[at] = jnp.where(odd, east, west)
    for store in stores:
        store.wait()


def edges(pieces, reach):
    rows = len(pieces)
    shape = pieces[0].shape
    lane = lane_ids(shape)
    west = jnp.zeros(shape, F32)
    east = west
    for r, part in enumerate(pieces):
        first = rows * reach + reach * r
        west = jnp.where((lane >= first) & (lane < first + reach), pltpu.roll(part, first % LANES, 1), west)
        first = reach * r
        east = jnp.where((lane >= first) & (lane < first + reach), pltpu.roll(part, (first + reach) % LANES, 1), east)
    return west, east


def in_order(pieces, here):
    bit = 1
    while bit < len(pieces):
        turn = (here // bit) % 2 == 1
        pieces = [jnp.where(turn, pieces[i ^ bit], pieces[i]) for i in range(len(pieces))]
        bit *= 2
    return pieces


def given_kernel(rows, reach, *refs):
    a_ref, place_ref = refs[:2]
    xv_ref, near_ref, far_ref, v_ref = refs[-4:]
    here = place_ref[3]
    share = refs[2].shape[1]
    for i, piece in enumerate(in_order([ref[:PAIRS] for ref in refs[2:-4]], here)):
        v_ref[:, i * share : (i + 1) * share] = piece
    high, low = split(v_ref[...])
    both = lax.dot_general(jnp.concatenate([high, low], axis=0), a_ref[...], NT, preferred_element_type=F32)
    xv = both[:PAIRS] + both[PAIRS:]
    xv_ref[...] = xv
    west, east = edges([xv[:, r * LANES : (r + 1) * LANES] for r in range(rows)], reach)
    odd = here % 2 == 1
    near_ref[...] = jnp.where(odd, west, east)
    far_ref[...] = jnp.where(odd, east, west)


def masked_products(vs, u, low, chunk, m_ref):
    modes, days = vs.shape
    acc = None
    for first in range(0, days, chunk):
        at = slice(first, first + chunk)
        v = vs[:, at]
        high, lower = split(jnp.concatenate([v * v[j : j + 1] for j in (low, low + 1)], axis=0))
        left = jnp.concatenate([high, lower], axis=0)
        part = jnp.dot(left, m_ref[at], preferred_element_type=F32)
        acc = part if acc is None else acc + part
    acc = acc[: 2 * modes] + acc[2 * modes :]
    return jnp.concatenate(
        [jnp.sum(u * acc[j * modes : (j + 1) * modes], axis=0, keepdims=True) for j in range(2)], axis=0
    )


def first_products_kernel(chunk, *refs):
    near_ref, far_ref, place_ref, m_ref, spread_ref, u_own_ref, row_own_ref = refs[:7]
    base_ref, v_ref, mh_ref, u_ref, row_ref = refs[-5:]
    share = refs[7].shape[1]
    for i, piece in enumerate(in_order([ref[...] for ref in refs[7:-5]], place_ref[3])):
        v_ref[:, i * share : (i + 1) * share] = piece
    odd = place_ref[3] % 2 == 1
    west = jnp.where(odd, near_ref[...], far_ref[...])
    east = jnp.where(odd, far_ref[...], near_ref[...])
    modes, own = u_own_ref.shape
    base = modes + 8
    lane = lane_ids((base, LANES))
    fields = jnp.where(lane < LANES // 2, west[:base], east[:base])
    u_own, u_halo, row_halo = (u_own_ref[...], fields[:modes], fields[modes : modes + 1])
    u_ref[:, :own] = u_own
    u_ref[:, own:] = u_halo
    row_ref[:, :own] = row_own_ref[...]
    row_ref[:, own:] = row_halo
    coast = as_column(row_halo).astype(jnp.int32)
    half = LANES // 2
    groups = [slice(base + half * g, base + half * (g + 1)) for g in range((west.shape[0] - base) // half)]
    words = jnp.concatenate([jnp.concatenate([west[at], east[at]], axis=0) for at in groups], axis=1)
    unpack_days(words.astype(jnp.int32) * coast, spread_ref, mh_ref)
    base_ref[:, :own] = masked_products(v_ref, u_own, 0, chunk, m_ref)
    base_ref[:, own:] = masked_products(v_ref, u_halo, 0, chunk, mh_ref)


def next_products_kernel(step, chunk, m_ref, mh_ref, v_ref, u_ref, base_ref):
    low = 2 * step
    own = m_ref.shape[1]
    mode = lax.broadcasted_iota(jnp.int32, u_ref.shape, 0)
    u = jnp.where((mode >= low - 2) & (mode < low), 0.0, u_ref[...])
    base_ref[:, :own] = masked_products(v_ref, u[:, :own], low, chunk, m_ref)
    base_ref[:, own:] = masked_products(v_ref, u[:, own:], low, chunk, mh_ref)


def changed_products(vn, un, pair, m_ref, mh_ref):
    high, lower = split(jnp.concatenate([vn * pair[0:1], vn * pair[1:2]], axis=0))
    left = jnp.concatenate([high, lower], axis=0)
    acc = jnp.concatenate(
        [
            jnp.dot(left, m_ref[...], preferred_element_type=F32),
            jnp.dot(left, mh_ref[...], preferred_element_type=F32),
        ],
        axis=1,
    )
    acc = acc[:4] + acc[4:]
    return jnp.concatenate([un[0:1] * acc[2 * j : 2 * j + 1] + un[1:2] * acc[2 * j + 1 : 2 * j + 2] for j in range(2)], axis=0)


def new_fields(pair, u_pair, coast, proj):
    v0, v1 = (pair[0:1], pair[1:2])
    h00, h01, h11 = (total_of(v0 * v0), total_of(v0 * v1), total_of(v1 * v1))
    add0, add1 = solve_pair(h00, h01, h01, h11, proj[0:1], proj[1:2])
    return coast * (u_pair + jnp.concatenate([add0, add1], axis=0))


def first_fields_kernel(rows, reach, near_ref, far_ref, place_ref, v_ref, u_ref, row_ref, xv_ref, base_ref, w_ref, xh_ref):
    odd = place_ref[3] % 2 == 1
    west = jnp.where(odd, near_ref[...], far_ref[...])
    east = jnp.where(odd, far_ref[...], near_ref[...])
    xh = jnp.where(lane_ids((PAIRS, LANES)) < LANES // 2, west, east)
    xh_ref[...] = xh
    proj = jnp.concatenate([xv_ref[:2], xh[:2]], axis=1) - base_ref[...]
    coast = row_ref[...]
    count = 2 * rows
    w_ref[:count] = to_block(new_fields(v_ref[:2], u_ref[:2], coast, proj), rows, reach)
    w_ref[count:] = to_block(jnp.concatenate([coast, coast], axis=0), rows, reach)


def fields_kernel(step, rows, reach, total, *refs):
    m_ref, mh_ref, v_ref, u_ref, row_ref, xv_ref, xh_ref, base_ref, sum_ref, block_ref, w_ref, v_out, u_out = refs
    low = 2 * step
    vn, un = new_pair(rows, reach, total, sum_ref, block_ref)
    pair = v_ref[low : low + 2]
    given = jnp.concatenate([xv_ref[low : low + 2], xh_ref[low : low + 2]], axis=1)
    proj = given - base_ref[...] - changed_products(vn, un, pair, m_ref, mh_ref)
    w_ref[...] = to_block(new_fields(pair, u_ref[low : low + 2], row_ref[...], proj), rows, reach)
    v_out[...] = v_ref[...]
    u_out[...] = u_ref[...]
    v_out[low - 2 : low] = vn
    u_out[low - 2 : low] = un


def new_pair(rows, reach, total, sum_ref, block_ref):
    days = sum_ref.shape[1] - LANES
    gram = sum_ref[:, days:]
    g00, g01, g11 = (gram[0:1, 0:1], gram[0:1, 1:2], gram[1:2, 1:2])
    n0, n1 = (jnp.sqrt(g00 / total + EPS), jnp.sqrt(g11 / total + EPS))
    g00, g01, g11 = (g00 / (n0 * n0), g01 / (n0 * n1), g11 / (n1 * n1))
    determ = g00 * g11 - g01 * g01
    p0, p1 = (sum_ref[0:1, :days], sum_ref[1:2, :days])
    cross = g01 / determ
    first = (g11 / determ / n0) * p0 - (cross / n1) * p1
    second = (g00 / determ / n1) * p1 - (cross / n0) * p0
    field = from_block(block_ref[...], rows, reach)
    unit = jnp.concatenate([field[0:1] / n0, field[1:2] / n1], axis=0)
    return jnp.concatenate([first, second], axis=0), unit


def sums_kernel(step, rows, chunk, *refs):
    m_ref, a_ref, v_ref, u_ref, place_ref, klon_ref, cosl_ref, w_ref, gb_ref, ga_ref = refs[:10]
    refs = refs[10:]
    if step:
        coef_ref, sum_ref, block_ref = refs
    else:
        sum_ref, block_ref, coef_ref = refs
    days = v_ref.shape[1]
    low = 2 * step
    own = rows * LANES
    count = 2 * rows
    row0, nlat, odd = (place_ref[0], place_ref[1], place_ref[2])

    def assemble(mid, a, b):
        is_odd = odd == 1
        return jnp.concatenate([jnp.where(is_odd, a, b), mid, jnp.where(is_odd, b, a)], axis=0)

    w = assemble(w_ref[:count], ga_ref[:count], gb_ref[:count])
    tall = 3 * count
    north = lambda z: pltpu.roll(z, 2, 0)
    south = lambda z: pltpu.roll(z, tall - 2, 0)
    west = lambda z: pltpu.roll(z, 1, 1)
    east = lambda z: pltpu.roll(z, 2 * LANES - 1, 1)
    if step == 0:
        coast = assemble(w_ref[count:], ga_ref[count:], gb_ref[count:])
        row = row0 - rows + lax.broadcasted_iota(jnp.int32, (tall, 2 * LANES), 0) // 2
        coast = jnp.where((row >= 0) & (row < nlat), coast, 0.0)
        klon = klon_ref[...] * coast
        klat = KLAT * coast
        parts = [klat * north(coast), klat * south(coast), klon * west(coast), klon * east(coast)]
        parts.append(1.0 - ((parts[0] + parts[1]) + (parts[2] + parts[3])))
        for i, part in enumerate(parts):
            coef_ref[i * tall : (i + 1) * tall] = part
    an, as_, aw, ae, stay = (coef_ref[i * tall : (i + 1) * tall] for i in range(5))
    for _ in range(SWEEPS):
        w = stay * w + (an * north(w) + as_ * south(w)) + (aw * west(w) + ae * east(w))
    block = w[count : 2 * count]
    block_ref[...] = block
    cells = lambda z: jnp.concatenate([z[2 * r : 2 * r + 2, :LANES] for r in range(rows)], axis=1)
    fresh = cells(block)
    weighted = cells(block * cosl_ref[...])
    u = u_ref[:, :own]
    modes = u.shape[0]
    high, lower = split(jnp.concatenate([u * weighted[0:1], u * weighted[1:2]], axis=0))
    left = jnp.concatenate([high, lower], axis=0)
    high, lower = split(weighted)
    left_a = jnp.concatenate([high, lower], axis=0)
    lane = lane_ids((1, LANES))
    for j in range(2):
        gram = [total_of(weighted[j : j + 1] * fresh[i : i + 1]) for i in range(2)]
        sum_ref[j : j + 1, days:] = jnp.where(lane == 0, gram[0], jnp.where(lane == 1, gram[1], 0.0))
    old = [[total_of(weighted[j : j + 1] * u[low + i : low + i + 1]) for i in range(2)] for j in range(2)]
    for first in range(0, days, chunk):
        at = slice(first, first + chunk)
        masked = jnp.dot(left, m_ref[:, at], preferred_element_type=F32)
        given = jnp.dot(left_a, a_ref[:, at], preferred_element_type=F32)
        v = v_ref[:, at]
        for j in range(2):
            part = masked[j * modes : (j + 1) * modes] + masked[(2 + j) * modes : (3 + j) * modes]
            sum_ref[j : j + 1, at] = (
                given[j : j + 1]
                + given[2 + j : 3 + j]
                - jnp.sum(v * part, axis=0, keepdims=True)
                + old[j][0] * v[low : low + 1]
                + old[j][1] * v[low + 1 : low + 2]
            )


def last_kernel(rows, reach, total, *refs):
    v_ref, u_ref, sum_ref, block_ref, place_ref = refs[:5]
    maps_out, series_out, maps_new, series_new, sems = refs[7:]
    share = series_new.shape[1]
    stores = [
        pltpu.make_async_copy(maps_new, maps_out.at[pl.ds(0, PAIRS)], sems.at[0]),
        pltpu.make_async_copy(series_new, series_out.at[pl.ds(0, PAIRS)], sems.at[1]),
    ]
    vn, un = new_pair(rows, reach, total, sum_ref, block_ref)
    u = jnp.concatenate([u_ref[: PAIRS - 2], un], axis=0)
    for r in range(rows):
        maps_new[:, r, :] = u[:, r * LANES : (r + 1) * LANES]
    stores[0].start()
    v = jnp.concatenate([v_ref[: PAIRS - 2], vn], axis=0)
    mine = v[:, :share]
    for i in range(1, v.shape[1] // share):
        mine = jnp.where(place_ref[3] == i, v[:, i * share : (i + 1) * share], mine)
    series_new[...] = mine
    stores[1].start()
    for store in stores:
        store.wait()


def call(kernel, name, outs, scratch, args, smem=(), mib=24, flops=0, copies=0, in_hbm=(), out_hbm=(), aliases={}):
    moved = sum(z.size * z.dtype.itemsize for z in args)
    hbm = pl.BlockSpec(memory_space=pl.ANY)
    args = [pltpu.with_memory_space_constraint(z, pltpu.HBM) if i in in_hbm else z for i, z in enumerate(args)]
    return pl.pallas_call(
        kernel,
        out_shape=[jax.ShapeDtypeStruct(s, t) for s, t in outs],
        in_specs=[SMEM if i in smem else hbm if i in in_hbm else VMEM for i in range(len(args))],
        out_specs=[hbm if i in out_hbm else VMEM for i in range(len(outs))],
        scratch_shapes=[pltpu.VMEM(s, t) for s, t in scratch] + ([pltpu.SemaphoreType.DMA((copies,))] if copies else []),
        input_output_aliases=aliases,
        compiler_params=pltpu.CompilerParams(vmem_limit_bytes=mib * 2**20),
        cost_estimate=pl.CostEstimate(flops=flops, bytes_accessed=moved, transcendentals=0),
        name=name,
    )(*args)


def latitude_cos(rows, nrows):
    degree = -60.0 + 120.0 * (rows.astype(F32) + 0.5) / nrows
    return jnp.cos(degree * (jnp.pi / 180.0))


def shards(sea_heat_deviations, missing_date_bitmask, ocean_binary_mask, mode_maps, mode_series):
    rows, columns, days = sea_heat_deviations.shape
    modes, words = (mode_maps.shape[0], missing_date_bitmask.shape[2])
    nlat = rows * lax.axis_size("lat")
    total = float(modes * nlat * columns * lax.axis_size("lon"))
    own, reach = (rows * columns, SWEEPS * STEPS)
    sides = 2 * rows * reach
    cells = own + sides
    assert columns == LANES and sides == LANES and rows == SWEEPS and days == BITS * words
    chunk = days // 5
    row0 = lax.axis_index("lat") * rows
    here = lax.axis_index("lon")
    place = jnp.stack([row0, jnp.int32(nlat), lax.axis_index("lat") % 2, here]).astype(jnp.int32)
    tall = row0 - rows + jnp.arange(6 * rows) // 2
    cos_tall = latitude_cos(tall, nlat)[:, None]
    klon = jnp.broadcast_to(KLON / (cos_tall * cos_tall), (6 * rows, 2 * LANES))
    cosl = jnp.broadcast_to(cos_tall[2 * rows : 4 * rows], (2 * rows, 2 * LANES))

    words_per = words // LANES
    flags_scratch = [((2 * LANES, days // words_per), BF16), ((1, days // words_per), jnp.int32)]
    edge = ((modes + 8 + rows * reach * words_per, LANES), F32)
    inputs = [missing_date_bitmask.reshape(own, words), ocean_binary_mask, sea_heat_deviations.reshape(own, days)]
    inputs += [mode_maps, mode_series]
    place, klon, cosl = lax.optimization_barrier((place, klon, cosl))
    m, a, m_days, spread, u, row, near, far, maps_out, series_out = call(
        functools.partial(own_flags_kernel, reach),
        "own_flags",
        [((own, days), BF16), ((own, days), BF16), ((days, own), BF16), ((days // words_per, 2 * LANES), BF16)]
        + [((modes, own), F32), ((1, own), F32), edge, edge]
        + [(mode_maps.shape, F32), (mode_series.shape, F32)],
        [((own, words), jnp.int32), ((rows, LANES), jnp.int32), ((own, days), BF16)]
        + [(mode_maps.shape, F32), (mode_series.shape, F32), *flags_scratch],
        [*inputs, place],
        smem=(5,),
        in_hbm=range(5),
        out_hbm=(8, 9),
        copies=6 + rows,
        flops=4 * LANES * own * days,
    )
    if lax.axis_size("lon") == 8:
        pieces = [swap(mode_series, 0, b | 1) for b in (2, 4, 6)]
        *pieces, m, a, m_days = lax.optimization_barrier((*pieces, m, a, m_days))
        pieces = [z for piece in pieces for z in (swap(piece, 0, 1), piece)]
        pieces = [mode_series, swap(mode_series, 0, 1), *pieces]
    else:
        pieces = [lax.all_gather(mode_series, "lon", axis=1, tiled=True)]
    near, far = lon_partners(near, far)
    xv, near_xv, far_xv = call(
        functools.partial(given_kernel, rows, reach),
        "given",
        [((PAIRS, own), F32), ((PAIRS, LANES), F32), ((PAIRS, LANES), F32)],
        [((PAIRS, days), F32)],
        [a, place, *pieces],
        smem=(1,),
        flops=4 * PAIRS * own * days,
    )
    near_xv, far_xv = lon_partners(near_xv, far_xv)
    base, v, m_halo, u, row = call(
        functools.partial(first_products_kernel, chunk),
        "first_products",
        [((2, cells), F32), ((modes, days), F32), ((days, sides), BF16), ((modes, cells), F32), ((1, cells), F32)],
        [],
        [near, far, place, m_days, spread, u, row, *pieces],
        smem=(2,),
        flops=8 * modes * cells * days,
    )

    count = 2 * rows
    summed = block = None
    coefs = []
    for step in range(STEPS):
        if step == 0:
            fresh, xv_halo = call(
                functools.partial(first_fields_kernel, rows, reach),
                "fields_0",
                [((2 * count, 2 * LANES), F32), ((PAIRS, sides), F32)],
                [],
                [near_xv, far_xv, place, v, u, row, xv, base],
                smem=(2,),
            )
        else:
            fresh, v, u = call(
                functools.partial(fields_kernel, step, rows, reach, total),
                f"fields_{step}",
                [((count, 2 * LANES), F32), ((modes, days), F32), ((modes, cells), F32)],
                [],
                [m_days, m_halo, v, u, row, xv, xv_halo, base, summed, block],
                flops=8 * modes * cells * days,
            )
        got_a, got_b = lat_partners(fresh)
        outs = [((2, days + LANES), F32), ((count, 2 * LANES), F32)]
        coef = ((5 * 3 * count, 2 * LANES), F32)
        partial_sums, block, *made = call(
            functools.partial(sums_kernel, step, rows, chunk),
            f"sums_{step}",
            outs if step else [*outs, coef],
            [],
            [m, a, v, u, place, klon, cosl, fresh, got_b, got_a, *coefs],
            smem=(4,),
            flops=8 * modes * own * days,
        )
        coefs = coefs or made
        if step + 1 < STEPS:
            (base,) = call(
                functools.partial(next_products_kernel, step + 1, chunk),
                f"next_products_{step + 1}",
                [((2, cells), F32)],
                [],
                [m_days, m_halo, v, u],
                flops=8 * modes * cells * days,
            )
        summed = sum_all(partial_sums)
    return call(
        functools.partial(last_kernel, rows, reach, total),
        "last",
        [(mode_maps.shape, F32), (mode_series.shape, F32)],
        [((PAIRS, rows, columns), F32), ((PAIRS, mode_series.shape[1]), F32)],
        [v, u, summed, block, place, maps_out, series_out],
        smem=(4,),
        in_hbm=(5, 6),
        out_hbm=(0, 1),
        copies=2,
        aliases={5: 0, 6: 1},
    )


def solution(mesh):
    in_specs = (
        P("lat", "lon", None),
        P("lat", "lon", None),
        P("lat", "lon"),
        P(None, "lat", "lon"),
        P(None, "lon"),
    )
    out_specs = (P(None, "lat", "lon"), P(None, "lon"))
    return jax.shard_map(shards, mesh=mesh, in_specs=in_specs, out_specs=out_specs, check_vma=False)
```

```python
import functools

import jax
import jax.numpy as jnp
from jax import lax
from jax.experimental import pallas as pl
from jax.experimental.pallas import tpu as pltpu
from jax.sharding import PartitionSpec as P

STEPS = 4
SWEEPS = 4
PAIRS = 2 * STEPS
BITS = 15
LANES = 128

KLAT = 0.2
KLON = 0.05
EPS = 1e-06
F32 = jnp.float32
BF16 = jnp.bfloat16
VMEM = pl.BlockSpec(memory_space=pltpu.VMEM)
SMEM = pl.BlockSpec(memory_space=pltpu.SMEM)
NT = (((1,), (1,)), ((), ()))


def pairing(lat_map, lon_map):
    nlat, nlon = (lax.axis_size("lat"), lax.axis_size("lon"))
    return [(i * nlon + j, lat_map(i) * nlon + lon_map(j)) for i in range(nlat) for j in range(nlon)]


def swap(x, lat_bits, lon_bits):
    return lax.ppermute(x, ("lat", "lon"), pairing(lambda i: i ^ lat_bits, lambda j: j ^ lon_bits))


def sum_all(x):
    nlat, nlon = (lax.axis_size("lat"), lax.axis_size("lon"))
    if nlat & (nlat - 1) or nlon & (nlon - 1):
        return lax.psum(x, ("lat", "lon"))
    core = 1 if nlon > 1 else 0
    if core:
        x = x + swap(x, 0, core)
    for size, first, on_lat in ((nlat, 1, True), (nlon, 2, False)):
        bit = first
        while bit < size:
            bits = lambda b: (b, core) if on_lat else (0, b | core)
            if 2 * bit < size:
                near, far, both = (swap(x, *bits(b)) for b in (bit, 2 * bit, 3 * bit))
                x = (x + near) + (both + far)
                bit *= 4
            else:
                x = x + swap(x, *bits(bit))
                bit *= 2
    return x


def lat_partners(x):
    count = lax.axis_size("lat")
    same = lambda j: j
    got_a = lax.ppermute(x, ("lat", "lon"), pairing(lambda i: i ^ 1, same))
    got_b = lax.ppermute(x, ("lat", "lon"), pairing(lambda i: (i + 1 if i % 2 else i - 1) % count, same))
    return got_a, got_b


def lon_partners(near, far):
    count = lax.axis_size("lon")
    same = lambda i: i
    got_far = lax.ppermute(far, ("lat", "lon"), pairing(same, lambda j: (j + 1 if j % 2 else j - 1) % count))
    return swap(near, 0, 1), got_far


def split(x):
    high = x.astype(BF16)
    return high, (x - high.astype(F32)).astype(BF16)


def solve_pair(g00, g01, g10, g11, right0, right1):
    determ = g00 * g11 - g01 * g10
    return (g11 * right0 - g01 * right1) / determ, (g00 * right1 - g10 * right0) / determ


def total_of(x):
    return jnp.sum(x, axis=1, keepdims=True)


def lane_ids(shape):
    return lax.broadcasted_iota(jnp.int32, shape, 1)


def to_block(field, rows, reach):
    n, own = (field.shape[0], rows * LANES)
    halo = field[:, own:]
    lane = lane_ids((n, LANES))
    parts = []
    for r in range(rows):
        east = pltpu.roll(halo, (LANES - rows * reach - reach * r) % LANES, 1)
        west = pltpu.roll(halo, (LANES - reach - reach * r) % LANES, 1)
        edge = jnp.where(lane < LANES // 2, east, west)
        parts.append(jnp.concatenate([field[:, r * LANES : (r + 1) * LANES], edge], axis=1))
    return jnp.concatenate(parts, axis=0)


def from_block(block, rows, reach):
    n = block.shape[0] // rows
    lane = lane_ids((n, LANES))
    halo = jnp.zeros((n, LANES), F32)
    own = []
    for r in range(rows):
        part = block[r * n : (r + 1) * n]
        own.append(part[:, :LANES])
        edge = part[:, LANES:]
        east = pltpu.roll(edge, (rows * reach + reach * r) % LANES, 1)
        west = pltpu.roll(edge, (reach * r + reach) % LANES, 1)
        first = reach * r
        halo = jnp.where((lane >= first) & (lane < first + reach), west, halo)
        first = rows * reach + reach * r
        halo = jnp.where((lane >= first) & (lane < first + reach), east, halo)
    return jnp.concatenate(own + [halo], axis=1)


def unpack_words(words, spread_ref, bit_ref):
    top = ((words >> 8) << 8).astype(F32).astype(BF16)
    bottom = (words & 255).astype(F32).astype(BF16)
    spread = spread_ref[...]
    each = jnp.dot(jnp.concatenate([top, bottom], axis=1), spread, preferred_element_type=F32).astype(jnp.int32)
    return jnp.where((each & bit_ref[...]) == 0, 1.0, 0.0).astype(BF16)


def fill_spread(spread_ref, bit_ref):
    days = spread_ref.shape[1]
    word = lax.broadcasted_iota(jnp.int32, (LANES, days), 0)
    rest = lane_ids((LANES, days)) - BITS * word
    hit = jnp.where((rest >= 0) & (rest < BITS), 1.0, 0.0).astype(BF16)
    spread_ref[:LANES] = hit
    spread_ref[LANES:] = hit
    word = jnp.where((rest >= 0) & (rest < BITS), rest, 0)
    bit_ref[...] = jnp.left_shift(1, jnp.sum(word, axis=0, keepdims=True))


def fill_spread_days(spread_ref):
    days = spread_ref.shape[0]
    rest = lax.broadcasted_iota(jnp.int32, (days, LANES), 0) - BITS * lane_ids((days, LANES))
    hit = jnp.where((rest >= 0) & (rest < BITS), 1.0, 0.0).astype(BF16)
    spread_ref[:, :LANES] = hit
    spread_ref[:, LANES:] = hit


def unpack_days(words, spread_ref, m_ref):
    days = spread_ref.shape[0]
    step = days // 5
    for g in range(words.shape[1] // LANES):
        group = words[:, g * LANES : (g + 1) * LANES]
        top = ((group >> 8) << 8).astype(F32).astype(BF16)
        bottom = (group & 255).astype(F32).astype(BF16)
        both = jnp.concatenate([top, bottom], axis=1)
        for first in range(0, days, step):
            each = lax.dot_general(spread_ref[first : first + step], both, NT, preferred_element_type=F32).astype(jnp.int32)
            day = first + lax.broadcasted_iota(jnp.int32, (step, LANES), 0)
            bit = jnp.left_shift(1, day - BITS * ((day * 34953) >> 19))
            for c in range(0, each.shape[1], LANES):
                flags = jnp.where((each[:, c : c + LANES] & bit) == 0, 1.0, 0.0).astype(BF16)
                m_ref[g * days + first : g * days + first + step, c : c + LANES] = flags


def as_column(row):
    return jnp.transpose(jnp.broadcast_to(row, (8, LANES)))[:, :1]


def own_flags_kernel(reach, *refs):
    words_hbm, coast_hbm, x_hbm, maps_hbm, series_hbm, place_ref = refs[:6]
    m_ref, a_ref, held_ref, u_ref, row_ref, near_ref, far_ref, maps_out, series_out = refs[6:15]
    words_ref, coast_ref, x_ref, maps_ref, series_ref, spread_ref, bit_ref, sems = refs[15:]
    rows = coast_ref.shape[0]
    loads = [
        pltpu.make_async_copy(words_hbm, words_ref, sems.at[0]),
        pltpu.make_async_copy(coast_hbm, coast_ref, sems.at[1]),
    ]
    for r in range(rows):
        at = pl.ds(r * LANES, LANES)
        loads.append(pltpu.make_async_copy(x_hbm.at[at], x_ref.at[at], sems.at[2 + r]))
    loads.append(pltpu.make_async_copy(maps_hbm, maps_ref, sems.at[2 + rows]))
    loads.append(pltpu.make_async_copy(series_hbm, series_ref, sems.at[3 + rows]))
    stores = [
        pltpu.make_async_copy(maps_ref, maps_out, sems.at[4 + rows]),
        pltpu.make_async_copy(series_ref, series_out, sems.at[5 + rows]),
    ]
    for load in loads:
        load.start()
    fill_spread(spread_ref, bit_ref)
    loads[0].wait()
    loads[1].wait()
    for load, store in zip(loads[-2:], stores, strict=True):
        load.wait()
        store.start()
    days = spread_ref.shape[1]
    coast_own = coast_ref[...].astype(F32)
    coasts = jnp.transpose(jnp.concatenate([coast_own] * (8 // rows), axis=0))
    for r in range(rows):
        coast = coasts[:, r : r + 1]
        ocean = coast.astype(BF16)
        coast = coast.astype(jnp.int32)
        loads[2 + r].wait()
        cell = slice(r * LANES, (r + 1) * LANES)
        for g in range(words_ref.shape[1] // LANES):
            words = words_ref[cell, g * LANES : (g + 1) * LANES] * coast
            held_ref[cell, g * LANES : (g + 1) * LANES] = words
            given = unpack_words(words, spread_ref, bit_ref)
            at = slice(g * days, (g + 1) * days)
            m_ref[cell, at] = given
            a_ref[cell, at] = x_ref[cell, at] * given * ocean
    modes = maps_ref.shape[0]
    pieces = []
    for r in range(rows):
        at = slice(r * LANES, (r + 1) * LANES)
        u = maps_ref[:, r, :]
        u_ref[:, at] = u
        row_ref[:, at] = coast_own[r : r + 1]
        pieces.append(jnp.concatenate([u, jnp.broadcast_to(coast_own[r : r + 1], (8, LANES))], axis=0))
    base = modes + 8
    odd = place_ref[3] % 2 == 1
    west, east = edges(pieces, reach)
    near_ref[:base] = jnp.where(odd, west, east)
    far_ref[:base] = jnp.where(odd, east, west)
    for g in range(words_ref.shape[1] // LANES):
        for r in range(rows):
            at = slice(base + reach * (rows * g + r), base + reach * (rows * g + r + 1))
            group = slice(g * LANES, (g + 1) * LANES)
            west = words_ref[r * LANES : r * LANES + reach, group].astype(F32)
            east = words_ref[(r + 1) * LANES - reach : (r + 1) * LANES, group].astype(F32)
            near_ref[at] = jnp.where(odd, west, east)
            far_ref[at] = jnp.where(odd, east, west)
    for store in stores:
        store.wait()


def edges(pieces, reach):
    rows = len(pieces)
    shape = pieces[0].shape
    lane = lane_ids(shape)
    west = jnp.zeros(shape, F32)
    east = west
    for r, part in enumerate(pieces):
        first = rows * reach + reach * r
        west = jnp.where((lane >= first) & (lane < first + reach), pltpu.roll(part, first % LANES, 1), west)
        first = reach * r
        east = jnp.where((lane >= first) & (lane < first + reach), pltpu.roll(part, (first + reach) % LANES, 1), east)
    return west, east


def in_order(pieces, here):
    bit = 1
    while bit < len(pieces):
        turn = (here // bit) % 2 == 1
        pieces = [jnp.where(turn, pieces[i ^ bit], pieces[i]) for i in range(len(pieces))]
        bit *= 2
    return pieces


def given_kernel(rows, reach, *refs):
    a_ref, place_ref = refs[:2]
    xv_ref, near_ref, far_ref, v_ref = refs[-4:]
    here = place_ref[3]
    share = refs[2].shape[1]
    for i, piece in enumerate(in_order([ref[:PAIRS] for ref in refs[2:-4]], here)):
        v_ref[:, i * share : (i + 1) * share] = piece
    high, low = split(v_ref[...])
    both = lax.dot_general(jnp.concatenate([high, low], axis=0), a_ref[...], NT, preferred_element_type=F32)
    xv = both[:PAIRS] + both[PAIRS:]
    xv_ref[...] = xv
    west, east = edges([xv[:, r * LANES : (r + 1) * LANES] for r in range(rows)], reach)
    odd = here % 2 == 1
    near_ref[...] = jnp.where(odd, west, east)
    far_ref[...] = jnp.where(odd, east, west)


def masked_products(vs, u, low, chunk, m_ref, by_day=True):
    modes, days = vs.shape
    acc = None
    for first in range(0, days, chunk):
        at = slice(first, first + chunk)
        v = vs[:, at]
        high, lower = split(jnp.concatenate([v * v[j : j + 1] for j in (low, low + 1)], axis=0))
        left = jnp.concatenate([high, lower], axis=0)
        if by_day:
            part = jnp.dot(left, m_ref[at], preferred_element_type=F32)
        else:
            part = lax.dot_general(left, m_ref[:, at], NT, preferred_element_type=F32)
        acc = part if acc is None else acc + part
    acc = acc[: 2 * modes] + acc[2 * modes :]
    return jnp.concatenate(
        [jnp.sum(u * acc[j * modes : (j + 1) * modes], axis=0, keepdims=True) for j in range(2)], axis=0
    )


def first_products_kernel(chunk, *refs):
    near_ref, far_ref, place_ref, m_ref, u_own_ref, row_own_ref = refs[:6]
    base_ref, inv_ref, v_ref, mh_ref, u_ref, row_ref, spread_ref = refs[-7:]
    fill_spread_days(spread_ref)
    share = refs[6].shape[1]
    for i, piece in enumerate(in_order([ref[...] for ref in refs[6:-7]], place_ref[3])):
        v_ref[:, i * share : (i + 1) * share] = piece
    odd = place_ref[3] % 2 == 1
    west = jnp.where(odd, near_ref[...], far_ref[...])
    east = jnp.where(odd, far_ref[...], near_ref[...])
    modes, own = u_own_ref.shape
    base = modes + 8
    lane = lane_ids((base, LANES))
    fields = jnp.where(lane < LANES // 2, west[:base], east[:base])
    u_own, u_halo, row_halo = (u_own_ref[...], fields[:modes], fields[modes : modes + 1])
    u_ref[:, :own] = u_own
    u_ref[:, own:] = u_halo
    row_ref[:, :own] = row_own_ref[...]
    row_ref[:, own:] = row_halo
    coast = as_column(row_halo).astype(jnp.int32)
    half = LANES // 2
    groups = [slice(base + half * g, base + half * (g + 1)) for g in range((west.shape[0] - base) // half)]
    words = jnp.concatenate([jnp.concatenate([west[at], east[at]], axis=0) for at in groups], axis=1)
    unpack_days(words.astype(jnp.int32) * coast, spread_ref, mh_ref)
    base_ref[:, :own] = masked_products(v_ref, u_own, 0, chunk, m_ref, by_day=False)
    base_ref[:, own:] = masked_products(v_ref, u_halo, 0, chunk, mh_ref)
    inv_ref[...] = inverse_rows(v_ref[:2])


def days_flags_kernel(held_ref, spread_ref, m_ref):
    unpack_days(held_ref[...], spread_ref, m_ref)


def inverse_rows(pair):
    v0, v1 = (pair[0:1], pair[1:2])
    h00, h01, h11 = (total_of(v0 * v0), total_of(v0 * v1), total_of(v1 * v1))
    determ = h00 * h11 - h01 * h01
    rows = [h11 / determ, h01 / determ, h00 / determ]
    rows = [jnp.broadcast_to(z, (1, LANES)) for z in rows]
    return jnp.concatenate(rows + [jnp.zeros((5, LANES), F32)], axis=0)


def along(row, length):
    return jnp.concatenate([row] * (length // LANES), axis=1)


def next_products_kernel(step, chunk, m_ref, mh_ref, v_ref, u_ref, base_ref, inv_ref):
    low = 2 * step
    own = m_ref.shape[1]
    mode = lax.broadcasted_iota(jnp.int32, u_ref.shape, 0)
    u = jnp.where((mode >= low - 2) & (mode < low), 0.0, u_ref[...])
    base_ref[:, :own] = masked_products(v_ref, u[:, :own], low, chunk, m_ref)
    base_ref[:, own:] = masked_products(v_ref, u[:, own:], low, chunk, mh_ref)
    inv_ref[...] = inverse_rows(v_ref[low : low + 2])


def masked_rows(first, second, m_ref, mh_ref):
    high, lower = split(jnp.concatenate([first * second[0:1], first * second[1:2]], axis=0))
    left = jnp.concatenate([high, lower], axis=0)
    acc = jnp.concatenate(
        [
            jnp.dot(left, m_ref[...], preferred_element_type=F32),
            jnp.dot(left, mh_ref[...], preferred_element_type=F32),
        ],
        axis=1,
    )
    return acc[:4] + acc[4:]


def new_fields(inv_ref, u_pair, coast, proj):
    first, other, last = (along(inv_ref[i : i + 1], proj.shape[1]) for i in range(3))
    p0, p1 = (proj[0:1], proj[1:2])
    return coast * (u_pair + jnp.concatenate([first * p0 - other * p1, last * p1 - other * p0], axis=0))


def first_fields_kernel(rows, reach, near_ref, far_ref, place_ref, inv_ref, u_ref, row_ref, xv_ref, base_ref, w_ref, xh_ref):
    odd = place_ref[3] % 2 == 1
    west = jnp.where(odd, near_ref[...], far_ref[...])
    east = jnp.where(odd, far_ref[...], near_ref[...])
    xh = jnp.where(lane_ids((PAIRS, LANES)) < LANES // 2, west, east)
    xh_ref[...] = xh
    proj = jnp.concatenate([xv_ref[:2], xh[:2]], axis=1) - base_ref[...]
    coast = row_ref[...]
    count = 2 * rows
    w_ref[:count] = to_block(new_fields(inv_ref, u_ref[:2], coast, proj), rows, reach)
    w_ref[count:] = to_block(jnp.concatenate([coast, coast], axis=0), rows, reach)


def fields_kernel(step, rows, reach, total, *refs):
    m_ref, mh_ref, v_ref, u_ref, row_ref, xv_ref, xh_ref, base_ref, inv_ref, sum_ref, block_ref, w_ref, v_out, u_out = refs
    low = 2 * step
    days = v_ref.shape[1]
    sums = sum_ref[:, :days]
    masked = masked_rows(sums, v_ref[low : low + 2], m_ref, mh_ref)
    mixes, norms = mixing(total, sum_ref)
    un = new_units(rows, reach, norms, block_ref)
    cells = un.shape[1]
    mixes = [[along(z, cells) for z in mix] for mix in mixes]
    changed = []
    for j in range(2):
        p0, p1 = (masked[2 * j : 2 * j + 1], masked[2 * j + 1 : 2 * j + 2])
        changed.append(sum(un[k : k + 1] * (mixes[k][0] * p0 + mixes[k][1] * p1) for k in range(2)))
    given = jnp.concatenate([xv_ref[low : low + 2], xh_ref[low : low + 2]], axis=1)
    proj = given - base_ref[...] - jnp.concatenate(changed, axis=0)
    w_ref[...] = to_block(new_fields(inv_ref, u_ref[low : low + 2], row_ref[...], proj), rows, reach)
    v_out[low - 2 : low] = new_series(total, sum_ref)
    u_out[low - 2 : low] = un


def mixing(total, sum_ref):
    days = sum_ref.shape[1] - 2 * LANES
    g00, g01 = (sum_ref[0:1, days : days + LANES], sum_ref[0:1, days + LANES :])
    g11 = sum_ref[1:2, days + LANES :]
    n0, n1 = (jnp.sqrt(g00 / total + EPS), jnp.sqrt(g11 / total + EPS))
    g00, g01, g11 = (g00 / (n0 * n0), g01 / (n0 * n1), g11 / (n1 * n1))
    determ = g00 * g11 - g01 * g01
    cross = g01 / determ
    return [[g11 / determ / n0, -(cross / n1)], [-(cross / n0), g00 / determ / n1]], (n0, n1)


def new_series(total, sum_ref):
    days = sum_ref.shape[1] - 2 * LANES
    p0, p1 = (sum_ref[0:1, :days], sum_ref[1:2, :days])
    mixes, _ = mixing(total, sum_ref)
    return jnp.concatenate([along(mix[0], days) * p0 + along(mix[1], days) * p1 for mix in mixes], axis=0)


def new_units(rows, reach, norms, block_ref):
    field = from_block(block_ref[...], rows, reach)
    return jnp.concatenate([field[k : k + 1] / along(norms[k], field.shape[1]) for k in range(2)], axis=0)


def sums_kernel(step, rows, chunk, *refs):
    m_ref, a_ref, v_ref, u_ref, place_ref, klon_ref, cosl_ref, w_ref, ga_ref, gb_ref = refs[:10]
    refs = refs[10:]
    if step:
        coef_ref, sum_ref, block_ref = refs
    else:
        sum_ref, block_ref, coef_ref = refs
    days = v_ref.shape[1]
    low = 2 * step
    own = rows * LANES
    count = 2 * rows
    row0, nlat, odd = (place_ref[0], place_ref[1], place_ref[2])

    def assemble(mid, a, b):
        is_odd = odd == 1
        return jnp.concatenate([jnp.where(is_odd, a, b), mid, jnp.where(is_odd, b, a)], axis=0)

    w = assemble(w_ref[:count], ga_ref[:count], gb_ref[:count])
    tall = 3 * count
    north = lambda z: pltpu.roll(z, 2, 0)
    south = lambda z: pltpu.roll(z, tall - 2, 0)
    west = lambda z: pltpu.roll(z, 1, 1)
    east = lambda z: pltpu.roll(z, 2 * LANES - 1, 1)
    if step == 0:
        coast = assemble(w_ref[count:], ga_ref[count:], gb_ref[count:])
        row = row0 - rows + lax.broadcasted_iota(jnp.int32, (tall, 2 * LANES), 0) // 2
        coast = jnp.where((row >= 0) & (row < nlat), coast, 0.0)
        klon = klon_ref[...] * coast
        klat = KLAT * coast
        parts = [klat * north(coast), klat * south(coast), klon * west(coast), klon * east(coast)]
        parts.append(1.0 - ((parts[0] + parts[1]) + (parts[2] + parts[3])))
        for i, part in enumerate(parts):
            coef_ref[i * tall : (i + 1) * tall] = part
    an, as_, aw, ae, stay = (coef_ref[i * tall : (i + 1) * tall] for i in range(5))
    for _ in range(SWEEPS):
        w = stay * w + (an * north(w) + as_ * south(w)) + (aw * west(w) + ae * east(w))
    block = w[count : 2 * count]
    block_ref[...] = block
    cells = lambda z: jnp.concatenate([z[2 * r : 2 * r + 2, :LANES] for r in range(rows)], axis=1)
    fresh = cells(block)
    weighted = cells(block * cosl_ref[...])
    u = u_ref[:, :own]
    modes = u.shape[0]
    high, lower = split(jnp.concatenate([u * weighted[0:1], u * weighted[1:2]], axis=0))
    left = jnp.concatenate([high, lower], axis=0)
    high, lower = split(weighted)
    left_a = jnp.concatenate([high, lower], axis=0)
    for j in range(2):
        for i in range(2):
            gram = total_of(weighted[j : j + 1] * fresh[i : i + 1])
            sum_ref[j : j + 1, days + i * LANES : days + (i + 1) * LANES] = jnp.broadcast_to(gram, (1, LANES))
    old = [[total_of(weighted[j : j + 1] * u[low + i : low + i + 1]) for i in range(2)] for j in range(2)]
    for first in range(0, days, chunk):
        at = slice(first, first + chunk)
        masked = jnp.dot(left, m_ref[:, at], preferred_element_type=F32)
        given = jnp.dot(left_a, a_ref[:, at], preferred_element_type=F32)
        v = v_ref[:, at]
        for j in range(2):
            part = masked[j * modes : (j + 1) * modes] + masked[(2 + j) * modes : (3 + j) * modes]
            sum_ref[j : j + 1, at] = (
                given[j : j + 1]
                + given[2 + j : 3 + j]
                - jnp.sum(v * part, axis=0, keepdims=True)
                + old[j][0] * v[low : low + 1]
                + old[j][1] * v[low + 1 : low + 2]
            )


def last_kernel(rows, reach, total, *refs):
    v_ref, u_ref, sum_ref, block_ref, place_ref = refs[:5]
    maps_out, series_out, maps_new, series_new, sems = refs[7:]
    share = series_new.shape[1]
    stores = [
        pltpu.make_async_copy(maps_new, maps_out.at[pl.ds(0, PAIRS)], sems.at[0]),
        pltpu.make_async_copy(series_new, series_out.at[pl.ds(0, PAIRS)], sems.at[1]),
    ]
    un = new_units(rows, reach, mixing(total, sum_ref)[1], block_ref)
    vn = new_series(total, sum_ref)
    u = jnp.concatenate([u_ref[: PAIRS - 2], un], axis=0)
    for r in range(rows):
        maps_new[:, r, :] = u[:, r * LANES : (r + 1) * LANES]
    stores[0].start()
    v = jnp.concatenate([v_ref[: PAIRS - 2], vn], axis=0)
    mine = v[:, :share]
    for i in range(1, v.shape[1] // share):
        mine = jnp.where(place_ref[3] == i, v[:, i * share : (i + 1) * share], mine)
    series_new[...] = mine
    stores[1].start()
    for store in stores:
        store.wait()


def call(kernel, name, outs, scratch, args, smem=(), mib=24, flops=0, copies=0, in_hbm=(), out_hbm=(), aliases={}, light=False):
    moved = 0 if light else sum(z.size * z.dtype.itemsize for z in args)
    hbm = pl.BlockSpec(memory_space=pl.ANY)
    args = [pltpu.with_memory_space_constraint(z, pltpu.HBM) if i in in_hbm else z for i, z in enumerate(args)]
    return pl.pallas_call(
        kernel,
        out_shape=[jax.ShapeDtypeStruct(s, t) for s, t in outs],
        in_specs=[SMEM if i in smem else hbm if i in in_hbm else VMEM for i in range(len(args))],
        out_specs=[hbm if i in out_hbm else VMEM for i in range(len(outs))],
        scratch_shapes=[pltpu.VMEM(s, t) for s, t in scratch] + ([pltpu.SemaphoreType.DMA((copies,))] if copies else []),
        input_output_aliases=aliases,
        compiler_params=pltpu.CompilerParams(vmem_limit_bytes=mib * 2**20),
        cost_estimate=pl.CostEstimate(flops=flops, bytes_accessed=moved, transcendentals=0),
        name=name,
    )(*args)


def latitude_cos(rows, nrows):
    degree = -60.0 + 120.0 * (rows.astype(F32) + 0.5) / nrows
    return jnp.cos(degree * (jnp.pi / 180.0))


def shards(sea_heat_deviations, missing_date_bitmask, ocean_binary_mask, mode_maps, mode_series):
    rows, columns, days = sea_heat_deviations.shape
    modes, words = (mode_maps.shape[0], missing_date_bitmask.shape[2])
    nlat = rows * lax.axis_size("lat")
    total = float(modes * nlat * columns * lax.axis_size("lon"))
    own, reach = (rows * columns, SWEEPS * STEPS)
    sides = 2 * rows * reach
    cells = own + sides
    assert columns == LANES and sides == LANES and rows == SWEEPS and days == BITS * words
    chunk = days // 5
    row0 = lax.axis_index("lat") * rows
    here = lax.axis_index("lon")
    place = jnp.stack([row0, jnp.int32(nlat), lax.axis_index("lat") % 2, here]).astype(jnp.int32)
    tall = row0 - rows + jnp.arange(6 * rows) // 2
    cos_tall = latitude_cos(tall, nlat)[:, None]
    klon = jnp.broadcast_to(KLON / (cos_tall * cos_tall), (6 * rows, 2 * LANES))
    cosl = jnp.broadcast_to(cos_tall[2 * rows : 4 * rows], (2 * rows, 2 * LANES))

    words_per = words // LANES
    flags_scratch = [((2 * LANES, days // words_per), BF16), ((1, days // words_per), jnp.int32)]
    edge = ((modes + 8 + rows * reach * words_per, LANES), F32)
    inputs = [missing_date_bitmask.reshape(own, words), ocean_binary_mask, sea_heat_deviations.reshape(own, days)]
    inputs += [mode_maps, mode_series]
    place, klon, cosl = lax.optimization_barrier((place, klon, cosl))
    m, a, held, u, row, near, far, maps_out, series_out = call(
        functools.partial(own_flags_kernel, reach),
        "own_flags",
        [((own, days), BF16), ((own, days), BF16), ((own, words), jnp.int32)]
        + [((modes, own), F32), ((1, own), F32), edge, edge]
        + [(mode_maps.shape, F32), (mode_series.shape, F32)],
        [((own, words), jnp.int32), ((rows, LANES), jnp.int32), ((own, days), BF16)]
        + [(mode_maps.shape, F32), (mode_series.shape, F32), *flags_scratch],
        [*inputs, place],
        smem=(5,),
        in_hbm=range(5),
        out_hbm=(7, 8),
        copies=6 + rows,
        flops=4 * LANES * own * days,
    )
    if lax.axis_size("lon") == 8:
        pieces = [swap(mode_series, 0, b | 1) for b in (2, 4, 6)]
        *pieces, m, a = lax.optimization_barrier((*pieces, m, a))
        pieces = [z for piece in pieces for z in (swap(piece, 0, 1), piece)]
        pieces = [mode_series, swap(mode_series, 0, 1), *pieces]
    else:
        pieces = [lax.all_gather(mode_series, "lon", axis=1, tiled=True)]
    near, far = lon_partners(near, far)
    xv, near_xv, far_xv = call(
        functools.partial(given_kernel, rows, reach),
        "given",
        [((PAIRS, own), F32), ((PAIRS, LANES), F32), ((PAIRS, LANES), F32)],
        [((PAIRS, days), F32)],
        [a, place, *pieces],
        smem=(1,),
        light=True,
    )
    near_xv, far_xv = lon_partners(near_xv, far_xv)
    base, inverse, v, m_halo, u, row, spread = call(
        functools.partial(first_products_kernel, chunk),
        "first_products",
        [((2, cells), F32), ((8, LANES), F32), ((modes, days), F32), ((days, sides), BF16), ((modes, cells), F32), ((1, cells), F32)]
        + [((days // words_per, 2 * LANES), BF16)],
        [],
        [near, far, place, m, u, row, *pieces],
        smem=(2,),
        flops=8 * modes * cells * days,
    )

    (m_days,) = call(
        days_flags_kernel,
        "days_flags",
        [((days, own), BF16)],
        [],
        [held, spread],
        flops=4 * LANES * own * days,
    )

    count = 2 * rows
    summed = block = None
    coefs = []
    for step in range(STEPS):
        if step == 0:
            fresh, xv_halo = call(
                functools.partial(first_fields_kernel, rows, reach),
                "fields_0",
                [((2 * count, 2 * LANES), F32), ((PAIRS, sides), F32)],
                [],
                [near_xv, far_xv, place, inverse, u, row, xv, base],
                smem=(2,),
            )
        else:
            fresh, v, u = call(
                functools.partial(fields_kernel, step, rows, reach, total),
                f"fields_{step}",
                [((count, 2 * LANES), F32), ((modes, days), F32), ((modes, cells), F32)],
                [],
                [m_days, m_halo, v, u, row, xv, xv_halo, base, inverse, summed, block],
                flops=8 * modes * cells * days,
                aliases={2: 1, 3: 2},
            )
        got_a, got_b = lat_partners(fresh)
        outs = [((2, days + 2 * LANES), F32), ((count, 2 * LANES), F32)]
        coef = ((5 * 3 * count, 2 * LANES), F32)
        partial_sums, block, *made = call(
            functools.partial(sums_kernel, step, rows, chunk),
            f"sums_{step}",
            outs if step else [*outs, coef],
            [],
            [m, a, v, u, place, klon, cosl, fresh, got_a, got_b, *coefs],
            smem=(4,),
            flops=8 * modes * own * days,
        )
        coefs = coefs or made
        if step + 1 < STEPS:
            base, inverse = call(
                functools.partial(next_products_kernel, step + 1, chunk),
                f"next_products_{step + 1}",
                [((2, cells), F32), ((8, LANES), F32)],
                [],
                [m_days, m_halo, v, u],
                flops=8 * modes * cells * days,
            )
        summed = sum_all(partial_sums)
    return call(
        functools.partial(last_kernel, rows, reach, total),
        "last",
        [(mode_maps.shape, F32), (mode_series.shape, F32)],
        [((PAIRS, rows, columns), F32), ((PAIRS, mode_series.shape[1]), F32)],
        [v, u, summed, block, place, maps_out, series_out],
        smem=(4,),
        in_hbm=(5, 6),
        out_hbm=(0, 1),
        copies=2,
        aliases={5: 0, 6: 1},
    )


def solution(mesh):
    in_specs = (
        P("lat", "lon", None),
        P("lat", "lon", None),
        P("lat", "lon"),
        P(None, "lat", "lon"),
        P(None, "lon"),
    )
    out_specs = (P(None, "lat", "lon"), P(None, "lon"))
    return jax.shard_map(shards, mesh=mesh, in_specs=in_specs, out_specs=out_specs, check_vma=False)
```

```python
import functools

import jax
import jax.numpy as jnp
from jax import lax
from jax.experimental import pallas as pl
from jax.experimental.pallas import tpu as pltpu
from jax.sharding import PartitionSpec as P

STEPS = 4
SWEEPS = 4
PAIRS = 2 * STEPS
BITS = 15
LANES = 128

KLAT = 0.2
KLON = 0.05
EPS = 1e-06
F32 = jnp.float32
BF16 = jnp.bfloat16
VMEM = pl.BlockSpec(memory_space=pltpu.VMEM)
SMEM = pl.BlockSpec(memory_space=pltpu.SMEM)
NT = (((1,), (1,)), ((), ()))


def pairing(lat_map, lon_map):
    nlat, nlon = (lax.axis_size("lat"), lax.axis_size("lon"))
    return [(i * nlon + j, lat_map(i) * nlon + lon_map(j)) for i in range(nlat) for j in range(nlon)]


def swap(x, lat_bits, lon_bits):
    return lax.ppermute(x, ("lat", "lon"), pairing(lambda i: i ^ lat_bits, lambda j: j ^ lon_bits))


def sum_all(x):
    nlat, nlon = (lax.axis_size("lat"), lax.axis_size("lon"))
    if nlat & (nlat - 1) or nlon & (nlon - 1):
        return lax.psum(x, ("lat", "lon"))
    core = 1 if nlon > 1 else 0
    if core:
        x = x + swap(x, 0, core)
    for size, first, on_lat in ((nlat, 1, True), (nlon, 2, False)):
        bit = first
        while bit < size:
            bits = lambda b: (b, core) if on_lat else (0, b | core)
            if 2 * bit < size:
                near, far, both = (swap(x, *bits(b)) for b in (bit, 2 * bit, 3 * bit))
                x = (x + near) + (far + both) if on_lat else (x + near) + (both + far)
                bit *= 4
            else:
                x = x + swap(x, *bits(bit))
                bit *= 2
    return x


def lat_partners(x):
    count = lax.axis_size("lat")
    same = lambda j: j
    got_a = lax.ppermute(x, ("lat", "lon"), pairing(lambda i: i ^ 1, same))
    got_b = lax.ppermute(x, ("lat", "lon"), pairing(lambda i: (i + 1 if i % 2 else i - 1) % count, same))
    return got_a, got_b


def lon_partners(near, far):
    count = lax.axis_size("lon")
    same = lambda i: i
    got_far = lax.ppermute(far, ("lat", "lon"), pairing(same, lambda j: (j + 1 if j % 2 else j - 1) % count))
    return swap(near, 0, 1), got_far


def split(x):
    high = x.astype(BF16)
    return high, (x - high.astype(F32)).astype(BF16)


def solve_pair(g00, g01, g10, g11, right0, right1):
    determ = g00 * g11 - g01 * g10
    return (g11 * right0 - g01 * right1) / determ, (g00 * right1 - g10 * right0) / determ


def total_of(x):
    return jnp.sum(x, axis=1, keepdims=True)


def lane_ids(shape):
    return lax.broadcasted_iota(jnp.int32, shape, 1)


def to_block(field, rows, reach):
    n, own = (field.shape[0], rows * LANES)
    halo = field[:, own:]
    lane = lane_ids((n, LANES))
    parts = []
    for r in range(rows):
        east = pltpu.roll(halo, (LANES - rows * reach - reach * r) % LANES, 1)
        west = pltpu.roll(halo, (LANES - reach - reach * r) % LANES, 1)
        edge = jnp.where(lane < LANES // 2, east, west)
        parts.append(jnp.concatenate([field[:, r * LANES : (r + 1) * LANES], edge], axis=1))
    return jnp.concatenate(parts, axis=0)


def from_block(block, rows, reach):
    n = block.shape[0] // rows
    lane = lane_ids((n, LANES))
    halo = jnp.zeros((n, LANES), F32)
    own = []
    for r in range(rows):
        part = block[r * n : (r + 1) * n]
        own.append(part[:, :LANES])
        edge = part[:, LANES:]
        east = pltpu.roll(edge, (rows * reach + reach * r) % LANES, 1)
        west = pltpu.roll(edge, (reach * r + reach) % LANES, 1)
        first = reach * r
        halo = jnp.where((lane >= first) & (lane < first + reach), west, halo)
        first = rows * reach + reach * r
        halo = jnp.where((lane >= first) & (lane < first + reach), east, halo)
    return jnp.concatenate(own + [halo], axis=1)


def unpack_words(words, spread_ref, bit_ref):
    top = ((words >> 8) << 8).astype(F32).astype(BF16)
    bottom = (words & 255).astype(F32).astype(BF16)
    spread = spread_ref[...]
    each = jnp.dot(jnp.concatenate([top, bottom], axis=1), spread, preferred_element_type=F32).astype(jnp.int32)
    return jnp.where((each & bit_ref[...]) == 0, 1.0, 0.0).astype(BF16)


def fill_spread(spread_ref, bit_ref):
    days = spread_ref.shape[1]
    word = lax.broadcasted_iota(jnp.int32, (LANES, days), 0)
    rest = lane_ids((LANES, days)) - BITS * word
    hit = jnp.where((rest >= 0) & (rest < BITS), 1.0, 0.0).astype(BF16)
    spread_ref[:LANES] = hit
    spread_ref[LANES:] = hit
    word = jnp.where((rest >= 0) & (rest < BITS), rest, 0)
    bit_ref[...] = jnp.left_shift(1, jnp.sum(word, axis=0, keepdims=True))


def fill_spread_days(spread_ref):
    days = spread_ref.shape[0]
    rest = lax.broadcasted_iota(jnp.int32, (days, LANES), 0) - BITS * lane_ids((days, LANES))
    hit = jnp.where((rest >= 0) & (rest < BITS), 1.0, 0.0).astype(BF16)
    spread_ref[:, :LANES] = hit
    spread_ref[:, LANES:] = hit


def unpack_days(words, spread_ref, m_ref):
    days = spread_ref.shape[0]
    step = days // 5
    for g in range(words.shape[1] // LANES):
        group = words[:, g * LANES : (g + 1) * LANES]
        top = ((group >> 8) << 8).astype(F32).astype(BF16)
        bottom = (group & 255).astype(F32).astype(BF16)
        both = jnp.concatenate([top, bottom], axis=1)
        for first in range(0, days, step):
            each = lax.dot_general(spread_ref[first : first + step], both, NT, preferred_element_type=F32).astype(jnp.int32)
            day = first + lax.broadcasted_iota(jnp.int32, (step, LANES), 0)
            bit = jnp.left_shift(1, day - BITS * ((day * 34953) >> 19))
            for c in range(0, each.shape[1], LANES):
                flags = jnp.where((each[:, c : c + LANES] & bit) == 0, 1.0, 0.0).astype(BF16)
                m_ref[g * days + first : g * days + first + step, c : c + LANES] = flags


def as_column(row):
    return jnp.transpose(jnp.broadcast_to(row, (8, LANES)))[:, :1]


def own_flags_kernel(reach, *refs):
    words_hbm, coast_hbm, x_hbm, maps_hbm, series_hbm, place_ref = refs[:6]
    m_ref, a_ref, held_ref, u_ref, row_ref, near_ref, far_ref, maps_out, series_out = refs[6:15]
    words_ref, coast_ref, x_ref, maps_ref, series_ref, spread_ref, bit_ref, sems = refs[15:]
    rows = coast_ref.shape[0]
    loads = [
        pltpu.make_async_copy(words_hbm, words_ref, sems.at[0]),
        pltpu.make_async_copy(coast_hbm, coast_ref, sems.at[1]),
    ]
    for r in range(rows):
        at = pl.ds(r * LANES, LANES)
        loads.append(pltpu.make_async_copy(x_hbm.at[at], x_ref.at[at], sems.at[2 + r]))
    loads.append(pltpu.make_async_copy(maps_hbm, maps_ref, sems.at[2 + rows]))
    loads.append(pltpu.make_async_copy(series_hbm, series_ref, sems.at[3 + rows]))
    stores = [
        pltpu.make_async_copy(maps_ref, maps_out, sems.at[4 + rows]),
        pltpu.make_async_copy(series_ref, series_out, sems.at[5 + rows]),
    ]
    for load in loads:
        load.start()
    fill_spread(spread_ref, bit_ref)
    loads[0].wait()
    loads[1].wait()
    for load, store in zip(loads[-2:], stores, strict=True):
        load.wait()
        store.start()
    days = spread_ref.shape[1]
    coast_own = coast_ref[...].astype(F32)
    coasts = jnp.transpose(jnp.concatenate([coast_own] * (8 // rows), axis=0))
    for r in range(rows):
        coast = coasts[:, r : r + 1]
        ocean = coast.astype(BF16)
        coast = coast.astype(jnp.int32)
        loads[2 + r].wait()
        cell = slice(r * LANES, (r + 1) * LANES)
        for g in range(words_ref.shape[1] // LANES):
            words = words_ref[cell, g * LANES : (g + 1) * LANES] * coast
            held_ref[cell, g * LANES : (g + 1) * LANES] = words
            given = unpack_words(words, spread_ref, bit_ref)
            at = slice(g * days, (g + 1) * days)
            m_ref[cell, at] = given
            a_ref[cell, at] = x_ref[cell, at] * given * ocean
    modes = maps_ref.shape[0]
    pieces = []
    for r in range(rows):
        at = slice(r * LANES, (r + 1) * LANES)
        u = maps_ref[:, r, :]
        u_ref[:, at] = u
        row_ref[:, at] = coast_own[r : r + 1]
        pieces.append(jnp.concatenate([u, jnp.broadcast_to(coast_own[r : r + 1], (8, LANES))], axis=0))
    base = modes + 8
    odd = place_ref[3] % 2 == 1
    west, east = edges(pieces, reach)
    near_ref[:base] = jnp.where(odd, west, east)
    far_ref[:base] = jnp.where(odd, east, west)
    for g in range(words_ref.shape[1] // LANES):
        for r in range(rows):
            at = slice(base + reach * (rows * g + r), base + reach * (rows * g + r + 1))
            group = slice(g * LANES, (g + 1) * LANES)
            west = words_ref[r * LANES : r * LANES + reach, group].astype(F32)
            east = words_ref[(r + 1) * LANES - reach : (r + 1) * LANES, group].astype(F32)
            near_ref[at] = jnp.where(odd, west, east)
            far_ref[at] = jnp.where(odd, east, west)
    for store in stores:
        store.wait()


def edges(pieces, reach):
    rows = len(pieces)
    shape = pieces[0].shape
    lane = lane_ids(shape)
    west = jnp.zeros(shape, F32)
    east = west
    for r, part in enumerate(pieces):
        first = rows * reach + reach * r
        west = jnp.where((lane >= first) & (lane < first + reach), pltpu.roll(part, first % LANES, 1), west)
        first = reach * r
        east = jnp.where((lane >= first) & (lane < first + reach), pltpu.roll(part, (first + reach) % LANES, 1), east)
    return west, east


def in_order(pieces, here):
    bit = 1
    while bit < len(pieces):
        turn = (here // bit) % 2 == 1
        pieces = [jnp.where(turn, pieces[i ^ bit], pieces[i]) for i in range(len(pieces))]
        bit *= 2
    return pieces


def given_kernel(rows, reach, *refs):
    a_ref, place_ref = refs[:2]
    xv_ref, near_ref, far_ref, v_ref = refs[-4:]
    here = place_ref[3]
    share = refs[2].shape[1]
    for i, piece in enumerate(in_order([ref[:PAIRS] for ref in refs[2:-4]], here)):
        v_ref[:, i * share : (i + 1) * share] = piece
    high, low = split(v_ref[...])
    both = lax.dot_general(jnp.concatenate([high, low], axis=0), a_ref[...], NT, preferred_element_type=F32)
    xv = both[:PAIRS] + both[PAIRS:]
    xv_ref[...] = xv
    west, east = edges([xv[:, r * LANES : (r + 1) * LANES] for r in range(rows)], reach)
    odd = here % 2 == 1
    near_ref[...] = jnp.where(odd, west, east)
    far_ref[...] = jnp.where(odd, east, west)


def masked_products(vs, u, low, chunk, m_ref, by_day=True):
    modes, days = vs.shape
    acc = None
    for first in range(0, days, chunk):
        at = slice(first, first + chunk)
        v = vs[:, at]
        high, lower = split(jnp.concatenate([v * v[j : j + 1] for j in (low, low + 1)], axis=0))
        left = jnp.concatenate([high, lower], axis=0)
        if by_day:
            part = jnp.dot(left, m_ref[at], preferred_element_type=F32)
        else:
            part = lax.dot_general(left, m_ref[:, at], NT, preferred_element_type=F32)
        acc = part if acc is None else acc + part
    acc = acc[: 2 * modes] + acc[2 * modes :]
    return jnp.concatenate(
        [jnp.sum(u * acc[j * modes : (j + 1) * modes], axis=0, keepdims=True) for j in range(2)], axis=0
    )


def first_products_kernel(chunk, *refs):
    near_ref, far_ref, place_ref, m_ref, u_own_ref, row_own_ref = refs[:6]
    base_ref, inv_ref, v_ref, mh_ref, u_ref, row_ref, spread_ref = refs[-7:]
    fill_spread_days(spread_ref)
    share = refs[6].shape[1]
    for i, piece in enumerate(in_order([ref[...] for ref in refs[6:-7]], place_ref[3])):
        v_ref[:, i * share : (i + 1) * share] = piece
    odd = place_ref[3] % 2 == 1
    west = jnp.where(odd, near_ref[...], far_ref[...])
    east = jnp.where(odd, far_ref[...], near_ref[...])
    modes, own = u_own_ref.shape
    base = modes + 8
    lane = lane_ids((base, LANES))
    fields = jnp.where(lane < LANES // 2, west[:base], east[:base])
    u_own, u_halo, row_halo = (u_own_ref[...], fields[:modes], fields[modes : modes + 1])
    u_ref[:, :own] = u_own
    u_ref[:, own:] = u_halo
    row_ref[:, :own] = row_own_ref[...]
    row_ref[:, own:] = row_halo
    coast = as_column(row_halo).astype(jnp.int32)
    half = LANES // 2
    groups = [slice(base + half * g, base + half * (g + 1)) for g in range((west.shape[0] - base) // half)]
    words = jnp.concatenate([jnp.concatenate([west[at], east[at]], axis=0) for at in groups], axis=1)
    unpack_days(words.astype(jnp.int32) * coast, spread_ref, mh_ref)
    base_ref[:, :own] = masked_products(v_ref, u_own, 0, chunk, m_ref, by_day=False)
    base_ref[:, own:] = masked_products(v_ref, u_halo, 0, chunk, mh_ref)
    inv_ref[...] = inverse_rows(v_ref[:2])


def days_flags_kernel(held_ref, spread_ref, m_ref):
    unpack_days(held_ref[...], spread_ref, m_ref)


def inverse_rows(pair):
    v0, v1 = (pair[0:1], pair[1:2])
    h00, h01, h11 = (total_of(v0 * v0), total_of(v0 * v1), total_of(v1 * v1))
    determ = h00 * h11 - h01 * h01
    rows = [h11 / determ, h01 / determ, h00 / determ]
    rows = [jnp.broadcast_to(z, (1, LANES)) for z in rows]
    return jnp.concatenate(rows + [jnp.zeros((5, LANES), F32)], axis=0)


def along(row, length):
    return jnp.concatenate([row] * (length // LANES), axis=1)


def next_products_kernel(step, chunk, m_ref, mh_ref, v_ref, u_ref, base_ref, inv_ref):
    low = 2 * step
    own = m_ref.shape[1]
    mode = lax.broadcasted_iota(jnp.int32, u_ref.shape, 0)
    u = jnp.where((mode >= low - 2) & (mode < low), 0.0, u_ref[...])
    base_ref[:, :own] = masked_products(v_ref, u[:, :own], low, chunk, m_ref)
    base_ref[:, own:] = masked_products(v_ref, u[:, own:], low, chunk, mh_ref)
    inv_ref[...] = inverse_rows(v_ref[low : low + 2])


def masked_rows(first, second, m_ref, mh_ref):
    high, lower = split(jnp.concatenate([first * second[0:1], first * second[1:2]], axis=0))
    left = jnp.concatenate([high, lower], axis=0)
    acc = jnp.concatenate(
        [
            jnp.dot(left, m_ref[...], preferred_element_type=F32),
            jnp.dot(left, mh_ref[...], preferred_element_type=F32),
        ],
        axis=1,
    )
    return acc[:4] + acc[4:]


def new_fields(inv_ref, u_pair, coast, proj):
    first, other, last = (along(inv_ref[i : i + 1], proj.shape[1]) for i in range(3))
    p0, p1 = (proj[0:1], proj[1:2])
    return coast * (u_pair + jnp.concatenate([first * p0 - other * p1, last * p1 - other * p0], axis=0))


def first_fields_kernel(rows, reach, near_ref, far_ref, place_ref, inv_ref, u_ref, row_ref, xv_ref, base_ref, w_ref, xh_ref):
    odd = place_ref[3] % 2 == 1
    west = jnp.where(odd, near_ref[...], far_ref[...])
    east = jnp.where(odd, far_ref[...], near_ref[...])
    xh = jnp.where(lane_ids((PAIRS, LANES)) < LANES // 2, west, east)
    xh_ref[...] = xh
    proj = jnp.concatenate([xv_ref[:2], xh[:2]], axis=1) - base_ref[...]
    coast = row_ref[...]
    count = 2 * rows
    w_ref[:count] = to_block(new_fields(inv_ref, u_ref[:2], coast, proj), rows, reach)
    w_ref[count:] = to_block(jnp.concatenate([coast, coast], axis=0), rows, reach)


def fields_kernel(step, rows, reach, total, *refs):
    m_ref, mh_ref, v_ref, u_ref, row_ref, xv_ref, xh_ref, base_ref, inv_ref, sum_ref, block_ref, w_ref, v_out, u_out = refs
    low = 2 * step
    days = v_ref.shape[1]
    sums = sum_ref[:, :days]
    masked = masked_rows(sums, v_ref[low : low + 2], m_ref, mh_ref)
    mixes, norms = mixing(total, sum_ref)
    un = new_units(rows, reach, norms, block_ref)
    cells = un.shape[1]
    mixes = [[along(z, cells) for z in mix] for mix in mixes]
    changed = []
    for j in range(2):
        p0, p1 = (masked[2 * j : 2 * j + 1], masked[2 * j + 1 : 2 * j + 2])
        changed.append(sum(un[k : k + 1] * (mixes[k][0] * p0 + mixes[k][1] * p1) for k in range(2)))
    given = jnp.concatenate([xv_ref[low : low + 2], xh_ref[low : low + 2]], axis=1)
    proj = given - base_ref[...] - jnp.concatenate(changed, axis=0)
    w_ref[...] = to_block(new_fields(inv_ref, u_ref[low : low + 2], row_ref[...], proj), rows, reach)
    v_out[low - 2 : low] = new_series(total, sum_ref)
    u_out[low - 2 : low] = un


def mixing(total, sum_ref):
    days = sum_ref.shape[1] - 2 * LANES
    g00, g01 = (sum_ref[0:1, days : days + LANES], sum_ref[0:1, days + LANES :])
    g11 = sum_ref[1:2, days + LANES :]
    n0, n1 = (jnp.sqrt(g00 / total + EPS), jnp.sqrt(g11 / total + EPS))
    g00, g01, g11 = (g00 / (n0 * n0), g01 / (n0 * n1), g11 / (n1 * n1))
    determ = g00 * g11 - g01 * g01
    cross = g01 / determ
    return [[g11 / determ / n0, -(cross / n1)], [-(cross / n0), g00 / determ / n1]], (n0, n1)


def new_series(total, sum_ref):
    days = sum_ref.shape[1] - 2 * LANES
    p0, p1 = (sum_ref[0:1, :days], sum_ref[1:2, :days])
    mixes, _ = mixing(total, sum_ref)
    return jnp.concatenate([along(mix[0], days) * p0 + along(mix[1], days) * p1 for mix in mixes], axis=0)


def new_units(rows, reach, norms, block_ref):
    field = from_block(block_ref[...], rows, reach)
    return jnp.concatenate([field[k : k + 1] / along(norms[k], field.shape[1]) for k in range(2)], axis=0)


def sums_kernel(step, rows, chunk, *refs):
    m_ref, a_ref, v_ref, u_ref, place_ref, klon_ref, cosl_ref, w_ref, ga_ref, gb_ref = refs[:10]
    refs = refs[10:]
    if step:
        coef_ref, sum_ref, block_ref = refs
    else:
        sum_ref, block_ref, coef_ref = refs
    days = v_ref.shape[1]
    low = 2 * step
    own = rows * LANES
    count = 2 * rows
    row0, nlat, odd = (place_ref[0], place_ref[1], place_ref[2])

    def assemble(mid, a, b):
        is_odd = odd == 1
        return jnp.concatenate([jnp.where(is_odd, a, b), mid, jnp.where(is_odd, b, a)], axis=0)

    w = assemble(w_ref[:count], ga_ref[:count], gb_ref[:count])
    tall = 3 * count
    north = lambda z: pltpu.roll(z, 2, 0)
    south = lambda z: pltpu.roll(z, tall - 2, 0)
    west = lambda z: pltpu.roll(z, 1, 1)
    east = lambda z: pltpu.roll(z, 2 * LANES - 1, 1)
    if step == 0:
        coast = assemble(w_ref[count:], ga_ref[count:], gb_ref[count:])
        row = row0 - rows + lax.broadcasted_iota(jnp.int32, (tall, 2 * LANES), 0) // 2
        coast = jnp.where((row >= 0) & (row < nlat), coast, 0.0)
        klon = klon_ref[...] * coast
        klat = KLAT * coast
        parts = [klat * north(coast), klat * south(coast), klon * west(coast), klon * east(coast)]
        parts.append(1.0 - ((parts[0] + parts[1]) + (parts[2] + parts[3])))
        for i, part in enumerate(parts):
            coef_ref[i * tall : (i + 1) * tall] = part
    an, as_, aw, ae, stay = (coef_ref[i * tall : (i + 1) * tall] for i in range(5))
    for _ in range(SWEEPS):
        w = stay * w + (an * north(w) + as_ * south(w)) + (aw * west(w) + ae * east(w))
    block = w[count : 2 * count]
    block_ref[...] = block
    cells = lambda z: jnp.concatenate([z[2 * r : 2 * r + 2, :LANES] for r in range(rows)], axis=1)
    fresh = cells(block)
    weighted = cells(block * cosl_ref[...])
    u = u_ref[:, :own]
    modes = u.shape[0]
    high, lower = split(jnp.concatenate([u * weighted[0:1], u * weighted[1:2]], axis=0))
    left = jnp.concatenate([high, lower], axis=0)
    high, lower = split(weighted)
    left_a = jnp.concatenate([high, lower], axis=0)
    for j in range(2):
        for i in range(2):
            gram = total_of(weighted[j : j + 1] * fresh[i : i + 1])
            sum_ref[j : j + 1, days + i * LANES : days + (i + 1) * LANES] = jnp.broadcast_to(gram, (1, LANES))
    old = [[total_of(weighted[j : j + 1] * u[low + i : low + i + 1]) for i in range(2)] for j in range(2)]
    for first in range(0, days, chunk):
        at = slice(first, first + chunk)
        masked = jnp.dot(left, m_ref[:, at], preferred_element_type=F32)
        given = jnp.dot(left_a, a_ref[:, at], preferred_element_type=F32)
        v = v_ref[:, at]
        for j in range(2):
            part = masked[j * modes : (j + 1) * modes] + masked[(2 + j) * modes : (3 + j) * modes]
            sum_ref[j : j + 1, at] = (
                given[j : j + 1]
                + given[2 + j : 3 + j]
                - jnp.sum(v * part, axis=0, keepdims=True)
                + old[j][0] * v[low : low + 1]
                + old[j][1] * v[low + 1 : low + 2]
            )


def last_kernel(rows, reach, total, *refs):
    v_ref, u_ref, sum_ref, block_ref, place_ref = refs[:5]
    maps_out, series_out, maps_new, series_new, held_ref, sems = refs[7:]
    share = series_new.shape[1]
    stores = [
        pltpu.make_async_copy(maps_new, maps_out.at[pl.ds(0, PAIRS)], sems.at[0]),
        pltpu.make_async_copy(series_new, series_out.at[pl.ds(0, PAIRS)], sems.at[1]),
    ]
    un = new_units(rows, reach, mixing(total, sum_ref)[1], block_ref)
    vn = new_series(total, sum_ref)
    u = jnp.concatenate([u_ref[: PAIRS - 2], un], axis=0)
    for r in range(rows):
        maps_new[:, r, :] = u[:, r * LANES : (r + 1) * LANES]
    stores[0].start()
    days = v_ref.shape[1]
    held_ref[: PAIRS - 2, :days] = v_ref[: PAIRS - 2]
    held_ref[PAIRS - 2 :, :days] = vn
    start = place_ref[3] * share
    tile = start // LANES
    width = held_ref.shape[1] - days + (share // LANES) * LANES
    window = held_ref[:, pl.ds(pl.multiple_of(tile * LANES, LANES), width)]
    series_new[...] = pltpu.roll(window, (width - (start - tile * LANES)) % width, 1)[:, :share]
    stores[1].start()
    for store in stores:
        store.wait()


def call(kernel, name, outs, scratch, args, smem=(), mib=24, flops=0, copies=0, in_hbm=(), out_hbm=(), aliases={}, light=False):
    moved = 0 if light else sum(z.size * z.dtype.itemsize for z in args)
    hbm = pl.BlockSpec(memory_space=pl.ANY)
    args = [pltpu.with_memory_space_constraint(z, pltpu.HBM) if i in in_hbm else z for i, z in enumerate(args)]
    return pl.pallas_call(
        kernel,
        out_shape=[jax.ShapeDtypeStruct(s, t) for s, t in outs],
        in_specs=[SMEM if i in smem else hbm if i in in_hbm else VMEM for i in range(len(args))],
        out_specs=[hbm if i in out_hbm else VMEM for i in range(len(outs))],
        scratch_shapes=[pltpu.VMEM(s, t) for s, t in scratch] + ([pltpu.SemaphoreType.DMA((copies,))] if copies else []),
        input_output_aliases=aliases,
        compiler_params=pltpu.CompilerParams(vmem_limit_bytes=mib * 2**20),
        cost_estimate=pl.CostEstimate(flops=flops, bytes_accessed=moved, transcendentals=0),
        name=name,
    )(*args)


def latitude_cos(rows, nrows):
    degree = -60.0 + 120.0 * (rows.astype(F32) + 0.5) / nrows
    return jnp.cos(degree * (jnp.pi / 180.0))


def shards(sea_heat_deviations, missing_date_bitmask, ocean_binary_mask, mode_maps, mode_series):
    rows, columns, days = sea_heat_deviations.shape
    modes, words = (mode_maps.shape[0], missing_date_bitmask.shape[2])
    nlat = rows * lax.axis_size("lat")
    total = float(modes * nlat * columns * lax.axis_size("lon"))
    own, reach = (rows * columns, SWEEPS * STEPS)
    sides = 2 * rows * reach
    cells = own + sides
    assert columns == LANES and sides == LANES and rows == SWEEPS and days == BITS * words
    chunk = days // 5
    row0 = lax.axis_index("lat") * rows
    here = lax.axis_index("lon")
    place = jnp.stack([row0, jnp.int32(nlat), lax.axis_index("lat") % 2, here]).astype(jnp.int32)
    tall = row0 - rows + jnp.arange(6 * rows) // 2
    cos_tall = latitude_cos(tall, nlat)[:, None]
    klon = jnp.broadcast_to(KLON / (cos_tall * cos_tall), (6 * rows, 2 * LANES))
    cosl = jnp.broadcast_to(cos_tall[2 * rows : 4 * rows], (2 * rows, 2 * LANES))

    words_per = words // LANES
    flags_scratch = [((2 * LANES, days // words_per), BF16), ((1, days // words_per), jnp.int32)]
    edge = ((modes + 8 + rows * reach * words_per, LANES), F32)
    inputs = [missing_date_bitmask.reshape(own, words), ocean_binary_mask, sea_heat_deviations.reshape(own, days)]
    inputs += [mode_maps, mode_series]
    place, klon, cosl = lax.optimization_barrier((place, klon, cosl))
    m, a, held, u, row, near, far, maps_out, series_out = call(
        functools.partial(own_flags_kernel, reach),
        "own_flags",
        [((own, days), BF16), ((own, days), BF16), ((own, words), jnp.int32)]
        + [((modes, own), F32), ((1, own), F32), edge, edge]
        + [(mode_maps.shape, F32), (mode_series.shape, F32)],
        [((own, words), jnp.int32), ((rows, LANES), jnp.int32), ((own, days), BF16)]
        + [(mode_maps.shape, F32), (mode_series.shape, F32), *flags_scratch],
        [*inputs, place],
        smem=(5,),
        in_hbm=range(5),
        out_hbm=(7, 8),
        copies=6 + rows,
        flops=4 * LANES * own * days,
    )
    if lax.axis_size("lon") == 8:
        pieces = [swap(mode_series, 0, b | 1) for b in (2, 4, 6)]
        *pieces, m, a = lax.optimization_barrier((*pieces, m, a))
        pieces = [z for piece in pieces for z in (swap(piece, 0, 1), piece)]
        pieces = [mode_series, swap(mode_series, 0, 1), *pieces]
    else:
        pieces = [lax.all_gather(mode_series, "lon", axis=1, tiled=True)]
    near, far = lon_partners(near, far)
    xv, near_xv, far_xv = call(
        functools.partial(given_kernel, rows, reach),
        "given",
        [((PAIRS, own), F32), ((PAIRS, LANES), F32), ((PAIRS, LANES), F32)],
        [((PAIRS, days), F32)],
        [a, place, *pieces],
        smem=(1,),
        light=True,
    )
    near_xv, far_xv = lon_partners(near_xv, far_xv)
    base, inverse, v, m_halo, u, row, spread = call(
        functools.partial(first_products_kernel, chunk),
        "first_products",
        [((2, cells), F32), ((8, LANES), F32), ((modes, days), F32), ((days, sides), BF16), ((modes, cells), F32), ((1, cells), F32)]
        + [((days // words_per, 2 * LANES), BF16)],
        [],
        [near, far, place, m, u, row, *pieces],
        smem=(2,),
        flops=8 * modes * cells * days,
    )

    (m_days,) = call(
        days_flags_kernel,
        "days_flags",
        [((days, own), BF16)],
        [],
        [held, spread],
        flops=4 * LANES * own * days,
    )

    count = 2 * rows
    summed = block = None
    coefs = []
    for step in range(STEPS):
        if step == 0:
            fresh, xv_halo = call(
                functools.partial(first_fields_kernel, rows, reach),
                "fields_0",
                [((2 * count, 2 * LANES), F32), ((PAIRS, sides), F32)],
                [],
                [near_xv, far_xv, place, inverse, u, row, xv, base],
                smem=(2,),
            )
        else:
            fresh, v, u = call(
                functools.partial(fields_kernel, step, rows, reach, total),
                f"fields_{step}",
                [((count, 2 * LANES), F32), ((modes, days), F32), ((modes, cells), F32)],
                [],
                [m_days, m_halo, v, u, row, xv, xv_halo, base, inverse, summed, block],
                flops=8 * modes * cells * days,
                aliases={2: 1, 3: 2},
            )
        got_a, got_b = lat_partners(fresh)
        outs = [((2, days + 2 * LANES), F32), ((count, 2 * LANES), F32)]
        coef = ((5 * 3 * count, 2 * LANES), F32)
        partial_sums, block, *made = call(
            functools.partial(sums_kernel, step, rows, chunk),
            f"sums_{step}",
            outs if step else [*outs, coef],
            [],
            [m, a, v, u, place, klon, cosl, fresh, got_a, got_b, *coefs],
            smem=(4,),
            flops=8 * modes * own * days,
        )
        coefs = coefs or made
        if step + 1 < STEPS:
            base, inverse = call(
                functools.partial(next_products_kernel, step + 1, chunk),
                f"next_products_{step + 1}",
                [((2, cells), F32), ((8, LANES), F32)],
                [],
                [m_days, m_halo, v, u],
                flops=8 * modes * cells * days,
            )
        summed = sum_all(partial_sums)
    return call(
        functools.partial(last_kernel, rows, reach, total),
        "last",
        [(mode_maps.shape, F32), (mode_series.shape, F32)],
        [((PAIRS, rows, columns), F32), ((PAIRS, mode_series.shape[1]), F32), ((PAIRS, days + 2 * LANES), F32)],
        [v, u, summed, block, place, maps_out, series_out],
        smem=(4,),
        in_hbm=(5, 6),
        out_hbm=(0, 1),
        copies=2,
        aliases={5: 0, 6: 1},
    )


def solution(mesh):
    in_specs = (
        P("lat", "lon", None),
        P("lat", "lon", None),
        P("lat", "lon"),
        P(None, "lat", "lon"),
        P(None, "lon"),
    )
    out_specs = (P(None, "lat", "lon"), P(None, "lon"))
    return jax.shard_map(shards, mesh=mesh, in_specs=in_specs, out_specs=out_specs, check_vma=False)
```

```python
import functools

import jax
import jax.numpy as jnp
from jax import lax
from jax.experimental import pallas as pl
from jax.experimental.pallas import tpu as pltpu
from jax.sharding import PartitionSpec as P

STEPS = 4
SWEEPS = 4
PAIRS = 2 * STEPS
BITS = 15
LANES = 128

KLAT = 0.2
KLON = 0.05
EPS = 1e-06
F32 = jnp.float32
BF16 = jnp.bfloat16
VMEM = pl.BlockSpec(memory_space=pltpu.VMEM)
SMEM = pl.BlockSpec(memory_space=pltpu.SMEM)
NT = (((1,), (1,)), ((), ()))


def pairing(lat_map, lon_map):
    nlat, nlon = (lax.axis_size("lat"), lax.axis_size("lon"))
    return [(i * nlon + j, lat_map(i) * nlon + lon_map(j)) for i in range(nlat) for j in range(nlon)]


def swap(x, lat_bits, lon_bits):
    return lax.ppermute(x, ("lat", "lon"), pairing(lambda i: i ^ lat_bits, lambda j: j ^ lon_bits))


def sum_all(x):
    nlat, nlon = (lax.axis_size("lat"), lax.axis_size("lon"))
    if nlat & (nlat - 1) or nlon & (nlon - 1):
        return lax.psum(x, ("lat", "lon"))
    core = 1 if nlon > 1 else 0
    if core:
        x = x + swap(x, 0, core)
    for size, first, on_lat in ((nlat, 1, True), (nlon, 2, False)):
        bit = first
        while bit < size:
            bits = lambda b: (b, core) if on_lat else (0, b | core)
            if 2 * bit < size:
                near, far, both = (swap(x, *bits(b)) for b in (bit, 2 * bit, 3 * bit))
                x = (x + near) + (far + both) if on_lat else (x + near) + (both + far)
                bit *= 4
            else:
                x = x + swap(x, *bits(bit))
                bit *= 2
    return x


def lat_partners(x):
    count = lax.axis_size("lat")
    same = lambda j: j
    got_a = lax.ppermute(x, ("lat", "lon"), pairing(lambda i: i ^ 1, same))
    got_b = lax.ppermute(x, ("lat", "lon"), pairing(lambda i: (i + 1 if i % 2 else i - 1) % count, same))
    return got_a, got_b


def lon_partners(near, far):
    count = lax.axis_size("lon")
    same = lambda i: i
    got_far = lax.ppermute(far, ("lat", "lon"), pairing(same, lambda j: (j + 1 if j % 2 else j - 1) % count))
    return swap(near, 0, 1), got_far


def split(x):
    high = x.astype(BF16)
    return high, (x - high.astype(F32)).astype(BF16)


def solve_pair(g00, g01, g10, g11, right0, right1):
    determ = g00 * g11 - g01 * g10
    return (g11 * right0 - g01 * right1) / determ, (g00 * right1 - g10 * right0) / determ


def total_of(x):
    return jnp.sum(x, axis=1, keepdims=True)


def lane_ids(shape):
    return lax.broadcasted_iota(jnp.int32, shape, 1)


def to_block(field, rows, reach):
    n, own = (field.shape[0], rows * LANES)
    halo = field[:, own:]
    lane = lane_ids((n, LANES))
    parts = []
    for r in range(rows):
        east = pltpu.roll(halo, (LANES - rows * reach - reach * r) % LANES, 1)
        west = pltpu.roll(halo, (LANES - reach - reach * r) % LANES, 1)
        edge = jnp.where(lane < LANES // 2, east, west)
        parts.append(jnp.concatenate([field[:, r * LANES : (r + 1) * LANES], edge], axis=1))
    return jnp.concatenate(parts, axis=0)


def from_block(block, rows, reach):
    n = block.shape[0] // rows
    lane = lane_ids((n, LANES))
    halo = jnp.zeros((n, LANES), F32)
    own = []
    for r in range(rows):
        part = block[r * n : (r + 1) * n]
        own.append(part[:, :LANES])
        edge = part[:, LANES:]
        east = pltpu.roll(edge, (rows * reach + reach * r) % LANES, 1)
        west = pltpu.roll(edge, (reach * r + reach) % LANES, 1)
        first = reach * r
        halo = jnp.where((lane >= first) & (lane < first + reach), west, halo)
        first = rows * reach + reach * r
        halo = jnp.where((lane >= first) & (lane < first + reach), east, halo)
    return jnp.concatenate(own + [halo], axis=1)


def unpack_words(words, spread_ref, bit_ref):
    top = ((words >> 8) << 8).astype(F32).astype(BF16)
    bottom = (words & 255).astype(F32).astype(BF16)
    spread = spread_ref[...]
    each = jnp.dot(jnp.concatenate([top, bottom], axis=1), spread, preferred_element_type=F32).astype(jnp.int32)
    return jnp.where((each & bit_ref[...]) == 0, 1.0, 0.0).astype(BF16)


def fill_spread(spread_ref, bit_ref):
    days = spread_ref.shape[1]
    word = lax.broadcasted_iota(jnp.int32, (LANES, days), 0)
    rest = lane_ids((LANES, days)) - BITS * word
    hit = jnp.where((rest >= 0) & (rest < BITS), 1.0, 0.0).astype(BF16)
    spread_ref[:LANES] = hit
    spread_ref[LANES:] = hit
    word = jnp.where((rest >= 0) & (rest < BITS), rest, 0)
    bit_ref[...] = jnp.left_shift(1, jnp.sum(word, axis=0, keepdims=True))


def fill_spread_days(spread_ref):
    days = spread_ref.shape[0]
    rest = lax.broadcasted_iota(jnp.int32, (days, LANES), 0) - BITS * lane_ids((days, LANES))
    hit = jnp.where((rest >= 0) & (rest < BITS), 1.0, 0.0).astype(BF16)
    spread_ref[:, :LANES] = hit
    spread_ref[:, LANES:] = hit


def unpack_days(words, spread_ref, m_ref):
    days = spread_ref.shape[0]
    step = days // 5
    for g in range(words.shape[1] // LANES):
        group = words[:, g * LANES : (g + 1) * LANES]
        top = ((group >> 8) << 8).astype(F32).astype(BF16)
        bottom = (group & 255).astype(F32).astype(BF16)
        both = jnp.concatenate([top, bottom], axis=1)
        for first in range(0, days, step):
            each = lax.dot_general(spread_ref[first : first + step], both, NT, preferred_element_type=F32).astype(jnp.int32)
            day = first + lax.broadcasted_iota(jnp.int32, (step, LANES), 0)
            bit = jnp.left_shift(1, day - BITS * ((day * 34953) >> 19))
            for c in range(0, each.shape[1], LANES):
                flags = jnp.where((each[:, c : c + LANES] & bit) == 0, 1.0, 0.0).astype(BF16)
                m_ref[g * days + first : g * days + first + step, c : c + LANES] = flags


def as_column(row):
    return jnp.transpose(jnp.broadcast_to(row, (8, LANES)))[:, :1]


def own_flags_kernel(reach, *refs):
    words_hbm, coast_hbm, x_hbm, maps_hbm, series_hbm, place_ref = refs[:6]
    m_ref, a_ref, held_ref, u_ref, row_ref, near_ref, far_ref, maps_out, series_out = refs[6:15]
    words_ref, coast_ref, x_ref, maps_ref, series_ref, spread_ref, bit_ref, sems = refs[15:]
    rows = coast_ref.shape[0]
    loads = [
        pltpu.make_async_copy(words_hbm, words_ref, sems.at[0]),
        pltpu.make_async_copy(coast_hbm, coast_ref, sems.at[1]),
    ]
    for r in range(rows):
        at = pl.ds(r * LANES, LANES)
        loads.append(pltpu.make_async_copy(x_hbm.at[at], x_ref.at[at], sems.at[2 + r]))
    loads.append(pltpu.make_async_copy(maps_hbm, maps_ref, sems.at[2 + rows]))
    loads.append(pltpu.make_async_copy(series_hbm, series_ref, sems.at[3 + rows]))
    stores = [
        pltpu.make_async_copy(maps_ref, maps_out, sems.at[4 + rows]),
        pltpu.make_async_copy(series_ref, series_out, sems.at[5 + rows]),
    ]
    for load in loads:
        load.start()
    fill_spread(spread_ref, bit_ref)
    loads[0].wait()
    loads[1].wait()
    for load, store in zip(loads[-2:], stores, strict=True):
        load.wait()
        store.start()
    days = spread_ref.shape[1]
    coast_own = coast_ref[...].astype(F32)
    coasts = jnp.transpose(jnp.concatenate([coast_own] * (8 // rows), axis=0))
    for r in range(rows):
        coast = coasts[:, r : r + 1]
        ocean = coast.astype(BF16)
        coast = coast.astype(jnp.int32)
        loads[2 + r].wait()
        cell = slice(r * LANES, (r + 1) * LANES)
        for g in range(words_ref.shape[1] // LANES):
            words = words_ref[cell, g * LANES : (g + 1) * LANES] * coast
            held_ref[cell, g * LANES : (g + 1) * LANES] = words
            given = unpack_words(words, spread_ref, bit_ref)
            at = slice(g * days, (g + 1) * days)
            m_ref[cell, at] = given
            a_ref[cell, at] = x_ref[cell, at] * given * ocean
    modes = maps_ref.shape[0]
    pieces = []
    for r in range(rows):
        at = slice(r * LANES, (r + 1) * LANES)
        u = maps_ref[:, r, :]
        u_ref[:, at] = u
        row_ref[:, at] = coast_own[r : r + 1]
        pieces.append(jnp.concatenate([u, jnp.broadcast_to(coast_own[r : r + 1], (8, LANES))], axis=0))
    base = modes + 8
    odd = place_ref[3] % 2 == 1
    west, east = edges(pieces, reach)
    near_ref[:base] = jnp.where(odd, west, east)
    far_ref[:base] = jnp.where(odd, east, west)
    for g in range(words_ref.shape[1] // LANES):
        for r in range(rows):
            at = slice(base + reach * (rows * g + r), base + reach * (rows * g + r + 1))
            group = slice(g * LANES, (g + 1) * LANES)
            west = words_ref[r * LANES : r * LANES + reach, group].astype(F32)
            east = words_ref[(r + 1) * LANES - reach : (r + 1) * LANES, group].astype(F32)
            near_ref[at] = jnp.where(odd, west, east)
            far_ref[at] = jnp.where(odd, east, west)
    for store in stores:
        store.wait()


def edges(pieces, reach):
    rows = len(pieces)
    shape = pieces[0].shape
    lane = lane_ids(shape)
    west = jnp.zeros(shape, F32)
    east = west
    for r, part in enumerate(pieces):
        first = rows * reach + reach * r
        west = jnp.where((lane >= first) & (lane < first + reach), pltpu.roll(part, first % LANES, 1), west)
        first = reach * r
        east = jnp.where((lane >= first) & (lane < first + reach), pltpu.roll(part, (first + reach) % LANES, 1), east)
    return west, east


def in_order(pieces, here):
    bit = 1
    while bit < len(pieces):
        turn = (here // bit) % 2 == 1
        pieces = [jnp.where(turn, pieces[i ^ bit], pieces[i]) for i in range(len(pieces))]
        bit *= 2
    return pieces


def given_kernel(rows, reach, *refs):
    a_ref, place_ref = refs[:2]
    xv_ref, near_ref, far_ref, v_ref = refs[-4:]
    here = place_ref[3]
    share = refs[2].shape[1]
    for i, piece in enumerate(in_order([ref[:PAIRS] for ref in refs[2:-4]], here)):
        v_ref[:, i * share : (i + 1) * share] = piece
    high, low = split(v_ref[...])
    both = lax.dot_general(jnp.concatenate([high, low], axis=0), a_ref[...], NT, preferred_element_type=F32)
    xv = both[:PAIRS] + both[PAIRS:]
    xv_ref[...] = xv
    west, east = edges([xv[:, r * LANES : (r + 1) * LANES] for r in range(rows)], reach)
    odd = here % 2 == 1
    near_ref[...] = jnp.where(odd, west, east)
    far_ref[...] = jnp.where(odd, east, west)


def masked_products(vs, u, low, chunk, m_ref, by_day=True):
    modes, days = vs.shape
    acc = None
    for first in range(0, days, chunk):
        at = slice(first, first + chunk)
        v = vs[:, at]
        high, lower = split(jnp.concatenate([v * v[j : j + 1] for j in (low, low + 1)], axis=0))
        left = jnp.concatenate([high, lower], axis=0)
        if by_day:
            part = jnp.dot(left, m_ref[at], preferred_element_type=F32)
        else:
            part = lax.dot_general(left, m_ref[:, at], NT, preferred_element_type=F32)
        acc = part if acc is None else acc + part
    acc = acc[: 2 * modes] + acc[2 * modes :]
    return jnp.concatenate(
        [jnp.sum(u * acc[j * modes : (j + 1) * modes], axis=0, keepdims=True) for j in range(2)], axis=0
    )


def first_products_kernel(chunk, *refs):
    near_ref, far_ref, place_ref, m_ref, u_own_ref, row_own_ref = refs[:6]
    base_ref, inv_ref, v_ref, mh_ref, u_ref, row_ref, spread_ref = refs[-7:]
    fill_spread_days(spread_ref)
    share = refs[6].shape[1]
    for i, piece in enumerate(in_order([ref[...] for ref in refs[6:-7]], place_ref[3])):
        v_ref[:, i * share : (i + 1) * share] = piece
    odd = place_ref[3] % 2 == 1
    west = jnp.where(odd, near_ref[...], far_ref[...])
    east = jnp.where(odd, far_ref[...], near_ref[...])
    modes, own = u_own_ref.shape
    base = modes + 8
    lane = lane_ids((base, LANES))
    fields = jnp.where(lane < LANES // 2, west[:base], east[:base])
    u_own, u_halo, row_halo = (u_own_ref[...], fields[:modes], fields[modes : modes + 1])
    u_ref[:, :own] = u_own
    u_ref[:, own:] = u_halo
    row_ref[:, :own] = row_own_ref[...]
    row_ref[:, own:] = row_halo
    coast = as_column(row_halo).astype(jnp.int32)
    half = LANES // 2
    groups = [slice(base + half * g, base + half * (g + 1)) for g in range((west.shape[0] - base) // half)]
    words = jnp.concatenate([jnp.concatenate([west[at], east[at]], axis=0) for at in groups], axis=1)
    unpack_days(words.astype(jnp.int32) * coast, spread_ref, mh_ref)
    base_ref[:, :own] = masked_products(v_ref, u_own, 0, chunk, m_ref, by_day=False)
    base_ref[:, own:] = masked_products(v_ref, u_halo, 0, chunk, mh_ref)
    inv_ref[...] = inverse_rows(v_ref[:2])


def days_flags_kernel(held_ref, spread_ref, m_ref):
    unpack_days(held_ref[...], spread_ref, m_ref)


def inverse_rows(pair):
    v0, v1 = (pair[0:1], pair[1:2])
    h00, h01, h11 = (total_of(v0 * v0), total_of(v0 * v1), total_of(v1 * v1))
    determ = h00 * h11 - h01 * h01
    rows = [h11 / determ, h01 / determ, h00 / determ]
    rows = [jnp.broadcast_to(z, (1, LANES)) for z in rows]
    return jnp.concatenate(rows + [jnp.zeros((5, LANES), F32)], axis=0)


def along(row, length):
    return jnp.concatenate([row] * (length // LANES), axis=1)


def next_products_kernel(step, chunk, m_ref, mh_ref, v_ref, u_ref, base_ref, inv_ref):
    low = 2 * step
    own = m_ref.shape[1]
    mode = lax.broadcasted_iota(jnp.int32, u_ref.shape, 0)
    u = jnp.where((mode >= low - 2) & (mode < low), 0.0, u_ref[...])
    base_ref[:, :own] = masked_products(v_ref, u[:, :own], low, chunk, m_ref)
    base_ref[:, own:] = masked_products(v_ref, u[:, own:], low, chunk, mh_ref)
    inv_ref[...] = inverse_rows(v_ref[low : low + 2])


def masked_rows(first, second, m_ref, mh_ref):
    high, lower = split(jnp.concatenate([first * second[0:1], first * second[1:2]], axis=0))
    left = jnp.concatenate([high, lower], axis=0)
    acc = jnp.concatenate(
        [
            jnp.dot(left, m_ref[...], preferred_element_type=F32),
            jnp.dot(left, mh_ref[...], preferred_element_type=F32),
        ],
        axis=1,
    )
    return acc[:4] + acc[4:]


def new_fields(inv_ref, u_pair, coast, proj):
    first, other, last = (along(inv_ref[i : i + 1], proj.shape[1]) for i in range(3))
    p0, p1 = (proj[0:1], proj[1:2])
    return coast * (u_pair + jnp.concatenate([first * p0 - other * p1, last * p1 - other * p0], axis=0))


def first_fields_kernel(rows, reach, near_ref, far_ref, place_ref, inv_ref, u_ref, row_ref, xv_ref, base_ref, w_ref, xh_ref):
    odd = place_ref[3] % 2 == 1
    west = jnp.where(odd, near_ref[...], far_ref[...])
    east = jnp.where(odd, far_ref[...], near_ref[...])
    xh = jnp.where(lane_ids((PAIRS, LANES)) < LANES // 2, west, east)
    xh_ref[...] = xh
    proj = jnp.concatenate([xv_ref[:2], xh[:2]], axis=1) - base_ref[...]
    coast = row_ref[...]
    count = 2 * rows
    w_ref[:count] = to_block(new_fields(inv_ref, u_ref[:2], coast, proj), rows, reach)
    w_ref[count:] = to_block(jnp.concatenate([coast, coast], axis=0), rows, reach)


def fields_kernel(step, rows, reach, total, *refs):
    m_ref, mh_ref, v_ref, u_ref, row_ref, xv_ref, xh_ref, base_ref, inv_ref, sum_ref, block_ref, w_ref, v_out, u_out = refs
    low = 2 * step
    days = v_ref.shape[1]
    sums = sum_ref[:, :days]
    masked = masked_rows(sums, v_ref[low : low + 2], m_ref, mh_ref)
    mixes, norms = mixing(total, sum_ref)
    un = new_units(rows, reach, norms, block_ref)
    cells = un.shape[1]
    mixes = [[along(z, cells) for z in mix] for mix in mixes]
    changed = []
    for j in range(2):
        p0, p1 = (masked[2 * j : 2 * j + 1], masked[2 * j + 1 : 2 * j + 2])
        changed.append(sum(un[k : k + 1] * (mixes[k][0] * p0 + mixes[k][1] * p1) for k in range(2)))
    given = jnp.concatenate([xv_ref[low : low + 2], xh_ref[low : low + 2]], axis=1)
    proj = given - base_ref[...] - jnp.concatenate(changed, axis=0)
    w_ref[...] = to_block(new_fields(inv_ref, u_ref[low : low + 2], row_ref[...], proj), rows, reach)
    v_out[low - 2 : low] = new_series(total, sum_ref)
    u_out[low - 2 : low] = un


def mixing(total, sum_ref):
    days = sum_ref.shape[1] - 2 * LANES
    g00, g01 = (sum_ref[0:1, days : days + LANES], sum_ref[0:1, days + LANES :])
    g11 = sum_ref[1:2, days + LANES :]
    n0, n1 = (jnp.sqrt(g00 / total + EPS), jnp.sqrt(g11 / total + EPS))
    g00, g01, g11 = (g00 / (n0 * n0), g01 / (n0 * n1), g11 / (n1 * n1))
    determ = g00 * g11 - g01 * g01
    cross = g01 / determ
    return [[g11 / determ / n0, -(cross / n1)], [-(cross / n0), g00 / determ / n1]], (n0, n1)


def new_series(total, sum_ref):
    days = sum_ref.shape[1] - 2 * LANES
    p0, p1 = (sum_ref[0:1, :days], sum_ref[1:2, :days])
    mixes, _ = mixing(total, sum_ref)
    return jnp.concatenate([along(mix[0], days) * p0 + along(mix[1], days) * p1 for mix in mixes], axis=0)


def new_units(rows, reach, norms, block_ref):
    field = from_block(block_ref[...], rows, reach)
    return jnp.concatenate([field[k : k + 1] / along(norms[k], field.shape[1]) for k in range(2)], axis=0)


def sums_kernel(step, rows, chunk, *refs):
    m_ref, a_ref, v_ref, u_ref, place_ref, klon_ref, cosl_ref, w_ref, ga_ref, gb_ref = refs[:10]
    refs = refs[10:]
    if step:
        coef_ref, sum_ref, block_ref = refs
    else:
        sum_ref, block_ref, coef_ref = refs
    days = v_ref.shape[1]
    low = 2 * step
    own = rows * LANES
    count = 2 * rows
    row0, nlat, odd = (place_ref[0], place_ref[1], place_ref[2])

    def assemble(mid, a, b):
        is_odd = odd == 1
        return jnp.concatenate([jnp.where(is_odd, a, b), mid, jnp.where(is_odd, b, a)], axis=0)

    w = assemble(w_ref[:count], ga_ref[:count], gb_ref[:count])
    tall = 3 * count
    north = lambda z: pltpu.roll(z, 2, 0)
    south = lambda z: pltpu.roll(z, tall - 2, 0)
    west = lambda z: pltpu.roll(z, 1, 1)
    east = lambda z: pltpu.roll(z, 2 * LANES - 1, 1)
    if step == 0:
        coast = assemble(w_ref[count:], ga_ref[count:], gb_ref[count:])
        row = row0 - rows + lax.broadcasted_iota(jnp.int32, (tall, 2 * LANES), 0) // 2
        coast = jnp.where((row >= 0) & (row < nlat), coast, 0.0)
        klon = klon_ref[...] * coast
        klat = KLAT * coast
        parts = [klat * north(coast), klat * south(coast), klon * west(coast), klon * east(coast)]
        parts.append(1.0 - ((parts[0] + parts[1]) + (parts[2] + parts[3])))
        for i, part in enumerate(parts):
            coef_ref[i * tall : (i + 1) * tall] = part
    an, as_, aw, ae, stay = (coef_ref[i * tall : (i + 1) * tall] for i in range(5))
    for _ in range(SWEEPS):
        w = stay * w + (an * north(w) + as_ * south(w)) + (aw * west(w) + ae * east(w))
    block = w[count : 2 * count]
    block_ref[...] = block
    cells = lambda z: jnp.concatenate([z[2 * r : 2 * r + 2, :LANES] for r in range(rows)], axis=1)
    fresh = cells(block)
    weighted = cells(block * cosl_ref[...])
    u = u_ref[:, :own]
    modes = u.shape[0]
    high, lower = split(jnp.concatenate([u * weighted[0:1], u * weighted[1:2]], axis=0))
    left = jnp.concatenate([high, lower], axis=0)
    high, lower = split(weighted)
    left_a = jnp.concatenate([high, lower], axis=0)
    for j in range(2):
        for i in range(2):
            gram = total_of(weighted[j : j + 1] * fresh[i : i + 1])
            sum_ref[j : j + 1, days + i * LANES : days + (i + 1) * LANES] = jnp.broadcast_to(gram, (1, LANES))
    old = [[total_of(weighted[j : j + 1] * u[low + i : low + i + 1]) for i in range(2)] for j in range(2)]
    for first in range(0, days, chunk):
        at = slice(first, first + chunk)
        masked = jnp.dot(left, m_ref[:, at], preferred_element_type=F32)
        given = jnp.dot(left_a, a_ref[:, at], preferred_element_type=F32)
        v = v_ref[:, at]
        for j in range(2):
            part = masked[j * modes : (j + 1) * modes] + masked[(2 + j) * modes : (3 + j) * modes]
            sum_ref[j : j + 1, at] = (
                given[j : j + 1]
                + given[2 + j : 3 + j]
                - jnp.sum(v * part, axis=0, keepdims=True)
                + old[j][0] * v[low : low + 1]
                + old[j][1] * v[low + 1 : low + 2]
            )


def last_kernel(rows, reach, total, *refs):
    v_ref, u_ref, sum_ref, block_ref, place_ref = refs[:5]
    maps_out, series_out, maps_new, series_new, held_ref, sems = refs[7:]
    share = series_new.shape[1]
    stores = [
        pltpu.make_async_copy(maps_new, maps_out.at[pl.ds(0, PAIRS)], sems.at[0]),
        pltpu.make_async_copy(series_new, series_out.at[pl.ds(0, PAIRS)], sems.at[1]),
    ]
    un = new_units(rows, reach, mixing(total, sum_ref)[1], block_ref)
    vn = new_series(total, sum_ref)
    u = jnp.concatenate([u_ref[: PAIRS - 2], un], axis=0)
    for r in range(rows):
        maps_new[:, r, :] = u[:, r * LANES : (r + 1) * LANES]
    stores[0].start()
    days = v_ref.shape[1]
    held_ref[: PAIRS - 2, :days] = v_ref[: PAIRS - 2]
    held_ref[PAIRS - 2 :, :days] = vn
    start = place_ref[3] * share
    tile = start // LANES
    width = held_ref.shape[1] - days + (share // LANES) * LANES
    window = held_ref[:, pl.ds(pl.multiple_of(tile * LANES, LANES), width)]
    series_new[...] = pltpu.roll(window, (width - (start - tile * LANES)) % width, 1)[:, :share]
    stores[1].start()
    for store in stores:
        store.wait()


def call(kernel, name, outs, scratch, args, smem=(), mib=24, flops=0, copies=0, in_hbm=(), out_hbm=(), aliases={}, light=False):
    moved = 0 if light else sum(z.size * z.dtype.itemsize for z in args)
    hbm = pl.BlockSpec(memory_space=pl.ANY)
    args = [pltpu.with_memory_space_constraint(z, pltpu.HBM) if i in in_hbm else z for i, z in enumerate(args)]
    return pl.pallas_call(
        kernel,
        out_shape=[jax.ShapeDtypeStruct(s, t) for s, t in outs],
        in_specs=[SMEM if i in smem else hbm if i in in_hbm else VMEM for i in range(len(args))],
        out_specs=[hbm if i in out_hbm else VMEM for i in range(len(outs))],
        scratch_shapes=[pltpu.VMEM(s, t) for s, t in scratch] + ([pltpu.SemaphoreType.DMA((copies,))] if copies else []),
        input_output_aliases=aliases,
        compiler_params=pltpu.CompilerParams(vmem_limit_bytes=mib * 2**20),
        cost_estimate=pl.CostEstimate(flops=flops, bytes_accessed=moved, transcendentals=0),
        name=name,
    )(*args)


def latitude_cos(rows, nrows):
    degree = -60.0 + 120.0 * (rows.astype(F32) + 0.5) / nrows
    return jnp.cos(degree * (jnp.pi / 180.0))


def shards(sea_heat_deviations, missing_date_bitmask, ocean_binary_mask, mode_maps, mode_series):
    rows, columns, days = sea_heat_deviations.shape
    modes, words = (mode_maps.shape[0], missing_date_bitmask.shape[2])
    nlat = rows * lax.axis_size("lat")
    total = float(modes * nlat * columns * lax.axis_size("lon"))
    own, reach = (rows * columns, SWEEPS * STEPS)
    sides = 2 * rows * reach
    cells = own + sides
    assert columns == LANES and sides == LANES and rows == SWEEPS and days == BITS * words
    chunk = days // 5
    row0 = lax.axis_index("lat") * rows
    here = lax.axis_index("lon")
    place = jnp.stack([row0, jnp.int32(nlat), lax.axis_index("lat") % 2, here]).astype(jnp.int32)
    tall = row0 - rows + jnp.arange(6 * rows) // 2
    cos_tall = latitude_cos(tall, nlat)[:, None]
    klon = jnp.broadcast_to(KLON / (cos_tall * cos_tall), (6 * rows, 2 * LANES))
    cosl = jnp.broadcast_to(cos_tall[2 * rows : 4 * rows], (2 * rows, 2 * LANES))

    words_per = words // LANES
    flags_scratch = [((2 * LANES, days // words_per), BF16), ((1, days // words_per), jnp.int32)]
    edge = ((modes + 8 + rows * reach * words_per, LANES), F32)
    inputs = [missing_date_bitmask.reshape(own, words), ocean_binary_mask, sea_heat_deviations.reshape(own, days)]
    inputs += [mode_maps, mode_series]
    place, klon, cosl = lax.optimization_barrier((place, klon, cosl))
    m, a, held, u, row, near, far, maps_out, series_out = call(
        functools.partial(own_flags_kernel, reach),
        "own_flags",
        [((own, days), BF16), ((own, days), BF16), ((own, words), jnp.int32)]
        + [((modes, own), F32), ((1, own), F32), edge, edge]
        + [(mode_maps.shape, F32), (mode_series.shape, F32)],
        [((own, words), jnp.int32), ((rows, LANES), jnp.int32), ((own, days), BF16)]
        + [(mode_maps.shape, F32), (mode_series.shape, F32), *flags_scratch],
        [*inputs, place],
        smem=(5,),
        in_hbm=range(5),
        out_hbm=(7, 8),
        copies=6 + rows,
        flops=4 * LANES * own * days,
    )
    if lax.axis_size("lon") == 8:
        pieces = [swap(mode_series, 0, b | 1) for b in (2, 4, 6)]
        *pieces, m, a = lax.optimization_barrier((*pieces, m, a))
        pieces = [z for piece in pieces for z in (swap(piece, 0, 1), piece)]
        pieces = [mode_series, swap(mode_series, 0, 1), *pieces]
    else:
        pieces = [lax.all_gather(mode_series, "lon", axis=1, tiled=True)]
    near, far = lon_partners(near, far)
    xv, near_xv, far_xv = call(
        functools.partial(given_kernel, rows, reach),
        "given",
        [((PAIRS, own), F32), ((PAIRS, LANES), F32), ((PAIRS, LANES), F32)],
        [((PAIRS, days), F32)],
        [a, place, *pieces],
        smem=(1,),
        light=True,
    )
    near_xv, far_xv = lon_partners(near_xv, far_xv)
    base, inverse, v, m_halo, u, row, spread = call(
        functools.partial(first_products_kernel, chunk),
        "first_products",
        [((2, cells), F32), ((8, LANES), F32), ((modes, days), F32), ((days, sides), BF16), ((modes, cells), F32), ((1, cells), F32)]
        + [((days // words_per, 2 * LANES), BF16)],
        [],
        [near, far, place, m, u, row, *pieces],
        smem=(2,),
        flops=8 * modes * cells * days,
    )

    (m_days,) = call(
        days_flags_kernel,
        "days_flags",
        [((days, own), BF16)],
        [],
        [held, spread],
        flops=4 * LANES * own * days,
    )

    count = 2 * rows
    summed = block = None
    coefs = []
    for step in range(STEPS):
        if step == 0:
            fresh, xv_halo = call(
                functools.partial(first_fields_kernel, rows, reach),
                "fields_0",
                [((2 * count, 2 * LANES), F32), ((PAIRS, sides), F32)],
                [],
                [near_xv, far_xv, place, inverse, u, row, xv, base],
                smem=(2,),
            )
        else:
            fresh, v, u = call(
                functools.partial(fields_kernel, step, rows, reach, total),
                f"fields_{step}",
                [((count, 2 * LANES), F32), ((modes, days), F32), ((modes, cells), F32)],
                [],
                [m_days, m_halo, v, u, row, xv, xv_halo, base, inverse, summed, block],
                flops=8 * modes * cells * days,
                aliases={2: 1, 3: 2},
            )
        got_a, got_b = lat_partners(fresh)
        outs = [((2, days + 2 * LANES), F32), ((count, 2 * LANES), F32)]
        coef = ((5 * 3 * count, 2 * LANES), F32)
        partial_sums, block, *made = call(
            functools.partial(sums_kernel, step, rows, days),
            f"sums_{step}",
            outs if step else [*outs, coef],
            [],
            [m, a, v, u, place, klon, cosl, fresh, got_a, got_b, *coefs],
            smem=(4,),
            flops=8 * modes * own * days,
        )
        coefs = coefs or made
        if step + 1 < STEPS:
            base, inverse = call(
                functools.partial(next_products_kernel, step + 1, chunk),
                f"next_products_{step + 1}",
                [((2, cells), F32), ((8, LANES), F32)],
                [],
                [m_days, m_halo, v, u],
                flops=8 * modes * cells * days,
            )
        summed = sum_all(partial_sums)
    return call(
        functools.partial(last_kernel, rows, reach, total),
        "last",
        [(mode_maps.shape, F32), (mode_series.shape, F32)],
        [((PAIRS, rows, columns), F32), ((PAIRS, mode_series.shape[1]), F32), ((PAIRS, days + 2 * LANES), F32)],
        [v, u, summed, block, place, maps_out, series_out],
        smem=(4,),
        in_hbm=(5, 6),
        out_hbm=(0, 1),
        copies=2,
        aliases={5: 0, 6: 1},
    )


def solution(mesh):
    in_specs = (
        P("lat", "lon", None),
        P("lat", "lon", None),
        P("lat", "lon"),
        P(None, "lat", "lon"),
        P(None, "lon"),
    )
    out_specs = (P(None, "lat", "lon"), P(None, "lon"))
    return jax.shard_map(shards, mesh=mesh, in_specs=in_specs, out_specs=out_specs, check_vma=False)
```

```python
import functools

import jax
import jax.numpy as jnp
from jax import lax
from jax.experimental import pallas as pl
from jax.experimental.pallas import tpu as pltpu
from jax.sharding import PartitionSpec as P

STEPS = 4
SWEEPS = 4
PAIRS = 2 * STEPS
BITS = 15
LANES = 128

KLAT = 0.2
KLON = 0.05
EPS = 1e-06
F32 = jnp.float32
BF16 = jnp.bfloat16
VMEM = pl.BlockSpec(memory_space=pltpu.VMEM)
SMEM = pl.BlockSpec(memory_space=pltpu.SMEM)
NT = (((1,), (1,)), ((), ()))


def pairing(lat_map, lon_map):
    nlat, nlon = (lax.axis_size("lat"), lax.axis_size("lon"))
    return [(i * nlon + j, lat_map(i) * nlon + lon_map(j)) for i in range(nlat) for j in range(nlon)]


def swap(x, lat_bits, lon_bits):
    return lax.ppermute(x, ("lat", "lon"), pairing(lambda i: i ^ lat_bits, lambda j: j ^ lon_bits))


def sum_all(x):
    nlat, nlon = (lax.axis_size("lat"), lax.axis_size("lon"))
    if nlat & (nlat - 1) or nlon & (nlon - 1):
        return lax.psum(x, ("lat", "lon"))
    core = 1 if nlon > 1 else 0
    if core:
        x = x + swap(x, 0, core)
    for size, first, on_lat in ((nlat, 1, True), (nlon, 2, False)):
        bit = first
        while bit < size:
            bits = lambda b: (b, core) if on_lat else (0, b | core)
            if 2 * bit < size:
                near, far, both = (swap(x, *bits(b)) for b in (bit, 2 * bit, 3 * bit))
                x = (x + near) + (far + both) if on_lat else (x + near) + (both + far)
                bit *= 4
            else:
                x = x + swap(x, *bits(bit))
                bit *= 2
    return x


def lat_partners(x):
    count = lax.axis_size("lat")
    same = lambda j: j
    got_a = lax.ppermute(x, ("lat", "lon"), pairing(lambda i: i ^ 1, same))
    got_b = lax.ppermute(x, ("lat", "lon"), pairing(lambda i: (i + 1 if i % 2 else i - 1) % count, same))
    return got_a, got_b


def lon_partners(near, far):
    count = lax.axis_size("lon")
    same = lambda i: i
    got_far = lax.ppermute(far, ("lat", "lon"), pairing(same, lambda j: (j + 1 if j % 2 else j - 1) % count))
    return swap(near, 0, 1), got_far


def split(x):
    high = x.astype(BF16)
    return high, (x - high.astype(F32)).astype(BF16)


def solve_pair(g00, g01, g10, g11, right0, right1):
    determ = g00 * g11 - g01 * g10
    return (g11 * right0 - g01 * right1) / determ, (g00 * right1 - g10 * right0) / determ


def total_of(x):
    return jnp.sum(x, axis=1, keepdims=True)


def lane_ids(shape):
    return lax.broadcasted_iota(jnp.int32, shape, 1)


def to_block(field, rows, reach):
    n, own = (field.shape[0], rows * LANES)
    halo = field[:, own:]
    lane = lane_ids((n, LANES))
    parts = []
    for r in range(rows):
        east = pltpu.roll(halo, (LANES - rows * reach - reach * r) % LANES, 1)
        west = pltpu.roll(halo, (LANES - reach - reach * r) % LANES, 1)
        edge = jnp.where(lane < LANES // 2, east, west)
        parts.append(jnp.concatenate([field[:, r * LANES : (r + 1) * LANES], edge], axis=1))
    return jnp.concatenate(parts, axis=0)


def from_block(block, rows, reach):
    n = block.shape[0] // rows
    lane = lane_ids((n, LANES))
    halo = jnp.zeros((n, LANES), F32)
    own = []
    for r in range(rows):
        part = block[r * n : (r + 1) * n]
        own.append(part[:, :LANES])
        edge = part[:, LANES:]
        east = pltpu.roll(edge, (rows * reach + reach * r) % LANES, 1)
        west = pltpu.roll(edge, (reach * r + reach) % LANES, 1)
        first = reach * r
        halo = jnp.where((lane >= first) & (lane < first + reach), west, halo)
        first = rows * reach + reach * r
        halo = jnp.where((lane >= first) & (lane < first + reach), east, halo)
    return jnp.concatenate(own + [halo], axis=1)


def unpack_words(words, spread_ref, bit_ref):
    top = ((words >> 8) << 8).astype(F32).astype(BF16)
    bottom = (words & 255).astype(F32).astype(BF16)
    spread = spread_ref[...]
    each = jnp.dot(jnp.concatenate([top, bottom], axis=1), spread, preferred_element_type=F32).astype(jnp.int32)
    return jnp.where((each & bit_ref[...]) == 0, 1.0, 0.0).astype(BF16)


def fill_spread(spread_ref, bit_ref):
    days = spread_ref.shape[1]
    word = lax.broadcasted_iota(jnp.int32, (LANES, days), 0)
    rest = lane_ids((LANES, days)) - BITS * word
    hit = jnp.where((rest >= 0) & (rest < BITS), 1.0, 0.0).astype(BF16)
    spread_ref[:LANES] = hit
    spread_ref[LANES:] = hit
    word = jnp.where((rest >= 0) & (rest < BITS), rest, 0)
    bit_ref[...] = jnp.left_shift(1, jnp.sum(word, axis=0, keepdims=True))


def fill_spread_days(spread_ref):
    days = spread_ref.shape[0]
    rest = lax.broadcasted_iota(jnp.int32, (days, LANES), 0) - BITS * lane_ids((days, LANES))
    hit = jnp.where((rest >= 0) & (rest < BITS), 1.0, 0.0).astype(BF16)
    spread_ref[:, :LANES] = hit
    spread_ref[:, LANES:] = hit


def unpack_days(words, spread_ref, m_ref):
    days = spread_ref.shape[0]
    step = days // 5
    for g in range(words.shape[1] // LANES):
        group = words[:, g * LANES : (g + 1) * LANES]
        top = ((group >> 8) << 8).astype(F32).astype(BF16)
        bottom = (group & 255).astype(F32).astype(BF16)
        both = jnp.concatenate([top, bottom], axis=1)
        for first in range(0, days, step):
            each = lax.dot_general(spread_ref[first : first + step], both, NT, preferred_element_type=F32).astype(jnp.int32)
            day = first + lax.broadcasted_iota(jnp.int32, (step, LANES), 0)
            bit = jnp.left_shift(1, day - BITS * ((day * 34953) >> 19))
            for c in range(0, each.shape[1], LANES):
                flags = jnp.where((each[:, c : c + LANES] & bit) == 0, 1.0, 0.0).astype(BF16)
                m_ref[g * days + first : g * days + first + step, c : c + LANES] = flags


def as_column(row):
    return jnp.transpose(jnp.broadcast_to(row, (8, LANES)))[:, :1]


def own_flags_kernel(reach, *refs):
    words_hbm, coast_hbm, x_hbm, maps_hbm, series_hbm, place_ref = refs[:6]
    m_ref, a_ref, held_ref, u_ref, row_ref, near_ref, far_ref, maps_out, series_out = refs[6:15]
    words_ref, coast_ref, x_ref, maps_ref, series_ref, spread_ref, bit_ref, sems = refs[15:]
    rows = coast_ref.shape[0]
    loads = [
        pltpu.make_async_copy(words_hbm, words_ref, sems.at[0]),
        pltpu.make_async_copy(coast_hbm, coast_ref, sems.at[1]),
    ]
    for r in range(rows):
        at = pl.ds(r * LANES, LANES)
        loads.append(pltpu.make_async_copy(x_hbm.at[at], x_ref.at[at], sems.at[2 + r]))
    loads.append(pltpu.make_async_copy(maps_hbm, maps_ref, sems.at[2 + rows]))
    loads.append(pltpu.make_async_copy(series_hbm, series_ref, sems.at[3 + rows]))
    stores = [
        pltpu.make_async_copy(maps_ref, maps_out, sems.at[4 + rows]),
        pltpu.make_async_copy(series_ref, series_out, sems.at[5 + rows]),
    ]
    for load in loads:
        load.start()
    fill_spread(spread_ref, bit_ref)
    loads[0].wait()
    loads[1].wait()
    for load, store in zip(loads[-2:], stores, strict=True):
        load.wait()
        store.start()
    days = spread_ref.shape[1]
    coast_own = coast_ref[...].astype(F32)
    coasts = jnp.transpose(jnp.concatenate([coast_own] * (8 // rows), axis=0))
    for r in range(rows):
        coast = coasts[:, r : r + 1]
        ocean = coast.astype(BF16)
        coast = coast.astype(jnp.int32)
        loads[2 + r].wait()
        cell = slice(r * LANES, (r + 1) * LANES)
        for g in range(words_ref.shape[1] // LANES):
            words = words_ref[cell, g * LANES : (g + 1) * LANES] * coast
            held_ref[cell, g * LANES : (g + 1) * LANES] = words
            given = unpack_words(words, spread_ref, bit_ref)
            at = slice(g * days, (g + 1) * days)
            m_ref[cell, at] = given
            a_ref[cell, at] = x_ref[cell, at] * given * ocean
    modes = maps_ref.shape[0]
    pieces = []
    for r in range(rows):
        at = slice(r * LANES, (r + 1) * LANES)
        u = maps_ref[:, r, :]
        u_ref[:, at] = u
        row_ref[:, at] = coast_own[r : r + 1]
        pieces.append(jnp.concatenate([u, jnp.broadcast_to(coast_own[r : r + 1], (8, LANES))], axis=0))
    base = modes + 8
    odd = place_ref[3] % 2 == 1
    west, east = edges(pieces, reach)
    near_ref[:base] = jnp.where(odd, west, east)
    far_ref[:base] = jnp.where(odd, east, west)
    for g in range(words_ref.shape[1] // LANES):
        for r in range(rows):
            at = slice(base + reach * (rows * g + r), base + reach * (rows * g + r + 1))
            group = slice(g * LANES, (g + 1) * LANES)
            west = words_ref[r * LANES : r * LANES + reach, group].astype(F32)
            east = words_ref[(r + 1) * LANES - reach : (r + 1) * LANES, group].astype(F32)
            near_ref[at] = jnp.where(odd, west, east)
            far_ref[at] = jnp.where(odd, east, west)
    for store in stores:
        store.wait()


def edges(pieces, reach):
    rows = len(pieces)
    shape = pieces[0].shape
    lane = lane_ids(shape)
    west = jnp.zeros(shape, F32)
    east = west
    for r, part in enumerate(pieces):
        first = rows * reach + reach * r
        west = jnp.where((lane >= first) & (lane < first + reach), pltpu.roll(part, first % LANES, 1), west)
        first = reach * r
        east = jnp.where((lane >= first) & (lane < first + reach), pltpu.roll(part, (first + reach) % LANES, 1), east)
    return west, east


def in_order(pieces, here):
    bit = 1
    while bit < len(pieces):
        turn = (here // bit) % 2 == 1
        pieces = [jnp.where(turn, pieces[i ^ bit], pieces[i]) for i in range(len(pieces))]
        bit *= 2
    return pieces


def given_kernel(rows, reach, *refs):
    a_ref, place_ref = refs[:2]
    xv_ref, near_ref, far_ref, v_ref = refs[-4:]
    here = place_ref[3]
    share = refs[2].shape[1]
    for i, piece in enumerate(in_order([ref[:PAIRS] for ref in refs[2:-4]], here)):
        v_ref[:, i * share : (i + 1) * share] = piece
    high, low = split(v_ref[...])
    both = lax.dot_general(jnp.concatenate([high, low], axis=0), a_ref[...], NT, preferred_element_type=F32)
    xv = both[:PAIRS] + both[PAIRS:]
    xv_ref[...] = xv
    west, east = edges([xv[:, r * LANES : (r + 1) * LANES] for r in range(rows)], reach)
    odd = here % 2 == 1
    near_ref[...] = jnp.where(odd, west, east)
    far_ref[...] = jnp.where(odd, east, west)


def masked_products(vs, u, low, chunk, m_ref, by_day=True):
    modes, days = vs.shape
    acc = None
    for first in range(0, days, chunk):
        at = slice(first, first + chunk)
        v = vs[:, at]
        high, lower = split(jnp.concatenate([v * v[j : j + 1] for j in (low, low + 1)], axis=0))
        left = jnp.concatenate([high, lower], axis=0)
        if by_day:
            part = jnp.dot(left, m_ref[at], preferred_element_type=F32)
        else:
            part = lax.dot_general(left, m_ref[:, at], NT, preferred_element_type=F32)
        acc = part if acc is None else acc + part
    acc = acc[: 2 * modes] + acc[2 * modes :]
    return jnp.concatenate(
        [jnp.sum(u * acc[j * modes : (j + 1) * modes], axis=0, keepdims=True) for j in range(2)], axis=0
    )


def first_products_kernel(chunk, *refs):
    near_ref, far_ref, place_ref, m_ref, u_own_ref, row_own_ref = refs[:6]
    base_ref, inv_ref, v_ref, mh_ref, u_ref, row_ref, spread_ref = refs[-7:]
    fill_spread_days(spread_ref)
    share = refs[6].shape[1]
    for i, piece in enumerate(in_order([ref[...] for ref in refs[6:-7]], place_ref[3])):
        v_ref[:, i * share : (i + 1) * share] = piece
    odd = place_ref[3] % 2 == 1
    west = jnp.where(odd, near_ref[...], far_ref[...])
    east = jnp.where(odd, far_ref[...], near_ref[...])
    modes, own = u_own_ref.shape
    base = modes + 8
    lane = lane_ids((base, LANES))
    fields = jnp.where(lane < LANES // 2, west[:base], east[:base])
    u_own, u_halo, row_halo = (u_own_ref[...], fields[:modes], fields[modes : modes + 1])
    u_ref[:, :own] = u_own
    u_ref[:, own:] = u_halo
    row_ref[:, :own] = row_own_ref[...]
    row_ref[:, own:] = row_halo
    coast = as_column(row_halo).astype(jnp.int32)
    half = LANES // 2
    groups = [slice(base + half * g, base + half * (g + 1)) for g in range((west.shape[0] - base) // half)]
    words = jnp.concatenate([jnp.concatenate([west[at], east[at]], axis=0) for at in groups], axis=1)
    unpack_days(words.astype(jnp.int32) * coast, spread_ref, mh_ref)
    base_ref[:, :own] = masked_products(v_ref, u_own, 0, chunk, m_ref, by_day=False)
    base_ref[:, own:] = masked_products(v_ref, u_halo, 0, chunk, mh_ref)
    inv_ref[...] = inverse_rows(v_ref[:2])


def days_flags_kernel(held_ref, spread_ref, m_ref):
    unpack_days(held_ref[...], spread_ref, m_ref)


def inverse_rows(pair):
    v0, v1 = (pair[0:1], pair[1:2])
    h00, h01, h11 = (total_of(v0 * v0), total_of(v0 * v1), total_of(v1 * v1))
    determ = h00 * h11 - h01 * h01
    rows = [h11 / determ, h01 / determ, h00 / determ]
    rows = [jnp.broadcast_to(z, (1, LANES)) for z in rows]
    return jnp.concatenate(rows + [jnp.zeros((5, LANES), F32)], axis=0)


def along(row, length):
    return jnp.concatenate([row] * (length // LANES), axis=1)


def next_products_kernel(step, chunk, m_ref, mh_ref, v_ref, u_ref, base_ref, inv_ref):
    low = 2 * step
    own = m_ref.shape[1]
    mode = lax.broadcasted_iota(jnp.int32, u_ref.shape, 0)
    u = jnp.where((mode >= low - 2) & (mode < low), 0.0, u_ref[...])
    base_ref[:, :own] = masked_products(v_ref, u[:, :own], low, chunk, m_ref)
    base_ref[:, own:] = masked_products(v_ref, u[:, own:], low, chunk, mh_ref)
    inv_ref[...] = inverse_rows(v_ref[low : low + 2])


def masked_rows(first, second, m_ref, mh_ref):
    high, lower = split(jnp.concatenate([first * second[0:1], first * second[1:2]], axis=0))
    left = jnp.concatenate([high, lower], axis=0)
    acc = jnp.concatenate(
        [
            jnp.dot(left, m_ref[...], preferred_element_type=F32),
            jnp.dot(left, mh_ref[...], preferred_element_type=F32),
        ],
        axis=1,
    )
    return acc[:4] + acc[4:]


def new_fields(inv_ref, u_pair, coast, proj):
    first, other, last = (along(inv_ref[i : i + 1], proj.shape[1]) for i in range(3))
    p0, p1 = (proj[0:1], proj[1:2])
    return coast * (u_pair + jnp.concatenate([first * p0 - other * p1, last * p1 - other * p0], axis=0))


def first_fields_kernel(rows, reach, near_ref, far_ref, place_ref, inv_ref, u_ref, row_ref, xv_ref, base_ref, w_ref, xh_ref):
    odd = place_ref[3] % 2 == 1
    west = jnp.where(odd, near_ref[...], far_ref[...])
    east = jnp.where(odd, far_ref[...], near_ref[...])
    xh = jnp.where(lane_ids((PAIRS, LANES)) < LANES // 2, west, east)
    xh_ref[...] = xh
    proj = jnp.concatenate([xv_ref[:2], xh[:2]], axis=1) - base_ref[...]
    coast = row_ref[...]
    count = 2 * rows
    w_ref[:count] = to_block(new_fields(inv_ref, u_ref[:2], coast, proj), rows, reach)
    w_ref[count:] = to_block(jnp.concatenate([coast, coast], axis=0), rows, reach)


def fields_kernel(step, rows, reach, total, *refs):
    m_ref, mh_ref, v_ref, u_ref, row_ref, xv_ref, xh_ref, base_ref, inv_ref, sum_ref, block_ref, w_ref, v_out, u_out = refs
    low = 2 * step
    days = v_ref.shape[1]
    sums = sum_ref[:, :days]
    masked = masked_rows(sums, v_ref[low : low + 2], m_ref, mh_ref)
    mixes, norms = mixing(total, sum_ref)
    un = new_units(rows, reach, norms, block_ref)
    cells = un.shape[1]
    mixes = [[along(z, cells) for z in mix] for mix in mixes]
    changed = []
    for j in range(2):
        p0, p1 = (masked[2 * j : 2 * j + 1], masked[2 * j + 1 : 2 * j + 2])
        changed.append(sum(un[k : k + 1] * (mixes[k][0] * p0 + mixes[k][1] * p1) for k in range(2)))
    given = jnp.concatenate([xv_ref[low : low + 2], xh_ref[low : low + 2]], axis=1)
    proj = given - base_ref[...] - jnp.concatenate(changed, axis=0)
    w_ref[...] = to_block(new_fields(inv_ref, u_ref[low : low + 2], row_ref[...], proj), rows, reach)
    v_out[low - 2 : low] = new_series(total, sum_ref)
    u_out[low - 2 : low] = un


def mixing(total, sum_ref):
    days = sum_ref.shape[1] - 2 * LANES
    g00, g01 = (sum_ref[0:1, days : days + LANES], sum_ref[0:1, days + LANES :])
    g11 = sum_ref[1:2, days + LANES :]
    n0, n1 = (jnp.sqrt(g00 / total + EPS), jnp.sqrt(g11 / total + EPS))
    g00, g01, g11 = (g00 / (n0 * n0), g01 / (n0 * n1), g11 / (n1 * n1))
    determ = g00 * g11 - g01 * g01
    cross = g01 / determ
    return [[g11 / determ / n0, -(cross / n1)], [-(cross / n0), g00 / determ / n1]], (n0, n1)


def new_series(total, sum_ref):
    days = sum_ref.shape[1] - 2 * LANES
    p0, p1 = (sum_ref[0:1, :days], sum_ref[1:2, :days])
    mixes, _ = mixing(total, sum_ref)
    return jnp.concatenate([along(mix[0], days) * p0 + along(mix[1], days) * p1 for mix in mixes], axis=0)


def new_units(rows, reach, norms, block_ref):
    field = from_block(block_ref[...], rows, reach)
    return jnp.concatenate([field[k : k + 1] / along(norms[k], field.shape[1]) for k in range(2)], axis=0)


def sums_kernel(step, rows, chunk, *refs):
    m_ref, a_ref, v_ref, u_ref, place_ref, klon_ref, cosl_ref, w_ref, ga_ref, gb_ref = refs[:10]
    refs = refs[10:]
    if step:
        coef_ref, sum_ref, block_ref = refs
    else:
        sum_ref, block_ref, coef_ref = refs
    days = v_ref.shape[1]
    low = 2 * step
    own = rows * LANES
    count = 2 * rows
    row0, nlat, odd = (place_ref[0], place_ref[1], place_ref[2])

    def assemble(mid, a, b):
        is_odd = odd == 1
        return jnp.concatenate([jnp.where(is_odd, a, b), mid, jnp.where(is_odd, b, a)], axis=0)

    w = assemble(w_ref[:count], ga_ref[:count], gb_ref[:count])
    tall = 3 * count
    north = lambda z: pltpu.roll(z, 2, 0)
    south = lambda z: pltpu.roll(z, tall - 2, 0)
    west = lambda z: pltpu.roll(z, 1, 1)
    east = lambda z: pltpu.roll(z, 2 * LANES - 1, 1)
    if step == 0:
        coast = assemble(w_ref[count:], ga_ref[count:], gb_ref[count:])
        row = row0 - rows + lax.broadcasted_iota(jnp.int32, (tall, 2 * LANES), 0) // 2
        coast = jnp.where((row >= 0) & (row < nlat), coast, 0.0)
        klon = klon_ref[...] * coast
        klat = KLAT * coast
        parts = [klat * north(coast), klat * south(coast), klon * west(coast), klon * east(coast)]
        parts.append(1.0 - ((parts[0] + parts[1]) + (parts[2] + parts[3])))
        for i, part in enumerate(parts):
            coef_ref[i * tall : (i + 1) * tall] = part
    an, as_, aw, ae, stay = (coef_ref[i * tall : (i + 1) * tall] for i in range(5))
    for _ in range(SWEEPS):
        w = stay * w + (an * north(w) + as_ * south(w)) + (aw * west(w) + ae * east(w))
    block = w[count : 2 * count]
    block_ref[...] = block
    cells = lambda z: jnp.concatenate([z[2 * r : 2 * r + 2, :LANES] for r in range(rows)], axis=1)
    fresh = cells(block)
    weighted = cells(block * cosl_ref[...])
    u = u_ref[:, :own]
    modes = u.shape[0]
    scaled = block * cosl_ref[...]
    parts = []
    for j in range(2):
        tiles = [u[:, r * LANES : (r + 1) * LANES] * scaled[2 * r + j : 2 * r + j + 1, :LANES] for r in range(rows)]
        parts.append(jnp.concatenate(tiles, axis=1))
    high, lower = split(jnp.concatenate(parts, axis=0))
    left = jnp.concatenate([high, lower], axis=0)
    high, lower = split(weighted)
    left_a = jnp.concatenate([high, lower], axis=0)
    for j in range(2):
        for i in range(2):
            gram = total_of(weighted[j : j + 1] * fresh[i : i + 1])
            sum_ref[j : j + 1, days + i * LANES : days + (i + 1) * LANES] = jnp.broadcast_to(gram, (1, LANES))
    old = [[total_of(weighted[j : j + 1] * u[low + i : low + i + 1]) for i in range(2)] for j in range(2)]
    for first in range(0, days, chunk):
        at = slice(first, first + chunk)
        masked = jnp.dot(left, m_ref[:, at], preferred_element_type=F32)
        given = jnp.dot(left_a, a_ref[:, at], preferred_element_type=F32)
        v = v_ref[:, at]
        for j in range(2):
            part = masked[j * modes : (j + 1) * modes] + masked[(2 + j) * modes : (3 + j) * modes]
            sum_ref[j : j + 1, at] = (
                given[j : j + 1]
                + given[2 + j : 3 + j]
                - jnp.sum(v * part, axis=0, keepdims=True)
                + old[j][0] * v[low : low + 1]
                + old[j][1] * v[low + 1 : low + 2]
            )


def last_kernel(rows, reach, total, *refs):
    v_ref, u_ref, sum_ref, block_ref, place_ref = refs[:5]
    maps_out, series_out, maps_new, series_new, held_ref, sems = refs[7:]
    share = series_new.shape[1]
    stores = [
        pltpu.make_async_copy(maps_new, maps_out.at[pl.ds(0, PAIRS)], sems.at[0]),
        pltpu.make_async_copy(series_new, series_out.at[pl.ds(0, PAIRS)], sems.at[1]),
    ]
    un = new_units(rows, reach, mixing(total, sum_ref)[1], block_ref)
    vn = new_series(total, sum_ref)
    u = jnp.concatenate([u_ref[: PAIRS - 2], un], axis=0)
    for r in range(rows):
        maps_new[:, r, :] = u[:, r * LANES : (r + 1) * LANES]
    stores[0].start()
    days = v_ref.shape[1]
    held_ref[: PAIRS - 2, :days] = v_ref[: PAIRS - 2]
    held_ref[PAIRS - 2 :, :days] = vn
    start = place_ref[3] * share
    tile = start // LANES
    width = held_ref.shape[1] - days + (share // LANES) * LANES
    window = held_ref[:, pl.ds(pl.multiple_of(tile * LANES, LANES), width)]
    series_new[...] = pltpu.roll(window, (width - (start - tile * LANES)) % width, 1)[:, :share]
    stores[1].start()
    for store in stores:
        store.wait()


def call(kernel, name, outs, scratch, args, smem=(), mib=24, flops=0, copies=0, in_hbm=(), out_hbm=(), aliases={}):
    moved = sum(z.size * z.dtype.itemsize for z in args)
    hbm = pl.BlockSpec(memory_space=pl.ANY)
    args = [pltpu.with_memory_space_constraint(z, pltpu.HBM) if i in in_hbm else z for i, z in enumerate(args)]
    return pl.pallas_call(
        kernel,
        out_shape=[jax.ShapeDtypeStruct(s, t) for s, t in outs],
        in_specs=[SMEM if i in smem else hbm if i in in_hbm else VMEM for i in range(len(args))],
        out_specs=[hbm if i in out_hbm else VMEM for i in range(len(outs))],
        scratch_shapes=[pltpu.VMEM(s, t) for s, t in scratch] + ([pltpu.SemaphoreType.DMA((copies,))] if copies else []),
        input_output_aliases=aliases,
        compiler_params=pltpu.CompilerParams(vmem_limit_bytes=mib * 2**20),
        cost_estimate=pl.CostEstimate(flops=flops, bytes_accessed=moved, transcendentals=0),
        name=name,
    )(*args)


def latitude_cos(rows, nrows):
    degree = -60.0 + 120.0 * (rows.astype(F32) + 0.5) / nrows
    return jnp.cos(degree * (jnp.pi / 180.0))


def shards(sea_heat_deviations, missing_date_bitmask, ocean_binary_mask, mode_maps, mode_series):
    rows, columns, days = sea_heat_deviations.shape
    modes, words = (mode_maps.shape[0], missing_date_bitmask.shape[2])
    nlat = rows * lax.axis_size("lat")
    total = float(modes * nlat * columns * lax.axis_size("lon"))
    own, reach = (rows * columns, SWEEPS * STEPS)
    sides = 2 * rows * reach
    cells = own + sides
    assert columns == LANES and sides == LANES and rows == SWEEPS and days == BITS * words
    chunk = days // 5
    row0 = lax.axis_index("lat") * rows
    here = lax.axis_index("lon")
    place = jnp.stack([row0, jnp.int32(nlat), lax.axis_index("lat") % 2, here]).astype(jnp.int32)
    tall = row0 - rows + jnp.arange(6 * rows) // 2
    cos_tall = latitude_cos(tall, nlat)[:, None]
    klon = jnp.broadcast_to(KLON / (cos_tall * cos_tall), (6 * rows, 2 * LANES))
    cosl = jnp.broadcast_to(cos_tall[2 * rows : 4 * rows], (2 * rows, 2 * LANES))

    words_per = words // LANES
    flags_scratch = [((2 * LANES, days // words_per), BF16), ((1, days // words_per), jnp.int32)]
    edge = ((modes + 8 + rows * reach * words_per, LANES), F32)
    inputs = [missing_date_bitmask.reshape(own, words), ocean_binary_mask, sea_heat_deviations.reshape(own, days)]
    inputs += [mode_maps, mode_series]
    place, klon, cosl = lax.optimization_barrier((place, klon, cosl))
    m, a, held, u, row, near, far, maps_out, series_out = call(
        functools.partial(own_flags_kernel, reach),
        "own_flags",
        [((own, days), BF16), ((own, days), BF16), ((own, words), jnp.int32)]
        + [((modes, own), F32), ((1, own), F32), edge, edge]
        + [(mode_maps.shape, F32), (mode_series.shape, F32)],
        [((own, words), jnp.int32), ((rows, LANES), jnp.int32), ((own, days), BF16)]
        + [(mode_maps.shape, F32), (mode_series.shape, F32), *flags_scratch],
        [*inputs, place],
        smem=(5,),
        in_hbm=range(5),
        out_hbm=(7, 8),
        copies=6 + rows,
        flops=4 * LANES * own * days,
    )
    if lax.axis_size("lon") == 8:
        pieces = [swap(mode_series, 0, b | 1) for b in (2, 4, 6)]
        *pieces, m, a = lax.optimization_barrier((*pieces, m, a))
        pieces = [z for piece in pieces for z in (swap(piece, 0, 1), piece)]
        pieces = [mode_series, swap(mode_series, 0, 1), *pieces]
    else:
        pieces = [lax.all_gather(mode_series, "lon", axis=1, tiled=True)]
    near, far = lon_partners(near, far)
    xv, near_xv, far_xv = call(
        functools.partial(given_kernel, rows, reach),
        "given",
        [((PAIRS, own), F32), ((PAIRS, LANES), F32), ((PAIRS, LANES), F32)],
        [((PAIRS, days), F32)],
        [a, place, *pieces],
        smem=(1,),
        flops=4 * PAIRS * own * days,
    )
    near_xv, far_xv = lon_partners(near_xv, far_xv)
    base, inverse, v, m_halo, u, row, spread = call(
        functools.partial(first_products_kernel, chunk),
        "first_products",
        [((2, cells), F32), ((8, LANES), F32), ((modes, days), F32), ((days, sides), BF16), ((modes, cells), F32), ((1, cells), F32)]
        + [((days // words_per, 2 * LANES), BF16)],
        [],
        [near, far, place, m, u, row, *pieces],
        smem=(2,),
        flops=8 * modes * cells * days,
    )

    (m_days,) = call(
        days_flags_kernel,
        "days_flags",
        [((days, own), BF16)],
        [],
        [held, spread],
        flops=4 * LANES * own * days,
    )

    count = 2 * rows
    summed = block = None
    coefs = []
    for step in range(STEPS):
        if step == 0:
            fresh, xv_halo = call(
                functools.partial(first_fields_kernel, rows, reach),
                "fields_0",
                [((2 * count, 2 * LANES), F32), ((PAIRS, sides), F32)],
                [],
                [near_xv, far_xv, place, inverse, u, row, xv, base],
                smem=(2,),
            )
        else:
            fresh, v, u = call(
                functools.partial(fields_kernel, step, rows, reach, total),
                f"fields_{step}",
                [((count, 2 * LANES), F32), ((modes, days), F32), ((modes, cells), F32)],
                [],
                [m_days, m_halo, v, u, row, xv, xv_halo, base, inverse, summed, block],
                flops=8 * modes * cells * days,
                aliases={2: 1, 3: 2},
            )
        got_a, got_b = lat_partners(fresh)
        if step == 0:
            got_a, got_b, m_days = lax.optimization_barrier((got_a, got_b, m_days))
        if step + 1 < STEPS:
            base, inverse = call(
                functools.partial(next_products_kernel, step + 1, chunk),
                f"next_products_{step + 1}",
                [((2, cells), F32), ((8, LANES), F32)],
                [],
                [m_days, m_halo, v, u],
                flops=8 * modes * cells * days,
            )
            if step:
                got_a, got_b, base, inverse = lax.optimization_barrier((got_a, got_b, base, inverse))
        outs = [((2, days + 2 * LANES), F32), ((count, 2 * LANES), F32)]
        coef = ((5 * 3 * count, 2 * LANES), F32)
        partial_sums, block, *made = call(
            functools.partial(sums_kernel, step, rows, days),
            f"sums_{step}",
            outs if step else [*outs, coef],
            [],
            [m, a, v, u, place, klon, cosl, fresh, got_a, got_b, *coefs],
            smem=(4,),
            flops=8 * modes * own * days,
        )
        coefs = coefs or made
        summed = sum_all(partial_sums)
    return call(
        functools.partial(last_kernel, rows, reach, total),
        "last",
        [(mode_maps.shape, F32), (mode_series.shape, F32)],
        [((PAIRS, rows, columns), F32), ((PAIRS, mode_series.shape[1]), F32), ((PAIRS, days + 2 * LANES), F32)],
        [v, u, summed, block, place, maps_out, series_out],
        smem=(4,),
        in_hbm=(5, 6),
        out_hbm=(0, 1),
        copies=2,
        aliases={5: 0, 6: 1},
    )


def solution(mesh):
    in_specs = (
        P("lat", "lon", None),
        P("lat", "lon", None),
        P("lat", "lon"),
        P(None, "lat", "lon"),
        P(None, "lon"),
    )
    out_specs = (P(None, "lat", "lon"), P(None, "lon"))
    return jax.shard_map(shards, mesh=mesh, in_specs=in_specs, out_specs=out_specs, check_vma=False)
```
